32 devices in a mesh: groups: 2 (over y), seq: 16 (over z, x, core).
Axes of the slice: x: 2, y: 2, z: 4, core: 2. Of those that a mesh axis runs over, the one named last changes fastest.
Arguments:
- tokens: bfloat16 [8192, 4096], P(('groups', 'seq')), parts along dimension 0, may hold values from -6 to 6
- input_norm_scale: float32 [4096], replicated, may hold values from 0.1 to 1.9
- key_matrix: bfloat16 [4096, 1024], replicated, may hold values from -0.09375 to 0.09375
- adapter_down_weight: bfloat16 [32, 4096, 64], P('seq'), may hold values from -0.09375 to 0.09375
- adapter_up_weight: bfloat16 [32, 64, 1024], P('seq'), may hold values from -0.75 to 0.75
- lengths: int32 [16], P('groups'), parts along dimension 0, may hold values from 1 to 1024, 4096 in all
- prompt_adapter_index: int32 [16, 1], P('groups'), parts along dimension 0, may hold values from 0 to 7
- active_adapter_ids: int32 [16], P('groups'), parts along dimension 0, may hold values from 0 to 31, as said below
- token_cache_device: int32 [8192, 1], P(('groups', 'seq')), parts along dimension 0, may hold values from 0 to 15; in each aligned block of 256 rows (0 to 255, 256 to 511, ...) at most 32 rows name the same one
Outputs:
- key_cache: bfloat16 [16384, 1024], P(('groups', 'seq')), parts along dimension 0
The draws below stay inside these ranges and needn't reach their ends.
There are 2 independent parts, one for each index of `groups`. The reference program is written for one: setup_inputs(seed, part) draws one part's arguments, and reference() takes and returns one part's arrays. A program takes and returns all parts, laid end to end along the dimension named above; an argument that names none is the same for every part. Nothing has to cross between parts.
Inputs may be any that keep to these rules, and one draw needn't show every extreme that they name: `active_adapter_ids`: distinct store ids; adapter a is held by device a // 2 of seq in its slot a % 2. `prompt_adapter_index`: every index is used by some prompt. `lengths`: the 4096 rows hold the prompts end to end. `token_cache_device`: the rows of one device name any one device at most 32 times.
All inputs are finite; a program needn't handle non-finite values.
Results may differ from the reference program's by a relative error of at most 0.0054.
Values may be sent and summed in bfloat16 or wider, within the bound.
No kernel may reach another device: no remote copies, remote signals or barrier semaphores. Data moves between devices by JAX's collectives and lax.ppermute only.
A program may use at most 128 MiB of HBM per device.

```python
import math
import jax
import jax.numpy as jnp
import numpy as np
from jax import lax

MODEL_DIM = 4096
KEY_FEATURES = 1024
HEAD = 128
ADAPTER_RANK = 64
ACTIVE_ADAPTERS = 8
ROWS_DEV = 256
TOKENS = 4096
PROMPTS = 8
ADAPTER_STORE = 32
MOST = 32
N_SEQ = 16


def draw_active_adapter_ids(key, part):
    return jax.random.permutation(key, ADAPTER_STORE)[:ACTIVE_ADAPTERS].astype(jnp.int32)


def level_of(own_key, dims, cuts, smallest, high):
    level, own = 1.0, jax.random.fold_in(own_key, 6)
    for axis_at, blocks in cuts:
        steps = jnp.exp(jax.random.uniform(jax.random.fold_in(own, axis_at), (blocks,), jnp.float32, smallest / len(cuts), high / len(cuts)))
        level = level * jnp.repeat(steps, dims[axis_at] // blocks).reshape([-1 if axis == axis_at else 1 for axis in range(len(dims))])
    return level


def picks_of(rng, rows, amount, top, lift):
    ranking = jax.random.permutation(jax.random.fold_in(rng, 1), amount)
    favour = ranking
    for power in range(3):
        favour = favour * favour // amount
    favour = favour * lift // amount
    tickets = jax.random.randint(jax.random.fold_in(rng, 2), (rows, amount), 0, 4096) + favour
    fixed_rows = jax.random.permutation(jax.random.fold_in(rng, 3), rows)[jnp.arange(amount) % rows]
    tickets = jnp.where(jnp.arange(rows)[:, None] == fixed_rows[None, :], 1 << 14, tickets)
    merit = tickets * amount + jnp.arange(amount)
    return lax.top_k(merit.astype(jnp.int32), top)[1].astype(jnp.int32)


def length_profile(amount, total, most, slope):
    portions = [(1 << 20) // math.isqrt(rank ** slope) + 1 for rank in range(2, amount + 1)]
    surplus, given = total - most - (amount - 1), [1] * (amount - 1)
    while surplus > 0:
        candidates = [i for i in range(amount - 1) if given[i] < most]
        whole, remaining = sum([portions[i] for i in candidates]), surplus
        for i in candidates:
            more = min(most - given[i], max(1, remaining * portions[i] // whole), surplus)
            given[i] = given[i] + more
            surplus = surplus - more
    return np.array([most] + given)


def ragged(key, number_of, total, reach, lean):
    if number_of == 2:
        one = jax.random.randint(key, (), max(1, total - reach), min(reach, total - 1) + 1)
        return jnp.stack([one, total - one])
    sizes = jnp.asarray(length_profile(number_of, total, reach, lean), jnp.int32)
    twos = (number_of - 1) // 2
    source_of, receiver = sizes[1:1 + 2 * twos:2], sizes[2:2 + 2 * twos:2]
    room = jnp.minimum(source_of - 1, reach - receiver)
    passed = jax.random.randint(jax.random.fold_in(key, 1), (twos,), 0, 1 << 20) % (room + 1)
    sizes = sizes.at[1:1 + 2 * twos:2].set(source_of - passed).at[2:2 + 2 * twos:2].set(receiver + passed)
    return sizes[jax.random.permutation(jax.random.fold_in(key, 2), number_of)]


def assign_block(rng, own, number, rows, amount, top, reach, skew):
    sequence = jax.random.permutation(rng, amount)
    packed, usual = load_shares(amount, rows * top, reach, skew, True), load_shares(amount, rows * top, reach, skew, False)
    places = jnp.arange(amount)

    def named(sizes, offset_by):
        used = int((sizes > 0).sum())
        fixed = max(1, used // 4)
        shifted = fixed + (places - fixed + offset_by * (used - fixed)) % max(1, amount - fixed)
        return jnp.zeros((amount,), jnp.int32).at[sequence[jnp.where(places < fixed, places, shifted)]].set(jnp.asarray(sizes, jnp.int32))

    sizes = jnp.where(number % 4 == 0, named(packed, number // 4), named(usual, number - number // 4 - 1))
    mixed = jax.random.permutation(jax.random.fold_in(own, 3), amount)
    source_of, sink = mixed[0:amount // 2 * 2:2], mixed[1:amount // 2 * 2:2]
    slack = jnp.minimum(sizes[source_of] - 1, reach - sizes[sink]) // 2
    slack = jnp.where((source_of == sequence[0]) | (sink == sequence[0]) | (sizes[sink] == 0), 0, jnp.maximum(slack, 0))
    shifted = jax.random.randint(jax.random.fold_in(own, 4), (amount // 2,), 0, 1 << 20) % (slack + 1)
    sizes = sizes.at[source_of].add(-shifted).at[sink].add(shifted)
    labels = jnp.searchsorted(jnp.cumsum(sizes), jnp.arange(rows * top), side="right").astype(jnp.int32)
    table = labels.reshape(top, rows).T
    table = table[jax.random.permutation(jax.random.fold_in(own, 1), rows)]
    offset_by = jax.random.randint(jax.random.fold_in(own, 2), (rows, 1), 0, top)
    return jnp.take_along_axis(table, (jnp.arange(top)[None, :] + offset_by) % top, axis=1)


def load_shares(amount, total, reach, lean, full):
    weights = [(1 << 20) // math.isqrt(rank ** lean) + 1 for rank in range(1, amount + 1)]
    largest = reach if full else min(reach, max(-(-total // amount), total * weights[0] // sum(weights)))
    least = 1 if total - largest >= amount - 1 else 0
    holding, rest = [largest] + [least] * (amount - 1), total - largest - least * (amount - 1)
    while rest > 0:
        candidates = [i for i in range(1, amount) if holding[i] < largest] or [i for i in range(1, amount) if holding[i] < reach]
        whole, left = sum([weights[i] for i in candidates]), rest
        for i in candidates:
            extra = min(reach - holding[i], max(1, left * weights[i] // whole), rest)
            holding[i] = holding[i] + extra
            rest = rest - extra
    return np.array(holding)


def bell_draw(rng, shape, deviation, reach, split=(), kind=jnp.bfloat16):
    gain = level_of(rng, shape, split, -0.22, 0.18) if split else 1.0
    result = jax.random.normal(rng, shape, jnp.float32) * deviation * gain
    return jnp.minimum(jnp.maximum(result, -reach), reach).astype(kind)


def setup_inputs(seed: int = 0, part: int = 0) -> dict:
    arg_keys = jax.random.split(jax.random.key(seed), 10)
    own_keys = jax.random.split(jax.random.fold_in(arg_keys[9], part), 10)
    tokens = bell_draw(own_keys[0], (TOKENS, MODEL_DIM), 1.0, 6.0, ((0, 16),))
    input_norm_scale = jnp.clip(1.0 + 0.18 * jax.random.normal(arg_keys[1], (MODEL_DIM,), jnp.float32), 0.1, 1.9)
    key_matrix = bell_draw(arg_keys[2], (MODEL_DIM, KEY_FEATURES), MODEL_DIM ** -0.5, 0.09375)
    adapter_down_weight = bell_draw(arg_keys[3], (ADAPTER_STORE, MODEL_DIM, ADAPTER_RANK), MODEL_DIM ** -0.5, 0.09375, ((0, 16),))
    adapter_up_weight = bell_draw(arg_keys[4], (ADAPTER_STORE, ADAPTER_RANK, KEY_FEATURES), ADAPTER_RANK ** -0.5, 0.75, ((0, 16),))
    lengths = ragged(own_keys[5], PROMPTS, TOKENS, 4 * ROWS_DEV, 2).astype(jnp.int32)
    prompt_adapter_index = picks_of(own_keys[6], PROMPTS, ACTIVE_ADAPTERS, 1, 2048)
    active_adapter_ids = draw_active_adapter_ids(jax.random.fold_in(jax.random.fold_in(arg_keys[9], part), 71), part)
    token_cache_device_keys = jax.random.split(jax.random.fold_in(own_keys[8], 1), TOKENS // ROWS_DEV)
    token_cache_device_turns = jax.random.permutation(jax.random.fold_in(own_keys[8], 3), TOKENS // ROWS_DEV)
    token_cache_device = jax.vmap(lambda own, number: assign_block(jax.random.fold_in(own_keys[8], 2), own, number, ROWS_DEV, N_SEQ, 1, MOST, 0))(token_cache_device_keys, token_cache_device_turns).reshape((TOKENS, 1))
    return {"tokens": tokens, "input_norm_scale": input_norm_scale, "key_matrix": key_matrix, "adapter_down_weight": adapter_down_weight, "adapter_up_weight": adapter_up_weight, "lengths": lengths, "prompt_adapter_index": prompt_adapter_index, "active_adapter_ids": active_adapter_ids, "token_cache_device": token_cache_device}


rope_theta = 500000.0
norm_eps = 1e-05

def rotate(projected, positions):
    half_head = HEAD // 2
    frequencies = rope_theta ** (-(jnp.arange(half_head, dtype=jnp.float32) * 2.0) / HEAD)
    angles = positions.astype(jnp.float32)[:, None] * frequencies[None, :]
    cosine = jnp.cos(angles)[:, None, :]
    sine_table = jnp.sin(angles)[:, None, :]
    per_head = projected.reshape(projected.shape[0], -1, HEAD)
    first_half = per_head[..., :half_head]
    second_half = per_head[..., half_head:]
    turned = jnp.concatenate([first_half * cosine - second_half * sine_table, second_half * cosine + first_half * sine_table], axis=-1)
    return turned.reshape(projected.shape)

def reference(tokens, input_norm_scale, key_matrix, adapter_down_weight, adapter_up_weight, lengths, prompt_adapter_index, active_adapter_ids, token_cache_device):
    prompt_ends = jnp.cumsum(lengths).astype(jnp.int32)
    prompt_starts = (prompt_ends - lengths).astype(jnp.int32)
    row_ids = jnp.arange(TOKENS, dtype=jnp.int32)
    prompt_ids = lax.optimization_barrier(jnp.sum((prompt_ends[None, :] <= row_ids[:, None]).astype(jnp.int32), axis=1))
    positions = row_ids - prompt_starts[prompt_ids]
    hot_slots = prompt_adapter_index[:, 0][prompt_ids]
    float_rows = tokens.astype(jnp.float32)
    inverse_rms = lax.rsqrt(lax.optimization_barrier(jnp.mean(float_rows * float_rows, axis=1, keepdims=True)) + norm_eps)
    normed = (float_rows * inverse_rms * input_norm_scale.astype(jnp.float32)[None, :]).astype(jnp.bfloat16)
    down_matrices = jnp.concatenate([adapter_down_weight[active_adapter_ids[entry_position_index]] for entry_position_index in range(ACTIVE_ADAPTERS)], axis=1)
    up_matrices = jnp.concatenate([adapter_up_weight[active_adapter_ids[entry_position_index]] for entry_position_index in range(ACTIVE_ADAPTERS)], axis=0)
    base_proj = jnp.dot(normed, key_matrix, preferred_element_type=jnp.float32)
    low_rank = jnp.dot(normed, down_matrices, preferred_element_type=jnp.float32).astype(jnp.bfloat16)
    column_owned = (jnp.arange(ACTIVE_ADAPTERS * ADAPTER_RANK, dtype=jnp.int32) // ADAPTER_RANK)[None, :] == hot_slots[:, None]
    low_rank = jnp.where(column_owned, low_rank, jnp.zeros_like(low_rank))
    projected = base_proj + jnp.dot(low_rank, up_matrices, preferred_element_type=jnp.float32)
    key_rows = rotate(projected, positions).astype(jnp.bfloat16)
    blocks = token_cache_device[:, 0].reshape(N_SEQ, ROWS_DEV)
    row_order = jnp.arange(ROWS_DEV, dtype=jnp.int32)
    earlier = row_order[None, :] < row_order[:, None]
    rank_within = lax.optimization_barrier(jnp.sum(((blocks[:, :, None] == blocks[:, None, :]) & earlier[None, :, :]).astype(jnp.int32), axis=2)).reshape(TOKENS)
    row_target = token_cache_device[:, 0] * (N_SEQ * MOST) + row_ids // ROWS_DEV * MOST + rank_within
    key_cache = jnp.zeros((N_SEQ * N_SEQ * MOST, KEY_FEATURES), jnp.bfloat16).at[row_target].set(key_rows)
    return key_cache
```

```python
import jax
import jax.numpy as jnp
from jax import lax
from jax.sharding import PartitionSpec as P

HEAD = 128
ADAPTER_RANK = 64


rope_theta = 500000.0
norm_eps = 1e-05


def spread(array, axis, root):
    mine = lax.axis_index(axis) == root
    return lax.psum(jnp.where(mine, array, jnp.zeros_like(array)), axis)


def rotate(projected, positions):
    half_head = HEAD // 2
    frequencies = rope_theta ** (-(jnp.arange(half_head, dtype=jnp.float32) * 2.0) / HEAD)
    angles = positions.astype(jnp.float32)[:, None] * frequencies[None, :]
    cosine = jnp.cos(angles)[:, None, :]
    sine_table = jnp.sin(angles)[:, None, :]
    per_head = projected.reshape(projected.shape[0], -1, HEAD)
    first_half = per_head[..., :half_head]
    second_half = per_head[..., half_head:]
    turned = jnp.concatenate(
        [
            first_half * cosine - second_half * sine_table,
            second_half * cosine + first_half * sine_table,
        ],
        axis=-1,
    )
    return turned.reshape(projected.shape)


def locate(lengths, prompt_adapter_index, first_row, row_count):
    prompt_ends = jnp.cumsum(lengths)
    prompt_starts = prompt_ends - lengths
    row_ids = first_row + jnp.arange(row_count, dtype=jnp.int32)
    prompt_ids = jnp.sum((prompt_ends[None, :] <= row_ids[:, None]).astype(jnp.int32), axis=1)
    prompt_match = prompt_ids[:, None] == jnp.arange(lengths.shape[0], dtype=jnp.int32)[None, :]
    prompt_start = jnp.sum(jnp.where(prompt_match, prompt_starts[None, :], 0), axis=1)
    hot_slots = jnp.sum(jnp.where(prompt_match, prompt_adapter_index[:, 0][None, :], 0), axis=1)
    return (row_ids - prompt_start, hot_slots)


PLANE = 4
PLANES = 4
SLOTS = 2


def swap(value, distance, peer_count):
    return lax.ppermute(value, "seq", [(i, i ^ distance) for i in range(peer_count)])


def rank_of(mask):
    counts = mask.astype(jnp.int32)
    return jnp.cumsum(counts) - counts


def gather_up(adapter_up_weight, active_adapter_ids, device):
    adapter_device = adapter_up_weight.shape[0]
    pieces = []
    for entry in range(active_adapter_ids.shape[0]):
        adapter = active_adapter_ids[entry]
        mine = adapter // adapter_device == device
        piece = lax.dynamic_index_in_dim(
            adapter_up_weight, adapter % adapter_device, 0, keepdims=False
        )
        pieces.append(jnp.where(mine, piece, jnp.zeros_like(piece)))
    return lax.psum(jnp.concatenate(pieces, axis=0), "seq")


def plane_low_rank(
    normed, adapter_down_weight, lengths, prompt_adapter_index, active_adapter_ids, device
):
    peer_count = PLANE * PLANES
    rows = normed.shape[0]
    width = normed.shape[1]
    quarter = width // PLANE
    adapter_device = adapter_down_weight.shape[0]
    hot_count = active_adapter_ids.shape[0]
    plane = device // PLANE
    place = device % PLANE
    turned = jnp.swapaxes(adapter_down_weight, 1, 2)

    def quarter_of(array, which):
        return lax.dynamic_slice_in_dim(array, which * quarter, quarter, array.ndim - 1)

    local = [quarter_of(turned, place)]
    for distance in range(1, PLANE):
        local.append(swap(quarter_of(turned, place ^ distance), distance, peer_count))
    token_quarters = [quarter_of(normed, place)]
    for distance in range(1, PLANE):
        token_quarters.append(
            swap(quarter_of(normed, place ^ distance), distance, peer_count)
        )
    plane_tokens = jnp.concatenate(token_quarters, axis=0)
    local = jnp.concatenate(local, axis=0)
    prompt_ends = jnp.cumsum(lengths)
    prompt_starts = prompt_ends - lengths
    plane_rows = PLANE * rows
    plane_first = jnp.arange(PLANES, dtype=jnp.int32) * plane_rows
    crosses = (prompt_starts[None, :] < plane_first[:, None] + plane_rows) & (
        prompt_ends[None, :] > plane_first[:, None]
    )
    names = (
        prompt_adapter_index[:, 0][:, None] == jnp.arange(hot_count, dtype=jnp.int32)[None, :]
    )
    need = jnp.any(crosses[:, :, None] & names[None, :, :], axis=1)
    owner = active_adapter_ids // adapter_device
    owner_plane = owner // PLANE
    local_index = ((owner % PLANE) ^ place) * adapter_device + active_adapter_ids % adapter_device
    need_here = jnp.any(
        need & (jnp.arange(PLANES, dtype=jnp.int32) == plane)[:, None], axis=0
    )
    sends = []
    receive_rank = jnp.zeros((hot_count,), jnp.int32)
    for distance in range(1, PLANES):
        other = plane ^ distance
        need_there = jnp.any(
            need & (jnp.arange(PLANES, dtype=jnp.int32) == other)[:, None], axis=0
        )
        send_mask = (owner_plane == plane) & need_there
        send_rank = rank_of(send_mask)
        wanted = send_mask[None, :] & (
            send_rank[None, :] == jnp.arange(hot_count, dtype=jnp.int32)[:, None]
        )
        sends.append(jnp.sum(jnp.where(wanted, local_index[None, :], 0), axis=1))
        receive_mask = (owner_plane == other) & need_here
        receive_rank = jnp.where(receive_mask, rank_of(receive_mask), receive_rank)
    pair_count = jnp.sum(
        (need[:, None, :] & (owner_plane[None, :] == jnp.arange(PLANES)[:, None])[None]).astype(
            jnp.int32
        ),
        axis=2,
    )
    off_plane = ~jnp.eye(PLANES, dtype=bool)
    most = jnp.max(jnp.where(off_plane, pair_count, 0))

    def send_slots(first, count):
        received = []
        for distance in range(1, PLANES):
            picks = [
                lax.dynamic_index_in_dim(local, sends[distance - 1][slot], 0)
                for slot in range(first, first + count)
            ]
            received.append(
                swap(jnp.concatenate(picks, axis=0), distance * PLANE, peer_count)
            )
        return received

    first_round = send_slots(0, SLOTS)
    owner_distance = owner_plane ^ plane

    def assemble(extra_count):
        def run(local, first_round):
            table = [local] + first_round
            if extra_count:
                table += send_slots(SLOTS, extra_count)
            table = jnp.concatenate(table, axis=0)
            base = local.shape[0]
            first_at = base + (owner_distance - 1) * SLOTS + receive_rank
            later_at = (
                base
                + (PLANES - 1) * SLOTS
                + (owner_distance - 1) * extra_count
                + receive_rank
                - SLOTS
            )
            at = jnp.where(
                owner_distance == 0,
                local_index,
                jnp.where(receive_rank < SLOTS, first_at, later_at),
            )
            at = jnp.where(need_here, at, 0)
            return jnp.concatenate(
                [lax.dynamic_index_in_dim(table, at[i], 0, keepdims=False) for i in range(hot_count)],
                axis=0,
            )

        return run

    case = jnp.where(most <= SLOTS, 0, jnp.where(most <= SLOTS + 1, 1, 2))
    down_rows = lax.switch(
        case,
        [assemble(0), assemble(1), assemble(hot_count - SLOTS)],
        local,
        first_round,
    )
    partial = lax.dot_general(
        down_rows, plane_tokens, (((1,), (1,)), ((), ())), preferred_element_type=jnp.float32
    ).reshape(hot_count, -1, plane_rows)
    total = None
    for distance in range(PLANE):
        _, hot_slots = locate(lengths, prompt_adapter_index, (device ^ distance) * rows, rows)
        here = partial[:, :, distance * rows : (distance + 1) * rows]
        used = (
            jnp.arange(hot_count, dtype=jnp.int32)[:, None, None] == hot_slots[None, None, :]
        )
        mine = jnp.sum(jnp.where(used, here, 0.0), axis=0)
        if distance:
            mine = swap(mine, distance, peer_count)
        total = mine if total is None else total + mine
    return total.astype(jnp.bfloat16)


def on_device(
    tokens,
    input_norm_scale,
    key_matrix,
    adapter_down_weight,
    adapter_up_weight,
    lengths,
    prompt_adapter_index,
    active_adapter_ids,
    token_cache_device,
):
    rows_dev = tokens.shape[0]
    peer_count = lax.axis_size("seq")
    device = lax.axis_index("seq")
    slot_count = max(4, 2 * rows_dev // peer_count)
    key_width = key_matrix.shape[1]
    hot_count = active_adapter_ids.shape[0]
    up_matrices = gather_up(adapter_up_weight, active_adapter_ids, device)
    targets = token_cache_device[:, 0]
    row_order = jnp.arange(rows_dev, dtype=jnp.int32)
    earlier = row_order[None, :] < row_order[:, None]
    rank_within = jnp.sum(
        ((targets[:, None] == targets[None, :]) & earlier).astype(jnp.int32), axis=1
    )
    slot_index = targets * slot_count + rank_within
    positions, hot_slots = locate(lengths, prompt_adapter_index, device * rows_dev, rows_dev)
    float_rows = tokens.astype(jnp.float32)
    inverse_rms = lax.rsqrt(jnp.mean(float_rows * float_rows, axis=1, keepdims=True) + norm_eps)
    normed = (float_rows * inverse_rms * input_norm_scale[None, :]).astype(jnp.bfloat16)
    base_proj = jnp.dot(normed, key_matrix, preferred_element_type=jnp.float32)
    if peer_count == PLANE * PLANES:
        low_rank = plane_low_rank(
            normed, adapter_down_weight, lengths, prompt_adapter_index, active_adapter_ids, device
        )
        owned = jnp.arange(hot_count, dtype=jnp.int32)[:, None, None] == hot_slots[None, None, :]
        low_rank = jnp.where(owned, low_rank[None], jnp.zeros_like(low_rank[None]))
        low_rank = low_rank.reshape(-1, rows_dev)
        adapted = lax.dot_general(
            low_rank, up_matrices, (((0,), (0,)), ((), ())), preferred_element_type=jnp.float32
        )
    else:
        adapter_device = adapter_down_weight.shape[0]
        down_list = []
        for entry in range(hot_count):
            adapter = active_adapter_ids[entry]
            down_list.append(
                spread(
                    lax.dynamic_index_in_dim(
                        adapter_down_weight, adapter % adapter_device, 0, keepdims=False
                    ),
                    "seq",
                    adapter // adapter_device,
                )
            )
        down_matrices = jnp.concatenate(down_list, axis=1)
        low_rank = jnp.dot(normed, down_matrices, preferred_element_type=jnp.float32).astype(
            jnp.bfloat16
        )
        column_owned = (jnp.arange(down_matrices.shape[1], dtype=jnp.int32) // ADAPTER_RANK)[
            None, :
        ] == hot_slots[:, None]
        low_rank = jnp.where(column_owned, low_rank, jnp.zeros_like(low_rank))
        adapted = jnp.dot(low_rank, up_matrices, preferred_element_type=jnp.float32)
    key_rows = rotate(base_proj + adapted, positions).astype(jnp.bfloat16)
    outgoing = (
        jnp.zeros((peer_count * slot_count, key_width), jnp.bfloat16).at[slot_index].set(key_rows)
    )
    outgoing = outgoing.reshape(peer_count, slot_count, key_width)
    result = lax.all_to_all(outgoing, "seq", split_axis=0, concat_axis=0, tiled=True)
    return result.reshape(peer_count * slot_count, key_width)


def solution(mesh):
    in_specs = (
        P(("groups", "seq"), None),
        P(),
        P(),
        P("seq", None, None),
        P("seq", None, None),
        P("groups"),
        P("groups", None),
        P("groups"),
        P(("groups", "seq"), None),
    )
    out_specs = P(("groups", "seq"), None)
    return jax.shard_map(
        on_device, mesh=mesh, in_specs=in_specs, out_specs=out_specs, check_vma=False
    )
```

```python
import functools

import jax
import jax.numpy as jnp
from jax import lax
from jax.experimental import pallas as pl
from jax.experimental.pallas import tpu as pltpu
from jax.sharding import PartitionSpec as P

HEAD = 128
ADAPTER_RANK = 64


rope_theta = 500000.0
norm_eps = 1e-05


def spread(array, axis, root):
    mine = lax.axis_index(axis) == root
    return lax.psum(jnp.where(mine, array, jnp.zeros_like(array)), axis)


def rotate(projected, positions):
    half_head = HEAD // 2
    frequencies = rope_theta ** (-(jnp.arange(half_head, dtype=jnp.float32) * 2.0) / HEAD)
    angles = positions.astype(jnp.float32)[:, None] * frequencies[None, :]
    cosine = jnp.cos(angles)[:, None, :]
    sine_table = jnp.sin(angles)[:, None, :]
    per_head = projected.reshape(projected.shape[0], -1, HEAD)
    first_half = per_head[..., :half_head]
    second_half = per_head[..., half_head:]
    turned = jnp.concatenate(
        [
            first_half * cosine - second_half * sine_table,
            second_half * cosine + first_half * sine_table,
        ],
        axis=-1,
    )
    return turned.reshape(projected.shape)


def locate(lengths, prompt_adapter_index, first_row, row_count):
    prompt_ends = jnp.cumsum(lengths)
    prompt_starts = prompt_ends - lengths
    row_ids = first_row + jnp.arange(row_count, dtype=jnp.int32)
    prompt_ids = jnp.sum((prompt_ends[None, :] <= row_ids[:, None]).astype(jnp.int32), axis=1)
    prompt_match = prompt_ids[:, None] == jnp.arange(lengths.shape[0], dtype=jnp.int32)[None, :]
    prompt_start = jnp.sum(jnp.where(prompt_match, prompt_starts[None, :], 0), axis=1)
    hot_slots = jnp.sum(jnp.where(prompt_match, prompt_adapter_index[:, 0][None, :], 0), axis=1)
    return (row_ids - prompt_start, hot_slots)


PLANE = 4
PLANES = 4
SLOT_CASES = ((2, 1, 1), (2, 2, 1), (2, 1, 2), (2, 2, 2), (3, 3, 3))
ANY = pl.BlockSpec(memory_space=pl.ANY)
SMEM = pl.BlockSpec(memory_space=pltpu.SMEM)
VMEM = pl.BlockSpec(memory_space=pltpu.VMEM)
VMEM_LIMIT = 40 * 1024 * 1024


def swap(value, distance, peer_count):
    return lax.ppermute(value, "seq", [(i, i ^ distance) for i in range(peer_count)])


def call(kernel, out_shape, in_specs, out_specs, scratch=(), **cost):
    return pl.pallas_call(
        kernel,
        out_shape=out_shape,
        in_specs=in_specs,
        out_specs=out_specs,
        scratch_shapes=list(scratch),
        compiler_params=pltpu.CompilerParams(vmem_limit_bytes=VMEM_LIMIT),
        cost_estimate=pl.CostEstimate(transcendentals=0, **cost) if cost else None,
    )


def plan_size(hot_count):
    return 5 * hot_count + 1


def plan_kernel(plane_rows, adapter_device, device_ref, length_ref, index_ref, id_ref, plan_ref):
    hot_count = id_ref.shape[0]
    device = device_ref[0]
    plane = lax.div(device, PLANE)
    place = device - plane * PLANE
    for at in range(3 * hot_count):
        plan_ref[at] = 0
    need = [jnp.int32(0)] * PLANES
    start = jnp.int32(0)
    for prompt in range(length_ref.shape[0]):
        end = start + length_ref[prompt]
        bit = lax.shift_left(jnp.int32(1), index_ref[prompt])
        for at in range(PLANES):
            hit = (start < (at + 1) * plane_rows) & (end > at * plane_rows)
            need[at] = need[at] | jnp.where(hit, bit, 0)
        start = end

    def need_of(which):
        total = jnp.int32(0)
        for at in range(PLANES):
            total = jnp.where(which == at, need[at], total)
        return total

    owner_plane = []
    kind = []
    slot = []
    local = []
    for entry in range(hot_count):
        adapter = id_ref[entry]
        owner = lax.div(adapter, adapter_device)
        owner_plane.append(lax.div(owner, PLANE))
        local.append(
            ((owner - owner_plane[entry] * PLANE) ^ place) * adapter_device
            + adapter
            - owner * adapter_device
        )
        kind.append(jnp.int32(0))
        slot.append(local[entry])
    need_here = need_of(plane)
    for distance in range(1, PLANES):
        other = plane ^ distance
        need_there = need_of(other)
        sent = jnp.int32(0)
        taken = jnp.int32(0)
        for entry in range(hot_count):
            plan_ref[(distance - 1) * hot_count + sent] = local[entry]
            wanted = lax.shift_right_logical(need_there, entry) & 1
            sent = sent + jnp.where(owner_plane[entry] == plane, wanted, 0)
            wanted = lax.shift_right_logical(need_here, entry) & 1
            wanted = jnp.where(owner_plane[entry] == other, wanted, 0)
            kind[entry] = jnp.where(wanted == 1, distance, kind[entry])
            slot[entry] = jnp.where(wanted == 1, taken, slot[entry])
            taken = taken + wanted
    for entry in range(hot_count):
        plan_ref[3 * hot_count + entry] = kind[entry]
        plan_ref[4 * hot_count + entry] = slot[entry]
    most = []
    for distance in range(1, PLANES):
        largest = jnp.int32(0)
        for at in range(PLANES):
            count = jnp.int32(0)
            for entry in range(hot_count):
                wanted = lax.shift_right_logical(need[at ^ distance], entry) & 1
                count = count + jnp.where(owner_plane[entry] == at, wanted, 0)
            largest = jnp.maximum(largest, count)
        most.append(largest)
    case = jnp.int32(len(SLOT_CASES))
    for at in reversed(range(len(SLOT_CASES))):
        fits = jnp.bool_(True)
        for distance in range(PLANES - 1):
            fits = fits & (most[distance] <= SLOT_CASES[at][distance])
        case = jnp.where(fits, at, case)
    plan_ref[5 * hot_count] = case


def pack_kernel(quarter, device_ref, down_ref, up_ref, *refs):
    outs = refs[:PLANE]
    sems = refs[PLANE]
    place = lax.rem(device_ref[0], PLANE)
    rank = down_ref.shape[1]
    part = rank // PLANE
    copies = []
    for distance in range(PLANE):
        other = place ^ distance
        columns = pl.ds(pl.multiple_of(other * quarter, quarter), quarter)
        copies.append(
            pltpu.make_async_copy(
                down_ref.at[:, :, columns],
                outs[distance].at[:, pl.ds(0, rank), :],
                sems.at[2 * distance],
            )
        )
        rows = pl.ds(pl.multiple_of(other * part, part), part)
        copies.append(
            pltpu.make_async_copy(
                up_ref.at[:, rows, :],
                outs[distance].at[:, pl.ds(rank, part), :],
                sems.at[2 * distance + 1],
            )
        )
    for copy in copies:
        copy.start()
    for copy in copies:
        copy.wait()


def select_kernel(slots, hot_count, adapter_device, plan_ref, *refs):
    local = refs[:PLANE]
    outs = refs[PLANE : PLANE + PLANES - 1]
    sems = refs[-1]
    waits = []
    for distance in range(1, PLANES):
        for slot in range(slots[distance - 1]):
            index = plan_ref[(distance - 1) * hot_count + slot]
            holder = lax.div(index, adapter_device)
            inner = index - holder * adapter_device
            target = outs[distance - 1].at[slot]
            sem = sems.at[len(waits)]
            for at in range(PLANE):

                @pl.when(holder == at)
                def _():
                    pltpu.make_async_copy(local[at].at[inner], target, sem).start()

            waits.append(pltpu.make_async_copy(local[0].at[0], target, sem))
    for wait in waits:
        wait.wait()


def collect_kernel(slots, rank, hot_count, adapter_device, plan_ref, *refs):
    local = refs[:PLANE]
    arrived = refs[PLANE : PLANE + PLANES - 1]
    down_ref, up_ref, sems = refs[PLANE + PLANES - 1 :]
    part = local[0].shape[1] - rank
    waits = []
    for entry in range(hot_count):
        kind = plan_ref[3 * hot_count + entry]
        slot = plan_ref[4 * hot_count + entry]

        def copies(source):
            return (
                pltpu.make_async_copy(
                    source.at[pl.ds(0, rank), :],
                    down_ref.at[pl.ds(entry * rank, rank), :],
                    sems.at[2 * entry],
                ),
                pltpu.make_async_copy(
                    source.at[pl.ds(rank, part), :], up_ref.at[entry], sems.at[2 * entry + 1]
                ),
            )

        holder = lax.div(slot, adapter_device)
        inner = slot - holder * adapter_device
        for at in range(PLANE):

            @pl.when((kind == 0) & (holder == at))
            def _():
                for copy in copies(local[at].at[inner]):
                    copy.start()

        for distance in range(1, PLANES):

            @pl.when(kind == distance)
            def _():
                for copy in copies(arrived[distance - 1].at[slot]):
                    copy.start()

        waits.extend(copies(local[0].at[0]))
    for wait in waits:
        wait.wait()


def hot_lanes(first_row, rows, length_ref, index_ref):
    row_ids = first_row + lax.broadcasted_iota(jnp.int32, (1, rows), 1)
    hot = jnp.zeros((1, rows), jnp.int32)
    start = jnp.int32(0)
    for prompt in range(length_ref.shape[0]):
        end = start + length_ref[prompt]
        hot = jnp.where((row_ids >= start) & (row_ids < end), index_ref[prompt], hot)
        start = end
    return hot


def partial_kernel(rank, device_ref, length_ref, index_ref, down_ref, *refs):
    tokens = refs[:PLANE]
    outs = refs[PLANE:]
    hot_count = down_ref.shape[0] // rank
    rows = tokens[0].shape[0]
    for distance in range(PLANE):
        product = lax.dot_general(
            down_ref[...],
            tokens[distance][...],
            (((1,), (1,)), ((), ())),
            preferred_element_type=jnp.float32,
        )
        hot = hot_lanes((device_ref[0] ^ distance) * rows, rows, length_ref, index_ref)
        total = jnp.zeros((rank, rows), jnp.float32)
        for entry in range(hot_count):
            total = jnp.where(hot == entry, product[entry * rank : (entry + 1) * rank], total)
        outs[distance][...] = total


def finish_kernel(
    rank, device_ref, length_ref, index_ref, base_ref, cosine_ref, sine_ref, slot_ref, *refs
):
    partials = refs[:PLANE]
    ups = refs[PLANE : 2 * PLANE]
    out_ref, low_ref, rows_ref = refs[2 * PLANE :]
    hot_count, part, key_width = ups[0].shape
    rows = base_ref.shape[0]
    place = lax.rem(device_ref[0], PLANE)
    total = partials[0][...]
    for distance in range(1, PLANE):
        total = total + partials[distance][...]
    low_ref[...] = total
    hot = hot_lanes(device_ref[0] * rows, rows, length_ref, index_ref)
    projected = base_ref[...]
    for distance in range(PLANE):
        first = pl.multiple_of((place ^ distance) * part, part)
        piece = low_ref[pl.ds(first, part), :].astype(jnp.bfloat16).astype(jnp.float32)
        spread_rows = jnp.concatenate(
            [jnp.where(hot == entry, piece, 0.0) for entry in range(hot_count)], axis=0
        ).astype(jnp.bfloat16)
        projected = projected + lax.dot_general(
            spread_rows,
            ups[distance][...].reshape(hot_count * part, key_width),
            (((0,), (0,)), ((), ())),
            preferred_element_type=jnp.float32,
        )
    cosine = cosine_ref[...]
    sine = sine_ref[...]
    for head in range(key_width // HEAD):
        columns = slice(head * HEAD, (head + 1) * HEAD)
        values = projected[:, columns]
        turned = values * cosine + pltpu.roll(values, HEAD // 2, 1) * sine
        rows_ref[:, columns] = turned.astype(jnp.bfloat16)
    slots = lax.broadcasted_iota(jnp.int32, (out_ref.shape[0], rows), 0)
    placed = (slots == slot_ref[...]).astype(jnp.bfloat16)
    out_ref[...] = jnp.dot(
        placed, rows_ref[...], preferred_element_type=jnp.float32
    ).astype(jnp.bfloat16)


def turn_tables(positions):
    half_head = HEAD // 2
    frequencies = rope_theta ** (-(jnp.arange(half_head, dtype=jnp.float32) * 2.0) / HEAD)
    angles = positions.astype(jnp.float32)[:, None] * frequencies[None, :]
    cosine = jnp.cos(angles)
    sine = jnp.sin(angles)
    return (
        jnp.concatenate([cosine, cosine], axis=1),
        jnp.concatenate([-sine, sine], axis=1),
    )


def planes_outgoing(
    normed,
    key_matrix,
    adapter_down_weight,
    adapter_up_weight,
    lengths,
    prompt_adapter_index,
    active_adapter_ids,
    positions,
    slot_index,
    out_rows,
):
    peer_count = PLANE * PLANES
    rows, width = normed.shape
    quarter = width // PLANE
    adapter_device, rank, key_width = adapter_up_weight.shape
    part = rank // PLANE
    hot_count = active_adapter_ids.shape[0]
    index = lax.axis_index("seq").astype(jnp.int32)
    place = index % PLANE
    device = index.reshape(1)
    prompt_index = prompt_adapter_index[:, 0]
    plan = call(
        functools.partial(plan_kernel, PLANE * rows, adapter_device),
        jax.ShapeDtypeStruct((plan_size(hot_count),), jnp.int32),
        [SMEM] * 4,
        SMEM,
    )(device, lengths, prompt_index, active_adapter_ids)
    piece = jax.ShapeDtypeStruct((adapter_device, rank + part, quarter), jnp.bfloat16)
    packed = call(
        functools.partial(pack_kernel, quarter),
        [piece] * PLANE,
        [SMEM, ANY, ANY],
        [ANY] * PLANE,
        [pltpu.SemaphoreType.DMA((2 * PLANE,))],
    )(device, jnp.swapaxes(adapter_down_weight, 1, 2), adapter_up_weight)
    local = [packed[0]] + [
        swap(packed[distance], distance, peer_count) for distance in range(1, PLANE)
    ]
    held = lax.optimization_barrier((normed, *local))
    sent_rows, local = held[0], list(held[1:])
    tokens = []
    for distance in range(PLANE):
        columns = lax.dynamic_slice_in_dim(sent_rows, (place ^ distance) * quarter, quarter, 1)
        tokens.append(swap(columns, distance, peer_count) if distance else columns)

    def branch(slots):
        def run(plan, *local):
            sends = call(
                functools.partial(select_kernel, slots, hot_count, adapter_device),
                [
                    jax.ShapeDtypeStruct((count, rank + part, quarter), jnp.bfloat16)
                    for count in slots
                ],
                [SMEM] + [ANY] * PLANE,
                [ANY] * len(slots),
                [pltpu.SemaphoreType.DMA((sum(slots),))],
            )(plan, *local)
            arrived = [
                swap(send, (at + 1) * PLANE, peer_count) for at, send in enumerate(sends)
            ]
            return call(
                functools.partial(collect_kernel, slots, rank, hot_count, adapter_device),
                (
                    jax.ShapeDtypeStruct((hot_count * rank, quarter), jnp.bfloat16),
                    jax.ShapeDtypeStruct((hot_count, part, key_width), jnp.bfloat16),
                ),
                [SMEM] + [ANY] * (PLANE + PLANES - 1),
                (ANY, ANY),
                [pltpu.SemaphoreType.DMA((2 * hot_count,))],
            )(plan, *local, *arrived)

        return run

    cases = [branch(slots) for slots in SLOT_CASES + ((hot_count,) * (PLANES - 1),)]
    down_rows, up_rows = lax.switch(plan[5 * hot_count], cases, plan, *local)
    ups = [up_rows] + [swap(up_rows, distance, peer_count) for distance in range(1, PLANE)]
    partials = call(
        functools.partial(partial_kernel, rank),
        [jax.ShapeDtypeStruct((rank, rows), jnp.float32)] * PLANE,
        [SMEM] * 3 + [VMEM] * (1 + PLANE),
        [VMEM] * PLANE,
        flops=2 * hot_count * rank * width * rows,
        bytes_accessed=6 * 1024 * 1024,
    )(device, lengths, prompt_index, down_rows, *tokens)
    partials = [partials[0]] + [
        swap(partials[distance], distance, peer_count) for distance in range(1, PLANE)
    ]
    base = jnp.dot(normed, key_matrix, preferred_element_type=jnp.float32)
    cosine, sine = turn_tables(positions)
    return call(
        functools.partial(finish_kernel, rank),
        jax.ShapeDtypeStruct((out_rows, key_width), jnp.bfloat16),
        [SMEM] * 3 + [VMEM] * (4 + 2 * PLANE),
        VMEM,
        [pltpu.VMEM((rank, rows), jnp.float32), pltpu.VMEM((rows, key_width), jnp.bfloat16)],
        flops=2 * rows * key_width * (hot_count * rank + out_rows),
        bytes_accessed=6 * 1024 * 1024,
    )(
        device,
        lengths,
        prompt_index,
        base,
        cosine,
        sine,
        slot_index.reshape(1, rows),
        *partials,
        *ups,
    )


def gathered_outgoing(
    normed,
    key_matrix,
    adapter_down_weight,
    adapter_up_weight,
    active_adapter_ids,
    positions,
    hot_slots,
    slot_index,
    out_rows,
):
    adapter_device = adapter_down_weight.shape[0]
    down_list = []
    up_list = []
    for entry in range(active_adapter_ids.shape[0]):
        adapter = active_adapter_ids[entry]
        for weight, gathered in ((adapter_down_weight, down_list), (adapter_up_weight, up_list)):
            mine = lax.dynamic_index_in_dim(weight, adapter % adapter_device, 0, keepdims=False)
            gathered.append(spread(mine, "seq", adapter // adapter_device))
    down_matrices = jnp.concatenate(down_list, axis=1)
    up_matrices = jnp.concatenate(up_list, axis=0)
    base_proj = jnp.dot(normed, key_matrix, preferred_element_type=jnp.float32)
    low_rank = jnp.dot(normed, down_matrices, preferred_element_type=jnp.float32).astype(
        jnp.bfloat16
    )
    column_owned = (jnp.arange(down_matrices.shape[1], dtype=jnp.int32) // ADAPTER_RANK)[
        None, :
    ] == hot_slots[:, None]
    low_rank = jnp.where(column_owned, low_rank, jnp.zeros_like(low_rank))
    projected = base_proj + jnp.dot(low_rank, up_matrices, preferred_element_type=jnp.float32)
    key_rows = rotate(projected, positions).astype(jnp.bfloat16)
    return jnp.zeros((out_rows, key_rows.shape[1]), jnp.bfloat16).at[slot_index].set(key_rows)


def on_device(
    tokens,
    input_norm_scale,
    key_matrix,
    adapter_down_weight,
    adapter_up_weight,
    lengths,
    prompt_adapter_index,
    active_adapter_ids,
    token_cache_device,
):
    rows_dev = tokens.shape[0]
    peer_count = lax.axis_size("seq")
    slot_count = max(4, 2 * rows_dev // peer_count)
    key_width = key_matrix.shape[1]
    targets = token_cache_device[:, 0]
    row_order = jnp.arange(rows_dev, dtype=jnp.int32)
    earlier = row_order[None, :] < row_order[:, None]
    rank_within = jnp.sum(
        ((targets[:, None] == targets[None, :]) & earlier).astype(jnp.int32), axis=1
    )
    slot_index = targets * slot_count + rank_within
    positions, hot_slots = locate(
        lengths, prompt_adapter_index, lax.axis_index("seq") * rows_dev, rows_dev
    )
    float_rows = tokens.astype(jnp.float32)
    inverse_rms = lax.rsqrt(jnp.mean(float_rows * float_rows, axis=1, keepdims=True) + norm_eps)
    normed = (float_rows * inverse_rms * input_norm_scale[None, :]).astype(jnp.bfloat16)
    out_rows = peer_count * slot_count
    if peer_count == PLANE * PLANES:
        outgoing = planes_outgoing(
            normed,
            key_matrix,
            adapter_down_weight,
            adapter_up_weight,
            lengths,
            prompt_adapter_index,
            active_adapter_ids,
            positions,
            slot_index,
            out_rows,
        )
    else:
        outgoing = gathered_outgoing(
            normed,
            key_matrix,
            adapter_down_weight,
            adapter_up_weight,
            active_adapter_ids,
            positions,
            hot_slots,
            slot_index,
            out_rows,
        )
    outgoing = outgoing.reshape(peer_count, slot_count, key_width)
    result = lax.all_to_all(outgoing, "seq", split_axis=0, concat_axis=0, tiled=True)
    return result.reshape(out_rows, key_width)


def solution(mesh):
    in_specs = (
        P(("groups", "seq"), None),
        P(),
        P(),
        P("seq", None, None),
        P("seq", None, None),
        P("groups"),
        P("groups", None),
        P("groups"),
        P(("groups", "seq"), None),
    )
    out_specs = P(("groups", "seq"), None)
    return jax.shard_map(
        on_device, mesh=mesh, in_specs=in_specs, out_specs=out_specs, check_vma=False
    )
```

```python
import functools

import jax
import jax.numpy as jnp
from jax import lax
from jax.experimental import pallas as pl
from jax.experimental.pallas import tpu as pltpu
from jax.sharding import PartitionSpec as P

HEAD = 128
ADAPTER_RANK = 64


rope_theta = 500000.0
norm_eps = 1e-05


def spread(array, axis, root):
    mine = lax.axis_index(axis) == root
    return lax.psum(jnp.where(mine, array, jnp.zeros_like(array)), axis)


def rotate(projected, positions):
    half_head = HEAD // 2
    frequencies = rope_theta ** (-(jnp.arange(half_head, dtype=jnp.float32) * 2.0) / HEAD)
    angles = positions.astype(jnp.float32)[:, None] * frequencies[None, :]
    cosine = jnp.cos(angles)[:, None, :]
    sine_table = jnp.sin(angles)[:, None, :]
    per_head = projected.reshape(projected.shape[0], -1, HEAD)
    first_half = per_head[..., :half_head]
    second_half = per_head[..., half_head:]
    turned = jnp.concatenate(
        [
            first_half * cosine - second_half * sine_table,
            second_half * cosine + first_half * sine_table,
        ],
        axis=-1,
    )
    return turned.reshape(projected.shape)


def locate(lengths, prompt_adapter_index, first_row, row_count):
    prompt_ends = jnp.cumsum(lengths)
    prompt_starts = prompt_ends - lengths
    row_ids = first_row + jnp.arange(row_count, dtype=jnp.int32)
    prompt_ids = jnp.sum((prompt_ends[None, :] <= row_ids[:, None]).astype(jnp.int32), axis=1)
    prompt_match = prompt_ids[:, None] == jnp.arange(lengths.shape[0], dtype=jnp.int32)[None, :]
    prompt_start = jnp.sum(jnp.where(prompt_match, prompt_starts[None, :], 0), axis=1)
    hot_slots = jnp.sum(jnp.where(prompt_match, prompt_adapter_index[:, 0][None, :], 0), axis=1)
    return (row_ids - prompt_start, hot_slots)


PLANE = 4
PLANES = 4
SLOT_CASES = ((2, 1, 1), (2, 2, 1), (2, 1, 2), (2, 2, 2), (3, 3, 3))
ANY = pl.BlockSpec(memory_space=pl.ANY)
SMEM = pl.BlockSpec(memory_space=pltpu.SMEM)
VMEM = pl.BlockSpec(memory_space=pltpu.VMEM)
VMEM_LIMIT = 40 * 1024 * 1024


def swap(value, distance, peer_count):
    return lax.ppermute(value, "seq", [(i, i ^ distance) for i in range(peer_count)])


def call(kernel, out_shape, in_specs, out_specs, scratch=(), **cost):
    return pl.pallas_call(
        kernel,
        out_shape=out_shape,
        in_specs=in_specs,
        out_specs=out_specs,
        scratch_shapes=list(scratch),
        compiler_params=pltpu.CompilerParams(vmem_limit_bytes=VMEM_LIMIT),
        cost_estimate=pl.CostEstimate(transcendentals=0, **cost) if cost else None,
    )


def plan_size(hot_count):
    return 5 * hot_count + 1


def plan_kernel(plane_rows, adapter_device, length_ref, index_ref, id_ref, plan_ref):
    hot_count = id_ref.shape[0]
    device = lax.axis_index("seq")
    plane = lax.div(device, PLANE)
    place = device - plane * PLANE
    for at in range(3 * hot_count):
        plan_ref[at] = 0
    need = [jnp.int32(0)] * PLANES
    start = jnp.int32(0)
    for prompt in range(length_ref.shape[0]):
        end = start + length_ref[prompt]
        bit = lax.shift_left(jnp.int32(1), index_ref[prompt])
        for at in range(PLANES):
            hit = (start < (at + 1) * plane_rows) & (end > at * plane_rows)
            need[at] = need[at] | jnp.where(hit, bit, 0)
        start = end

    def need_of(which):
        total = jnp.int32(0)
        for at in range(PLANES):
            total = jnp.where(which == at, need[at], total)
        return total

    owner_plane = []
    kind = []
    slot = []
    local = []
    for entry in range(hot_count):
        adapter = id_ref[entry]
        owner = lax.div(adapter, adapter_device)
        owner_plane.append(lax.div(owner, PLANE))
        local.append(
            ((owner - owner_plane[entry] * PLANE) ^ place) * adapter_device
            + adapter
            - owner * adapter_device
        )
        kind.append(jnp.int32(0))
        slot.append(local[entry])
    need_here = need_of(plane)
    for distance in range(1, PLANES):
        other = plane ^ distance
        need_there = need_of(other)
        sent = jnp.int32(0)
        taken = jnp.int32(0)
        for entry in range(hot_count):
            plan_ref[(distance - 1) * hot_count + sent] = local[entry]
            wanted = lax.shift_right_logical(need_there, entry) & 1
            sent = sent + jnp.where(owner_plane[entry] == plane, wanted, 0)
            wanted = lax.shift_right_logical(need_here, entry) & 1
            wanted = jnp.where(owner_plane[entry] == other, wanted, 0)
            kind[entry] = jnp.where(wanted == 1, distance, kind[entry])
            slot[entry] = jnp.where(wanted == 1, taken, slot[entry])
            taken = taken + wanted
    for entry in range(hot_count):
        plan_ref[3 * hot_count + entry] = kind[entry]
        plan_ref[4 * hot_count + entry] = slot[entry]
    most = []
    for distance in range(1, PLANES):
        largest = jnp.int32(0)
        for at in range(PLANES):
            count = jnp.int32(0)
            for entry in range(hot_count):
                wanted = lax.shift_right_logical(need[at ^ distance], entry) & 1
                count = count + jnp.where(owner_plane[entry] == at, wanted, 0)
            largest = jnp.maximum(largest, count)
        most.append(largest)
    case = jnp.int32(len(SLOT_CASES))
    for at in reversed(range(len(SLOT_CASES))):
        fits = jnp.bool_(True)
        for distance in range(PLANES - 1):
            fits = fits & (most[distance] <= SLOT_CASES[at][distance])
        case = jnp.where(fits, at, case)
    plan_ref[5 * hot_count] = case


def pack_kernel(quarter, down_ref, up_ref, *refs):
    outs = refs[:PLANE]
    sems = refs[PLANE]
    place = lax.rem(lax.axis_index("seq"), PLANE)
    rank = down_ref.shape[1]
    part = rank // PLANE
    copies = []
    for distance in range(PLANE):
        other = place ^ distance
        columns = pl.ds(pl.multiple_of(other * quarter, quarter), quarter)
        copies.append(
            pltpu.make_async_copy(
                down_ref.at[:, :, columns],
                outs[distance].at[:, pl.ds(0, rank), :],
                sems.at[2 * distance],
            )
        )
        rows = pl.ds(pl.multiple_of(other * part, part), part)
        copies.append(
            pltpu.make_async_copy(
                up_ref.at[:, rows, :],
                outs[distance].at[:, pl.ds(rank, part), :],
                sems.at[2 * distance + 1],
            )
        )
    for copy in copies:
        copy.start()
    for copy in copies:
        copy.wait()


def select_kernel(slots, hot_count, adapter_device, plan_ref, *refs):
    local = refs[:PLANE]
    outs = refs[PLANE : PLANE + PLANES - 1]
    sems = refs[-1]
    waits = []
    for distance in range(1, PLANES):
        for slot in range(slots[distance - 1]):
            index = plan_ref[(distance - 1) * hot_count + slot]
            holder = lax.div(index, adapter_device)
            inner = index - holder * adapter_device
            target = outs[distance - 1].at[slot]
            sem = sems.at[len(waits)]
            for at in range(PLANE):

                @pl.when(holder == at)
                def _():
                    pltpu.make_async_copy(local[at].at[inner], target, sem).start()

            waits.append(pltpu.make_async_copy(local[0].at[0], target, sem))
    for wait in waits:
        wait.wait()


def start_rows(plan_ref, hot_count, adapter_device, local, arrived, copy_of):
    waits = []
    for entry in range(hot_count):
        kind = plan_ref[3 * hot_count + entry]
        slot = plan_ref[4 * hot_count + entry]
        holder = lax.div(slot, adapter_device)
        inner = slot - holder * adapter_device
        for at in range(PLANE):

            @pl.when((kind == 0) & (holder == at))
            def _():
                copy_of(entry, local[at].at[inner]).start()

        for distance in range(1, PLANES):

            @pl.when(kind == distance)
            def _():
                copy_of(entry, arrived[distance - 1].at[slot]).start()

        waits.append(copy_of(entry, local[0].at[0]))
    return waits


def collect_kernel(rank, hot_count, adapter_device, plan_ref, *refs):
    local = refs[:PLANE]
    arrived = refs[PLANE : PLANE + PLANES - 1]
    up_ref, sems = refs[PLANE + PLANES - 1 :]
    part = up_ref.shape[1]
    waits = start_rows(
        plan_ref,
        hot_count,
        adapter_device,
        local,
        arrived,
        lambda entry, source: pltpu.make_async_copy(
            source.at[pl.ds(rank, part), :], up_ref.at[entry], sems.at[entry]
        ),
    )
    for wait in waits:
        wait.wait()


def hot_lanes(first_row, rows, length_ref, index_ref):
    row_ids = first_row + lax.broadcasted_iota(jnp.int32, (1, rows), 1)
    hot = jnp.zeros((1, rows), jnp.int32)
    start = jnp.int32(0)
    for prompt in range(length_ref.shape[0]):
        end = start + length_ref[prompt]
        hot = jnp.where((row_ids >= start) & (row_ids < end), index_ref[prompt], hot)
        start = end
    return hot


def partial_kernel(rank, hot_count, adapter_device, plan_ref, length_ref, index_ref, *refs):
    local = refs[:PLANE]
    arrived = refs[PLANE : PLANE + PLANES - 1]
    refs = refs[PLANE + PLANES - 1 :]
    tokens = refs[:PLANE]
    outs = refs[PLANE : 2 * PLANE]
    down_ref, sems = refs[2 * PLANE :]
    waits = start_rows(
        plan_ref,
        hot_count,
        adapter_device,
        local,
        arrived,
        lambda entry, source: pltpu.make_async_copy(
            source.at[pl.ds(0, rank), :],
            down_ref.at[pl.ds(entry * rank, rank), :],
            sems.at[entry],
        ),
    )
    for wait in waits:
        wait.wait()
    rows = tokens[0].shape[0]
    device = lax.axis_index("seq")
    for distance in range(PLANE):
        product = lax.dot_general(
            down_ref[...],
            tokens[distance][...],
            (((1,), (1,)), ((), ())),
            preferred_element_type=jnp.float32,
        )
        hot = hot_lanes((device ^ distance) * rows, rows, length_ref, index_ref)
        total = jnp.zeros((rank, rows), jnp.float32)
        for entry in range(hot_count):
            total = jnp.where(hot == entry, product[entry * rank : (entry + 1) * rank], total)
        outs[distance][...] = total


def finish_kernel(
    length_ref, index_ref, base_ref, cosine_ref, sine_ref, slot_ref, *refs
):
    partials = refs[:PLANE]
    ups = refs[PLANE : 2 * PLANE]
    out_ref, low_ref, rows_ref = refs[2 * PLANE :]
    hot_count, part, key_width = ups[0].shape
    rows = base_ref.shape[0]
    device = lax.axis_index("seq")
    place = lax.rem(device, PLANE)
    total = partials[0][...]
    for distance in range(1, PLANE):
        total = total + partials[distance][...]
    low_ref[...] = total
    hot = hot_lanes(device * rows, rows, length_ref, index_ref)
    projected = base_ref[...]
    for distance in range(PLANE):
        first = pl.multiple_of((place ^ distance) * part, part)
        piece = low_ref[pl.ds(first, part), :].astype(jnp.bfloat16).astype(jnp.float32)
        spread_rows = jnp.concatenate(
            [jnp.where(hot == entry, piece, 0.0) for entry in range(hot_count)], axis=0
        ).astype(jnp.bfloat16)
        projected = projected + lax.dot_general(
            spread_rows,
            ups[distance][...].reshape(hot_count * part, key_width),
            (((0,), (0,)), ((), ())),
            preferred_element_type=jnp.float32,
        )
    cosine = cosine_ref[...]
    sine = sine_ref[...]
    for head in range(key_width // HEAD):
        columns = slice(head * HEAD, (head + 1) * HEAD)
        values = projected[:, columns]
        turned = values * cosine + pltpu.roll(values, HEAD // 2, 1) * sine
        rows_ref[:, columns] = turned.astype(jnp.bfloat16)
    slots = lax.broadcasted_iota(jnp.int32, (out_ref.shape[0], rows), 0)
    placed = (slots == slot_ref[...]).astype(jnp.bfloat16)
    out_ref[...] = jnp.dot(
        placed, rows_ref[...], preferred_element_type=jnp.float32
    ).astype(jnp.bfloat16)


def turn_tables(positions):
    half_head = HEAD // 2
    frequencies = rope_theta ** (-(jnp.arange(half_head, dtype=jnp.float32) * 2.0) / HEAD)
    angles = positions.astype(jnp.float32)[:, None] * frequencies[None, :]
    cosine = jnp.cos(angles)
    sine = jnp.sin(angles)
    return (
        jnp.concatenate([cosine, cosine], axis=1),
        jnp.concatenate([-sine, sine], axis=1),
    )


def planes_outgoing(
    normed,
    key_matrix,
    adapter_down_weight,
    adapter_up_weight,
    lengths,
    prompt_adapter_index,
    active_adapter_ids,
    positions,
    slot_index,
    out_rows,
):
    peer_count = PLANE * PLANES
    rows, width = normed.shape
    quarter = width // PLANE
    adapter_device, rank, key_width = adapter_up_weight.shape
    part = rank // PLANE
    hot_count = active_adapter_ids.shape[0]
    place = lax.axis_index("seq") % PLANE
    prompt_index = prompt_adapter_index[:, 0]
    plan = call(
        functools.partial(plan_kernel, PLANE * rows, adapter_device),
        jax.ShapeDtypeStruct((plan_size(hot_count),), jnp.int32),
        [SMEM] * 3,
        SMEM,
    )(lengths, prompt_index, active_adapter_ids)
    piece = jax.ShapeDtypeStruct((adapter_device, rank + part, quarter), jnp.bfloat16)
    packed = call(
        functools.partial(pack_kernel, quarter),
        [piece] * PLANE,
        [ANY, ANY],
        [ANY] * PLANE,
        [pltpu.SemaphoreType.DMA((2 * PLANE,))],
    )(jnp.swapaxes(adapter_down_weight, 1, 2), adapter_up_weight)
    local = [packed[0]] + [
        swap(packed[distance], distance, peer_count) for distance in range(1, PLANE)
    ]
    columns = [
        lax.dynamic_slice_in_dim(normed, (place ^ distance) * quarter, quarter, 1)
        for distance in range(PLANE)
    ]
    base = jnp.dot(normed, key_matrix, preferred_element_type=jnp.float32)
    cosine, sine = turn_tables(positions)

    def branch(slots):
        def run(plan, lengths, prompt_index, base, cosine, sine, slot_index, columns, local):
            sends = call(
                functools.partial(select_kernel, slots, hot_count, adapter_device),
                [
                    jax.ShapeDtypeStruct((count, rank + part, quarter), jnp.bfloat16)
                    for count in slots
                ],
                [SMEM] + [ANY] * PLANE,
                [ANY] * len(slots),
                [pltpu.SemaphoreType.DMA((sum(slots),))],
            )(plan, *local)
            arrived = [
                swap(send, (at + 1) * PLANE, peer_count) for at, send in enumerate(sends)
            ]
            tokens = [columns[0]] + [
                swap(columns[distance], distance, peer_count) for distance in range(1, PLANE)
            ]
            up_rows = call(
                functools.partial(collect_kernel, rank, hot_count, adapter_device),
                jax.ShapeDtypeStruct((hot_count, part, key_width), jnp.bfloat16),
                [SMEM] + [ANY] * (PLANE + PLANES - 1),
                ANY,
                [pltpu.SemaphoreType.DMA((hot_count,))],
            )(plan, *local, *arrived)
            ups = [up_rows] + [
                swap(up_rows, distance, peer_count) for distance in range(1, PLANE)
            ]
            partials = call(
                functools.partial(partial_kernel, rank, hot_count, adapter_device),
                [jax.ShapeDtypeStruct((rank, rows), jnp.float32)] * PLANE,
                [SMEM] * 3 + [ANY] * (PLANE + PLANES - 1) + [VMEM] * PLANE,
                [VMEM] * PLANE,
                [
                    pltpu.VMEM((hot_count * rank, quarter), jnp.bfloat16),
                    pltpu.SemaphoreType.DMA((hot_count,)),
                ],
                flops=2 * hot_count * rank * width * rows,
                bytes_accessed=6 * 1024 * 1024,
            )(plan, lengths, prompt_index, *local, *arrived, *tokens)
            partials = [partials[0]] + [
                swap(partials[distance], distance, peer_count) for distance in range(1, PLANE)
            ]
            return call(
                finish_kernel,
                jax.ShapeDtypeStruct((out_rows, key_width), jnp.bfloat16),
                [SMEM] * 2 + [VMEM] * (4 + 2 * PLANE),
                VMEM,
                [
                    pltpu.VMEM((rank, rows), jnp.float32),
                    pltpu.VMEM((rows, key_width), jnp.bfloat16),
                ],
                flops=2 * rows * key_width * (hot_count * rank + out_rows),
                bytes_accessed=6 * 1024 * 1024,
            )(
                lengths,
                prompt_index,
                base,
                cosine,
                sine,
                slot_index.reshape(1, rows),
                *partials,
                *ups,
            )

        return run

    cases = [branch(slots) for slots in SLOT_CASES + ((hot_count,) * (PLANES - 1),)]
    return lax.switch(
        plan[5 * hot_count],
        cases,
        plan,
        lengths,
        prompt_index,
        base,
        cosine,
        sine,
        slot_index,
        columns,
        local,
    )


def gathered_outgoing(
    normed,
    key_matrix,
    adapter_down_weight,
    adapter_up_weight,
    active_adapter_ids,
    positions,
    hot_slots,
    slot_index,
    out_rows,
):
    adapter_device = adapter_down_weight.shape[0]
    down_list = []
    up_list = []
    for entry in range(active_adapter_ids.shape[0]):
        adapter = active_adapter_ids[entry]
        for weight, gathered in ((adapter_down_weight, down_list), (adapter_up_weight, up_list)):
            mine = lax.dynamic_index_in_dim(weight, adapter % adapter_device, 0, keepdims=False)
            gathered.append(spread(mine, "seq", adapter // adapter_device))
    down_matrices = jnp.concatenate(down_list, axis=1)
    up_matrices = jnp.concatenate(up_list, axis=0)
    base_proj = jnp.dot(normed, key_matrix, preferred_element_type=jnp.float32)
    low_rank = jnp.dot(normed, down_matrices, preferred_element_type=jnp.float32).astype(
        jnp.bfloat16
    )
    column_owned = (jnp.arange(down_matrices.shape[1], dtype=jnp.int32) // ADAPTER_RANK)[
        None, :
    ] == hot_slots[:, None]
    low_rank = jnp.where(column_owned, low_rank, jnp.zeros_like(low_rank))
    projected = base_proj + jnp.dot(low_rank, up_matrices, preferred_element_type=jnp.float32)
    key_rows = rotate(projected, positions).astype(jnp.bfloat16)
    return jnp.zeros((out_rows, key_rows.shape[1]), jnp.bfloat16).at[slot_index].set(key_rows)


def on_device(
    tokens,
    input_norm_scale,
    key_matrix,
    adapter_down_weight,
    adapter_up_weight,
    lengths,
    prompt_adapter_index,
    active_adapter_ids,
    token_cache_device,
):
    rows_dev = tokens.shape[0]
    peer_count = lax.axis_size("seq")
    slot_count = max(4, 2 * rows_dev // peer_count)
    key_width = key_matrix.shape[1]
    targets = token_cache_device[:, 0]
    row_order = jnp.arange(rows_dev, dtype=jnp.int32)
    earlier = row_order[None, :] < row_order[:, None]
    rank_within = jnp.sum(
        ((targets[:, None] == targets[None, :]) & earlier).astype(jnp.int32), axis=1
    )
    slot_index = targets * slot_count + rank_within
    positions, hot_slots = locate(
        lengths, prompt_adapter_index, lax.axis_index("seq") * rows_dev, rows_dev
    )
    float_rows = tokens.astype(jnp.float32)
    inverse_rms = lax.rsqrt(jnp.mean(float_rows * float_rows, axis=1, keepdims=True) + norm_eps)
    normed = (float_rows * inverse_rms * input_norm_scale[None, :]).astype(jnp.bfloat16)
    out_rows = peer_count * slot_count
    if peer_count == PLANE * PLANES:
        outgoing = planes_outgoing(
            normed,
            key_matrix,
            adapter_down_weight,
            adapter_up_weight,
            lengths,
            prompt_adapter_index,
            active_adapter_ids,
            positions,
            slot_index,
            out_rows,
        )
    else:
        outgoing = gathered_outgoing(
            normed,
            key_matrix,
            adapter_down_weight,
            adapter_up_weight,
            active_adapter_ids,
            positions,
            hot_slots,
            slot_index,
            out_rows,
        )
    outgoing = outgoing.reshape(peer_count, slot_count, key_width)
    result = lax.all_to_all(outgoing, "seq", split_axis=0, concat_axis=0, tiled=True)
    return result.reshape(out_rows, key_width)


def solution(mesh):
    in_specs = (
        P(("groups", "seq"), None),
        P(),
        P(),
        P("seq", None, None),
        P("seq", None, None),
        P("groups"),
        P("groups", None),
        P("groups"),
        P(("groups", "seq"), None),
    )
    out_specs = P(("groups", "seq"), None)
    return jax.shard_map(
        on_device, mesh=mesh, in_specs=in_specs, out_specs=out_specs, check_vma=False
    )
```

```python
import functools

import jax
import jax.numpy as jnp
from jax import lax
from jax.experimental import pallas as pl
from jax.experimental.pallas import tpu as pltpu
from jax.sharding import PartitionSpec as P

HEAD = 128
ADAPTER_RANK = 64


rope_theta = 500000.0
norm_eps = 1e-05


def spread(array, axis, root):
    mine = lax.axis_index(axis) == root
    return lax.psum(jnp.where(mine, array, jnp.zeros_like(array)), axis)


def rotate(projected, positions):
    half_head = HEAD // 2
    frequencies = rope_theta ** (-(jnp.arange(half_head, dtype=jnp.float32) * 2.0) / HEAD)
    angles = positions.astype(jnp.float32)[:, None] * frequencies[None, :]
    cosine = jnp.cos(angles)[:, None, :]
    sine_table = jnp.sin(angles)[:, None, :]
    per_head = projected.reshape(projected.shape[0], -1, HEAD)
    first_half = per_head[..., :half_head]
    second_half = per_head[..., half_head:]
    turned = jnp.concatenate(
        [
            first_half * cosine - second_half * sine_table,
            second_half * cosine + first_half * sine_table,
        ],
        axis=-1,
    )
    return turned.reshape(projected.shape)


def locate(lengths, prompt_adapter_index, first_row, row_count):
    prompt_ends = jnp.cumsum(lengths)
    prompt_starts = prompt_ends - lengths
    row_ids = first_row + jnp.arange(row_count, dtype=jnp.int32)
    prompt_ids = jnp.sum((prompt_ends[None, :] <= row_ids[:, None]).astype(jnp.int32), axis=1)
    prompt_match = prompt_ids[:, None] == jnp.arange(lengths.shape[0], dtype=jnp.int32)[None, :]
    prompt_start = jnp.sum(jnp.where(prompt_match, prompt_starts[None, :], 0), axis=1)
    hot_slots = jnp.sum(jnp.where(prompt_match, prompt_adapter_index[:, 0][None, :], 0), axis=1)
    return (row_ids - prompt_start, hot_slots)


PLANE = 4
PLANES = 4
SLOT_CASES = ((2, 1, 1), (2, 2, 1), (2, 1, 2), (2, 2, 2), (3, 3, 3))
FEW = 4
ANY = pl.BlockSpec(memory_space=pl.ANY)
HBM = pl.BlockSpec(memory_space=pltpu.HBM)
SMEM = pl.BlockSpec(memory_space=pltpu.SMEM)
VMEM = pl.BlockSpec(memory_space=pltpu.VMEM)
VMEM_LIMIT = 40 * 1024 * 1024


def swap(value, distance, peer_count):
    return lax.ppermute(value, "seq", [(i, i ^ distance) for i in range(peer_count)])


def call(kernel, out_shape, in_specs, out_specs, scratch=(), **cost):
    return pl.pallas_call(
        kernel,
        out_shape=out_shape,
        in_specs=in_specs,
        out_specs=out_specs,
        scratch_shapes=list(scratch),
        compiler_params=pltpu.CompilerParams(vmem_limit_bytes=VMEM_LIMIT),
        cost_estimate=pl.CostEstimate(transcendentals=0, **cost) if cost else None,
    )


FROM_KIND, FROM_SLOT, PLANE_LIST, DEVICE_LISTS, SECTIONS = 3, 4, 5, 6, 10


def bit_of(mask, entry):
    return lax.shift_right_logical(mask, entry) & 1


def plan_kernel(rows, adapter_device, length_ref, index_ref, id_ref, plan_ref):
    hot_count = id_ref.shape[0]
    device = lax.axis_index("seq")
    plane = lax.div(device, PLANE)
    place = device - plane * PLANE
    for at in range(FROM_KIND * hot_count):
        plan_ref[at] = 0
    for at in range(PLANE_LIST * hot_count, SECTIONS * hot_count):
        plan_ref[at] = -1
    devices = PLANE * PLANES
    uses = [jnp.int32(0)] * devices
    start = jnp.int32(0)
    for prompt in range(length_ref.shape[0]):
        end = start + length_ref[prompt]
        bit = lax.shift_left(jnp.int32(1), index_ref[prompt])
        for at in range(devices):
            hit = (start < (at + 1) * rows) & (end > at * rows)
            uses[at] = uses[at] | jnp.where(hit, bit, 0)
        start = end
    need = []
    for at in range(PLANES):
        mask = uses[at * PLANE]
        for inner in range(1, PLANE):
            mask = mask | uses[at * PLANE + inner]
        need.append(mask)

    def pick(masks, which):
        total = masks[0]
        for at in range(1, len(masks)):
            total = jnp.where(which == at, masks[at], total)
        return total

    def list_bits(section, mask):
        count = jnp.int32(0)
        for entry in range(hot_count):

            @pl.when(bit_of(mask, entry) == 1)
            def _():
                plan_ref[section * hot_count + count] = entry

            count = count + bit_of(mask, entry)
        return count

    owner_plane = []
    kind = []
    slot = []
    local = []
    for entry in range(hot_count):
        adapter = id_ref[entry]
        owner = lax.div(adapter, adapter_device)
        owner_plane.append(lax.div(owner, PLANE))
        local.append(
            ((owner - owner_plane[entry] * PLANE) ^ place) * adapter_device
            + adapter
            - owner * adapter_device
        )
        kind.append(jnp.int32(0))
        slot.append(local[entry])
    need_here = pick(need, plane)
    for distance in range(1, PLANES):
        other = plane ^ distance
        need_there = pick(need, other)
        sent = jnp.int32(0)
        taken = jnp.int32(0)
        for entry in range(hot_count):
            plan_ref[(distance - 1) * hot_count + sent] = local[entry]
            sent = sent + jnp.where(owner_plane[entry] == plane, bit_of(need_there, entry), 0)
            wanted = jnp.where(owner_plane[entry] == other, bit_of(need_here, entry), 0)
            kind[entry] = jnp.where(wanted == 1, distance, kind[entry])
            slot[entry] = jnp.where(wanted == 1, taken, slot[entry])
            taken = taken + wanted
    for entry in range(hot_count):
        plan_ref[FROM_KIND * hot_count + entry] = kind[entry]
        plan_ref[FROM_SLOT * hot_count + entry] = slot[entry]
    plan_ref[SECTIONS * hot_count] = list_bits(PLANE_LIST, need_here)
    for distance in range(PLANE):
        list_bits(DEVICE_LISTS + distance, pick(uses, device ^ distance))
    most = []
    for distance in range(1, PLANES):
        largest = jnp.int32(0)
        for at in range(PLANES):
            count = jnp.int32(0)
            for entry in range(hot_count):
                wanted = bit_of(need[at ^ distance], entry)
                count = count + jnp.where(owner_plane[entry] == at, wanted, 0)
            largest = jnp.maximum(largest, count)
        most.append(largest)
    few = jnp.bool_(True)
    for at in range(devices):
        count = jnp.int32(0)
        for entry in range(hot_count):
            count = count + bit_of(uses[at], entry)
        few = few & (count <= FEW)
    case = jnp.int32(len(SLOT_CASES))
    for at in reversed(range(len(SLOT_CASES))):
        fits = few
        for distance in range(PLANES - 1):
            fits = fits & (most[distance] <= SLOT_CASES[at][distance])
        case = jnp.where(fits, at, case)
    plan_ref[SECTIONS * hot_count + 1] = case


def norm_kernel(token_ref, scale_ref, out_ref, *quarter_refs):
    values = token_ref[...].astype(jnp.float32)
    inverse_rms = lax.rsqrt(jnp.mean(values * values, axis=1, keepdims=True) + norm_eps)
    out_ref[...] = (values * inverse_rms * scale_ref[...]).astype(jnp.bfloat16)
    place = lax.rem(lax.axis_index("seq"), PLANE)
    quarter = quarter_refs[0].shape[1]
    for distance in range(PLANE):
        first = pl.multiple_of((place ^ distance) * quarter, quarter)
        quarter_refs[distance][...] = out_ref[:, pl.ds(first, quarter)]


def pack_kernel(quarter, down_ref, up_ref, *refs):
    outs = refs[:PLANE]
    sems = refs[PLANE]
    place = lax.rem(lax.axis_index("seq"), PLANE)
    rank = down_ref.shape[1]
    part = rank // PLANE
    copies = []
    for distance in range(PLANE):
        other = place ^ distance
        columns = pl.ds(pl.multiple_of(other * quarter, quarter), quarter)
        copies.append(
            pltpu.make_async_copy(
                down_ref.at[:, :, columns],
                outs[distance].at[:, pl.ds(0, rank), :],
                sems.at[2 * distance],
            )
        )
        rows = pl.ds(pl.multiple_of(other * part, part), part)
        copies.append(
            pltpu.make_async_copy(
                up_ref.at[:, rows, :],
                outs[distance].at[:, pl.ds(rank, part), :],
                sems.at[2 * distance + 1],
            )
        )
    for copy in copies:
        copy.start()
    for copy in copies:
        copy.wait()


def select_kernel(slots, hot_count, adapter_device, plan_ref, *refs):
    local = refs[:PLANE]
    outs = refs[PLANE : PLANE + PLANES - 1]
    sems = refs[-1]
    waits = []
    for distance in range(1, PLANES):
        for slot in range(slots[distance - 1]):
            index = plan_ref[(distance - 1) * hot_count + slot]
            holder = lax.div(index, adapter_device)
            inner = index - holder * adapter_device
            target = outs[distance - 1].at[slot]
            sem = sems.at[len(waits)]
            for at in range(PLANE):

                @pl.when(holder == at)
                def _():
                    pltpu.make_async_copy(local[at].at[inner], target, sem).start()

            waits.append(pltpu.make_async_copy(local[0].at[0], target, sem))
    for wait in waits:
        wait.wait()


def start_rows(plan_ref, entry, hot_count, adapter_device, local, arrived, copy_of):
    kind = plan_ref[FROM_KIND * hot_count + entry]
    slot = plan_ref[FROM_SLOT * hot_count + entry]
    holder = lax.div(slot, adapter_device)
    inner = slot - holder * adapter_device
    for at in range(PLANE):

        @pl.when((kind == 0) & (holder == at))
        def _():
            copy_of(local[at].at[inner]).start()

    for distance in range(1, PLANES):

        @pl.when(kind == distance)
        def _():
            copy_of(arrived[distance - 1].at[slot]).start()


def collect_kernel(rank, hot_count, adapter_device, plan_ref, *refs):
    local = refs[:PLANE]
    arrived = refs[PLANE : PLANE + PLANES - 1]
    outs = refs[PLANE + PLANES - 1 : -1]
    sems = refs[-1]
    count, part, _ = outs[0].shape
    waits = []
    for distance in range(PLANE):
        for at in range(count):
            entry = jnp.maximum(plan_ref[(DEVICE_LISTS + distance) * hot_count + at], 0)
            copy_of = lambda source, distance=distance, at=at: pltpu.make_async_copy(
                source.at[pl.ds(rank, part), :],
                outs[distance].at[at],
                sems.at[distance * count + at],
            )
            start_rows(plan_ref, entry, hot_count, adapter_device, local, arrived, copy_of)
            waits.append(copy_of(local[0].at[0]))
    for wait in waits:
        wait.wait()


def hot_lanes(first_row, rows, length_ref, index_ref):
    row_ids = first_row + lax.broadcasted_iota(jnp.int32, (1, rows), 1)
    hot = jnp.zeros((1, rows), jnp.int32)
    start = jnp.int32(0)
    for prompt in range(length_ref.shape[0]):
        end = start + length_ref[prompt]
        hot = jnp.where((row_ids >= start) & (row_ids < end), index_ref[prompt], hot)
        start = end
    return hot


def partial_kernel(rank, hot_count, adapter_device, plan_ref, length_ref, index_ref, *refs):
    local = refs[:PLANE]
    arrived = refs[PLANE : PLANE + PLANES - 1]
    refs = refs[PLANE + PLANES - 1 :]
    tokens = refs[:PLANE]
    outs = refs[PLANE : 2 * PLANE]
    down_ref, sems = refs[2 * PLANE :]
    device = lax.axis_index("seq")
    rows = tokens[0].shape[0]
    half = hot_count // 2
    entries = [plan_ref[PLANE_LIST * hot_count + at] for at in range(hot_count)]

    def copy_of(at):
        return lambda source: pltpu.make_async_copy(
            source.at[pl.ds(0, rank), :],
            down_ref.at[pl.ds(at * rank, rank), :],
            sems.at[at],
        )

    def run(first, last):
        for at in range(first, last):
            start_rows(
                plan_ref,
                jnp.maximum(entries[at], 0),
                hot_count,
                adapter_device,
                local,
                arrived,
                copy_of(at),
            )
        for at in range(first, last):
            copy_of(at)(local[0].at[0]).wait()
        for distance in range(PLANE):
            product = lax.dot_general(
                down_ref[first * rank : last * rank],
                tokens[distance][...],
                (((1,), (1,)), ((), ())),
                preferred_element_type=jnp.float32,
            )
            hot = hot_lanes((device ^ distance) * rows, rows, length_ref, index_ref)
            total = outs[distance][...] if first else jnp.zeros((rank, rows), jnp.float32)
            for at in range(first, last):
                piece = product[(at - first) * rank : (at - first + 1) * rank]
                total = jnp.where(hot == entries[at], piece, total)
            outs[distance][...] = total

    run(0, half)

    @pl.when(plan_ref[SECTIONS * hot_count] > half)
    def _():
        run(half, hot_count)


def finish_kernel(
    hot_count,
    plan_ref,
    length_ref,
    index_ref,
    base_ref,
    cosine_ref,
    sine_ref,
    slot_ref,
    *refs,
):
    partials = refs[:PLANE]
    ups = refs[PLANE : 2 * PLANE]
    out_ref, low_ref, rows_ref = refs[2 * PLANE :]
    count, part, key_width = ups[0].shape
    rows = base_ref.shape[0]
    device = lax.axis_index("seq")
    place = lax.rem(device, PLANE)
    total = partials[0][...]
    for distance in range(1, PLANE):
        total = total + partials[distance][...]
    low_ref[...] = total
    hot = hot_lanes(device * rows, rows, length_ref, index_ref)
    entries = [plan_ref[DEVICE_LISTS * hot_count + at] for at in range(count)]
    projected = base_ref[...]
    for distance in range(PLANE):
        first = pl.multiple_of((place ^ distance) * part, part)
        piece = low_ref[pl.ds(first, part), :]
        spread_rows = jnp.concatenate(
            [jnp.where(hot == entry, piece, 0.0) for entry in entries], axis=0
        ).astype(jnp.bfloat16)
        projected = projected + lax.dot_general(
            spread_rows,
            ups[distance][...].reshape(count * part, key_width),
            (((0,), (0,)), ((), ())),
            preferred_element_type=jnp.float32,
        )
    cosine = cosine_ref[...]
    sine = sine_ref[...]
    for head in range(key_width // HEAD):
        columns = slice(head * HEAD, (head + 1) * HEAD)
        values = projected[:, columns]
        turned = values * cosine + pltpu.roll(values, HEAD // 2, 1) * sine
        rows_ref[:, columns] = turned.astype(jnp.bfloat16)
    slots = lax.broadcasted_iota(jnp.int32, (out_ref.shape[0], rows), 0)
    placed = (slots == slot_ref[...]).astype(jnp.bfloat16)
    out_ref[...] = jnp.dot(
        placed, rows_ref[...], preferred_element_type=jnp.float32
    ).astype(jnp.bfloat16)


def turn_tables(positions):
    half_head = HEAD // 2
    frequencies = rope_theta ** (-(jnp.arange(half_head, dtype=jnp.float32) * 2.0) / HEAD)
    angles = positions.astype(jnp.float32)[:, None] * frequencies[None, :]
    cosine = jnp.cos(angles)
    sine = jnp.sin(angles)
    return (
        jnp.concatenate([cosine, cosine], axis=1),
        jnp.concatenate([-sine, sine], axis=1),
    )


def planes_outgoing(
    tokens,
    input_norm_scale,
    key_matrix,
    adapter_down_weight,
    adapter_up_weight,
    lengths,
    prompt_adapter_index,
    active_adapter_ids,
    positions,
    slot_index,
    out_rows,
):
    peer_count = PLANE * PLANES
    rows, width = tokens.shape
    quarter = width // PLANE
    adapter_device, rank, key_width = adapter_up_weight.shape
    part = rank // PLANE
    hot_count = active_adapter_ids.shape[0]
    prompt_index = prompt_adapter_index[:, 0]
    piece = jax.ShapeDtypeStruct((adapter_device, rank + part, quarter), jnp.bfloat16)
    packed = call(
        functools.partial(pack_kernel, quarter),
        [piece] * PLANE,
        [HBM, HBM],
        [ANY] * PLANE,
        [pltpu.SemaphoreType.DMA((2 * PLANE,))],
    )(jnp.swapaxes(adapter_down_weight, 1, 2), adapter_up_weight)
    local = [packed[0]] + [
        swap(packed[distance], distance, peer_count) for distance in range(1, PLANE)
    ]
    plan = call(
        functools.partial(plan_kernel, rows, adapter_device),
        jax.ShapeDtypeStruct((SECTIONS * hot_count + 2,), jnp.int32),
        [SMEM] * 3,
        SMEM,
    )(lengths, prompt_index, active_adapter_ids)
    block = rows // 4
    normed, *columns = pl.pallas_call(
        norm_kernel,
        grid=(4,),
        out_shape=[jax.ShapeDtypeStruct((rows, width), jnp.bfloat16)]
        + [jax.ShapeDtypeStruct((rows, quarter), jnp.bfloat16)] * PLANE,
        in_specs=[
            pl.BlockSpec((block, width), lambda at: (at, 0)),
            pl.BlockSpec((1, width), lambda at: (0, 0)),
        ],
        out_specs=[pl.BlockSpec((block, width), lambda at: (at, 0))]
        + [pl.BlockSpec((block, quarter), lambda at: (at, 0))] * PLANE,
        compiler_params=pltpu.CompilerParams(vmem_limit_bytes=VMEM_LIMIT),
    )(tokens, input_norm_scale.reshape(1, width))
    columns[1] = swap(columns[1], 1, peer_count)
    base = jnp.dot(normed, key_matrix, preferred_element_type=jnp.float32)
    cosine, sine = turn_tables(positions)

    def branch(slots, count):
        def run(plan, lengths, prompt_index, base, cosine, sine, slot_index, columns, local):
            sends = call(
                functools.partial(select_kernel, slots, hot_count, adapter_device),
                [
                    jax.ShapeDtypeStruct((slot, rank + part, quarter), jnp.bfloat16)
                    for slot in slots
                ],
                [SMEM] + [ANY] * PLANE,
                [ANY] * len(slots),
                [pltpu.SemaphoreType.DMA((sum(slots),))],
            )(plan, *local)
            arrived = [
                swap(send, (at + 1) * PLANE, peer_count) for at, send in enumerate(sends)
            ]
            tokens = columns[:2] + [
                swap(columns[distance], distance, peer_count) for distance in range(2, PLANE)
            ]
            ups = call(
                functools.partial(collect_kernel, rank, hot_count, adapter_device),
                [jax.ShapeDtypeStruct((count, part, key_width), jnp.bfloat16)] * PLANE,
                [SMEM] + [ANY] * (PLANE + PLANES - 1),
                [ANY] * PLANE,
                [pltpu.SemaphoreType.DMA((PLANE * count,))],
            )(plan, *local, *arrived)
            ups = [ups[0]] + [
                swap(ups[distance], distance, peer_count) for distance in range(1, PLANE)
            ]
            partials = call(
                functools.partial(partial_kernel, rank, hot_count, adapter_device),
                [jax.ShapeDtypeStruct((rank, rows), jnp.float32)] * PLANE,
                [SMEM] * 3 + [ANY] * (PLANE + PLANES - 1) + [VMEM] * PLANE,
                [VMEM] * PLANE,
                [
                    pltpu.VMEM((hot_count * rank, quarter), jnp.bfloat16),
                    pltpu.SemaphoreType.DMA((hot_count,)),
                ],
                flops=2 * hot_count * rank * width * rows,
                bytes_accessed=6 * 1024 * 1024,
            )(plan, lengths, prompt_index, *local, *arrived, *tokens)
            partials = [partials[0]] + [
                swap(partials[distance], distance, peer_count) for distance in range(1, PLANE)
            ]
            return call(
                functools.partial(finish_kernel, hot_count),
                jax.ShapeDtypeStruct((out_rows, key_width), jnp.bfloat16),
                [SMEM] * 3 + [VMEM] * (4 + 2 * PLANE),
                VMEM,
                [
                    pltpu.VMEM((rank, rows), jnp.float32),
                    pltpu.VMEM((rows, key_width), jnp.bfloat16),
                ],
                flops=2 * rows * key_width * (hot_count * rank + out_rows),
                bytes_accessed=6 * 1024 * 1024,
            )(
                plan,
                lengths,
                prompt_index,
                base,
                cosine,
                sine,
                slot_index.reshape(1, rows),
                *partials,
                *ups,
            )

        return run

    cases = [branch(slots, FEW) for slots in SLOT_CASES]
    cases.append(branch((hot_count,) * (PLANES - 1), hot_count))
    return lax.switch(
        plan[SECTIONS * hot_count + 1],
        cases,
        plan,
        lengths,
        prompt_index,
        base,
        cosine,
        sine,
        slot_index,
        columns,
        local,
    )


def gathered_outgoing(
    tokens,
    input_norm_scale,
    key_matrix,
    adapter_down_weight,
    adapter_up_weight,
    active_adapter_ids,
    positions,
    hot_slots,
    slot_index,
    out_rows,
):
    float_rows = tokens.astype(jnp.float32)
    inverse_rms = lax.rsqrt(jnp.mean(float_rows * float_rows, axis=1, keepdims=True) + norm_eps)
    normed = (float_rows * inverse_rms * input_norm_scale[None, :]).astype(jnp.bfloat16)
    adapter_device = adapter_down_weight.shape[0]
    down_list = []
    up_list = []
    for entry in range(active_adapter_ids.shape[0]):
        adapter = active_adapter_ids[entry]
        for weight, gathered in ((adapter_down_weight, down_list), (adapter_up_weight, up_list)):
            mine = lax.dynamic_index_in_dim(weight, adapter % adapter_device, 0, keepdims=False)
            gathered.append(spread(mine, "seq", adapter // adapter_device))
    down_matrices = jnp.concatenate(down_list, axis=1)
    up_matrices = jnp.concatenate(up_list, axis=0)
    base_proj = jnp.dot(normed, key_matrix, preferred_element_type=jnp.float32)
    low_rank = jnp.dot(normed, down_matrices, preferred_element_type=jnp.float32).astype(
        jnp.bfloat16
    )
    column_owned = (jnp.arange(down_matrices.shape[1], dtype=jnp.int32) // ADAPTER_RANK)[
        None, :
    ] == hot_slots[:, None]
    low_rank = jnp.where(column_owned, low_rank, jnp.zeros_like(low_rank))
    projected = base_proj + jnp.dot(low_rank, up_matrices, preferred_element_type=jnp.float32)
    key_rows = rotate(projected, positions).astype(jnp.bfloat16)
    return jnp.zeros((out_rows, key_rows.shape[1]), jnp.bfloat16).at[slot_index].set(key_rows)


def on_device(
    tokens,
    input_norm_scale,
    key_matrix,
    adapter_down_weight,
    adapter_up_weight,
    lengths,
    prompt_adapter_index,
    active_adapter_ids,
    token_cache_device,
):
    rows_dev = tokens.shape[0]
    peer_count = lax.axis_size("seq")
    slot_count = max(4, 2 * rows_dev // peer_count)
    key_width = key_matrix.shape[1]
    targets = token_cache_device[:, 0]
    row_order = jnp.arange(rows_dev, dtype=jnp.int32)
    earlier = row_order[None, :] < row_order[:, None]
    rank_within = jnp.sum(
        ((targets[:, None] == targets[None, :]) & earlier).astype(jnp.int32), axis=1
    )
    slot_index = targets * slot_count + rank_within
    positions, hot_slots = locate(
        lengths, prompt_adapter_index, lax.axis_index("seq") * rows_dev, rows_dev
    )
    out_rows = peer_count * slot_count
    if peer_count == PLANE * PLANES:
        outgoing = planes_outgoing(
            tokens,
            input_norm_scale,
            key_matrix,
            adapter_down_weight,
            adapter_up_weight,
            lengths,
            prompt_adapter_index,
            active_adapter_ids,
            positions,
            slot_index,
            out_rows,
        )
    else:
        outgoing = gathered_outgoing(
            tokens,
            input_norm_scale,
            key_matrix,
            adapter_down_weight,
            adapter_up_weight,
            active_adapter_ids,
            positions,
            hot_slots,
            slot_index,
            out_rows,
        )
    outgoing = outgoing.reshape(peer_count, slot_count, key_width)
    result = lax.all_to_all(outgoing, "seq", split_axis=0, concat_axis=0, tiled=True)
    return result.reshape(out_rows, key_width)


def solution(mesh):
    in_specs = (
        P(("groups", "seq"), None),
        P(),
        P(),
        P("seq", None, None),
        P("seq", None, None),
        P("groups"),
        P("groups", None),
        P("groups"),
        P(("groups", "seq"), None),
    )
    out_specs = P(("groups", "seq"), None)
    return jax.shard_map(
        on_device, mesh=mesh, in_specs=in_specs, out_specs=out_specs, check_vma=False
    )
```

```python
import functools

import jax
import jax.numpy as jnp
from jax import lax
from jax.experimental import pallas as pl
from jax.experimental.pallas import tpu as pltpu
from jax.sharding import PartitionSpec as P

HEAD = 128
ADAPTER_RANK = 64


rope_theta = 500000.0
norm_eps = 1e-05


def spread(array, axis, root):
    mine = lax.axis_index(axis) == root
    return lax.psum(jnp.where(mine, array, jnp.zeros_like(array)), axis)


def rotate(projected, positions):
    half_head = HEAD // 2
    frequencies = rope_theta ** (-(jnp.arange(half_head, dtype=jnp.float32) * 2.0) / HEAD)
    angles = positions.astype(jnp.float32)[:, None] * frequencies[None, :]
    cosine = jnp.cos(angles)[:, None, :]
    sine_table = jnp.sin(angles)[:, None, :]
    per_head = projected.reshape(projected.shape[0], -1, HEAD)
    first_half = per_head[..., :half_head]
    second_half = per_head[..., half_head:]
    turned = jnp.concatenate(
        [
            first_half * cosine - second_half * sine_table,
            second_half * cosine + first_half * sine_table,
        ],
        axis=-1,
    )
    return turned.reshape(projected.shape)


def locate(lengths, prompt_adapter_index, first_row, row_count):
    prompt_ends = jnp.cumsum(lengths)
    prompt_starts = prompt_ends - lengths
    row_ids = first_row + jnp.arange(row_count, dtype=jnp.int32)
    prompt_ids = jnp.sum((prompt_ends[None, :] <= row_ids[:, None]).astype(jnp.int32), axis=1)
    prompt_match = prompt_ids[:, None] == jnp.arange(lengths.shape[0], dtype=jnp.int32)[None, :]
    prompt_start = jnp.sum(jnp.where(prompt_match, prompt_starts[None, :], 0), axis=1)
    hot_slots = jnp.sum(jnp.where(prompt_match, prompt_adapter_index[:, 0][None, :], 0), axis=1)
    return (row_ids - prompt_start, hot_slots)


PLANE = 4
PLANES = 4
SLOT_CASES = ((2, 1, 1), (3, 2, 1), (3, 1, 2), (3, 2, 2), (3, 3, 1), (3, 1, 3), (4, 3, 3))
FEW = 4
ANY = pl.BlockSpec(memory_space=pl.ANY)
SMEM = pl.BlockSpec(memory_space=pltpu.SMEM)
VMEM = pl.BlockSpec(memory_space=pltpu.VMEM)
VMEM_LIMIT = 40 * 1024 * 1024


def swap(value, distance, peer_count):
    return lax.ppermute(value, "seq", [(i, i ^ distance) for i in range(peer_count)])


def call(kernel, out_shape, in_specs, out_specs, scratch=(), limit=VMEM_LIMIT, **cost):
    return pl.pallas_call(
        kernel,
        out_shape=out_shape,
        in_specs=in_specs,
        out_specs=out_specs,
        scratch_shapes=list(scratch),
        compiler_params=pltpu.CompilerParams(vmem_limit_bytes=limit),
        cost_estimate=pl.CostEstimate(transcendentals=0, **cost) if cost else None,
    )


FROM_KIND, FROM_SLOT, PLANE_LIST, DEVICE_LISTS, SECTIONS = 3, 4, 5, 6, 10


def bit_of(mask, entry):
    return lax.shift_right_logical(mask, entry) & 1


def plan_kernel(rows, adapter_device, length_ref, index_ref, id_ref, plan_ref):
    hot_count = id_ref.shape[0]
    device = lax.axis_index("seq")
    plane = lax.div(device, PLANE)
    place = device - plane * PLANE
    for at in range(FROM_KIND * hot_count):
        plan_ref[at] = 0
    for at in range(PLANE_LIST * hot_count, SECTIONS * hot_count):
        plan_ref[at] = -1
    devices = PLANE * PLANES
    uses = [jnp.int32(0)] * devices
    start = jnp.int32(0)
    for prompt in range(length_ref.shape[0]):
        end = start + length_ref[prompt]
        bit = lax.shift_left(jnp.int32(1), index_ref[prompt])
        for at in range(devices):
            hit = (start < (at + 1) * rows) & (end > at * rows)
            uses[at] = uses[at] | jnp.where(hit, bit, 0)
        start = end
    need = []
    for at in range(PLANES):
        mask = uses[at * PLANE]
        for inner in range(1, PLANE):
            mask = mask | uses[at * PLANE + inner]
        need.append(mask)

    def pick(masks, which):
        total = masks[0]
        for at in range(1, len(masks)):
            total = jnp.where(which == at, masks[at], total)
        return total

    def list_bits(section, mask):
        count = jnp.int32(0)
        for entry in range(hot_count):

            @pl.when(bit_of(mask, entry) == 1)
            def _():
                plan_ref[section * hot_count + count] = entry

            count = count + bit_of(mask, entry)
        return count

    owner_plane = []
    kind = []
    slot = []
    local = []
    for entry in range(hot_count):
        adapter = id_ref[entry]
        owner = lax.div(adapter, adapter_device)
        owner_plane.append(lax.div(owner, PLANE))
        local.append(
            ((owner - owner_plane[entry] * PLANE) ^ place) * adapter_device
            + adapter
            - owner * adapter_device
        )
        kind.append(jnp.int32(0))
        slot.append(local[entry])
    need_here = pick(need, plane)
    for distance in range(1, PLANES):
        other = plane ^ distance
        need_there = pick(need, other)
        sent = jnp.int32(0)
        taken = jnp.int32(0)
        for entry in range(hot_count):
            plan_ref[(distance - 1) * hot_count + sent] = local[entry]
            sent = sent + jnp.where(owner_plane[entry] == plane, bit_of(need_there, entry), 0)
            wanted = jnp.where(owner_plane[entry] == other, bit_of(need_here, entry), 0)
            kind[entry] = jnp.where(wanted == 1, distance, kind[entry])
            slot[entry] = jnp.where(wanted == 1, taken, slot[entry])
            taken = taken + wanted
    for entry in range(hot_count):
        plan_ref[FROM_KIND * hot_count + entry] = kind[entry]
        plan_ref[FROM_SLOT * hot_count + entry] = slot[entry]
    plan_ref[SECTIONS * hot_count] = list_bits(PLANE_LIST, need_here)
    for distance in range(PLANE):
        list_bits(DEVICE_LISTS + distance, pick(uses, device ^ distance))
    most = []
    for distance in range(1, PLANES):
        largest = jnp.int32(0)
        for at in range(PLANES):
            count = jnp.int32(0)
            for entry in range(hot_count):
                wanted = bit_of(need[at ^ distance], entry)
                count = count + jnp.where(owner_plane[entry] == at, wanted, 0)
            largest = jnp.maximum(largest, count)
        most.append(largest)
    few = jnp.bool_(True)
    for at in range(devices):
        count = jnp.int32(0)
        for entry in range(hot_count):
            count = count + bit_of(uses[at], entry)
        few = few & (count <= FEW)
    case = jnp.int32(len(SLOT_CASES))
    for at in reversed(range(len(SLOT_CASES))):
        fits = few
        for distance in range(PLANES - 1):
            fits = fits & (most[distance] <= SLOT_CASES[at][distance])
        case = jnp.where(fits, at, case)
    plan_ref[SECTIONS * hot_count + 1] = case


def norm_kernel(token_ref, scale_ref, out_ref, *quarter_refs):
    values = token_ref[...].astype(jnp.float32)
    inverse_rms = lax.rsqrt(jnp.mean(values * values, axis=1, keepdims=True) + norm_eps)
    out_ref[...] = (values * inverse_rms * scale_ref[...]).astype(jnp.bfloat16)
    place = lax.rem(lax.axis_index("seq"), PLANE)
    quarter = quarter_refs[0].shape[1]
    for distance in range(PLANE):
        first = pl.multiple_of((place ^ distance) * quarter, quarter)
        quarter_refs[distance][...] = out_ref[:, pl.ds(first, quarter)]


def pack_kernel(quarter, down_ref, up_ref, *refs):
    outs = refs[:PLANE]
    sems = refs[PLANE]
    place = lax.rem(lax.axis_index("seq"), PLANE)
    rank = down_ref.shape[1]
    part = rank // PLANE
    copies = []
    for distance in range(PLANE):
        other = place ^ distance
        columns = pl.ds(pl.multiple_of(other * quarter, quarter), quarter)
        copies.append(
            pltpu.make_async_copy(
                down_ref.at[:, :, columns],
                outs[distance].at[:, pl.ds(0, rank), :],
                sems.at[2 * distance],
            )
        )
        rows = pl.ds(pl.multiple_of(other * part, part), part)
        copies.append(
            pltpu.make_async_copy(
                up_ref.at[:, rows, :],
                outs[distance].at[:, pl.ds(rank, part), :],
                sems.at[2 * distance + 1],
            )
        )
    for copy in copies:
        copy.start()
    for copy in copies:
        copy.wait()


def select_kernel(slots, hot_count, adapter_device, plan_ref, *refs):
    local = refs[:PLANE]
    outs = refs[PLANE : PLANE + PLANES - 1]
    sems = refs[-1]
    waits = []
    for distance in range(1, PLANES):
        for slot in range(slots[distance - 1]):
            index = plan_ref[(distance - 1) * hot_count + slot]
            holder = lax.div(index, adapter_device)
            inner = index - holder * adapter_device
            target = outs[distance - 1].at[slot]
            sem = sems.at[len(waits)]
            for at in range(PLANE):

                @pl.when(holder == at)
                def _():
                    pltpu.make_async_copy(local[at].at[inner], target, sem).start()

            waits.append(pltpu.make_async_copy(local[0].at[0], target, sem))
    for wait in waits:
        wait.wait()


def start_rows(plan_ref, entry, hot_count, adapter_device, local, arrived, copy_of):
    kind = plan_ref[FROM_KIND * hot_count + entry]
    slot = plan_ref[FROM_SLOT * hot_count + entry]

    @pl.when(kind == 0)
    def _():
        holder = lax.div(slot, adapter_device)
        inner = slot - holder * adapter_device
        for at in range(PLANE):

            @pl.when(holder == at)
            def _():
                copy_of(local[at].at[inner]).start()

    for distance in range(1, PLANES):

        @pl.when(kind == distance)
        def _():
            copy_of(arrived[distance - 1].at[slot]).start()


def collect_kernel(rank, hot_count, adapter_device, plan_ref, *refs):
    local = refs[:PLANE]
    arrived = refs[PLANE : PLANE + PLANES - 1]
    outs = refs[PLANE + PLANES - 1 : -1]
    sems = refs[-1]
    count, part, _ = outs[0].shape
    waits = []
    for distance in range(PLANE):
        for at in range(count):
            entry = jnp.maximum(plan_ref[(DEVICE_LISTS + distance) * hot_count + at], 0)
            copy_of = lambda source, distance=distance, at=at: pltpu.make_async_copy(
                source.at[pl.ds(rank, part), :],
                outs[distance].at[at],
                sems.at[distance * count + at],
            )
            start_rows(plan_ref, entry, hot_count, adapter_device, local, arrived, copy_of)
            waits.append(copy_of(local[0].at[0]))
    for wait in waits:
        wait.wait()


def hot_lanes(first_row, rows, length_ref, index_ref):
    row_ids = first_row + lax.broadcasted_iota(jnp.int32, (1, rows), 1)
    hot = jnp.zeros((1, rows), jnp.int32)
    start = jnp.int32(0)
    for prompt in range(length_ref.shape[0]):
        end = start + length_ref[prompt]
        hot = jnp.where((row_ids >= start) & (row_ids < end), index_ref[prompt], hot)
        start = end
    return hot


def partial_kernel(rank, hot_count, adapter_device, plan_ref, length_ref, index_ref, *refs):
    local = refs[:PLANE]
    arrived = refs[PLANE : PLANE + PLANES - 1]
    refs = refs[PLANE + PLANES - 1 :]
    tokens = refs[:PLANE]
    outs = refs[PLANE : 2 * PLANE]
    down_ref, sems = refs[2 * PLANE :]
    device = lax.axis_index("seq")
    rows = tokens[0].shape[0]
    half = hot_count // 2
    entries = [plan_ref[PLANE_LIST * hot_count + at] for at in range(hot_count)]

    def copy_of(at):
        return lambda source: pltpu.make_async_copy(
            source.at[pl.ds(0, rank), :],
            down_ref.at[pl.ds(at * rank, rank), :],
            sems.at[at],
        )

    def run(first, last):
        for at in range(first, last):
            start_rows(
                plan_ref,
                jnp.maximum(entries[at], 0),
                hot_count,
                adapter_device,
                local,
                arrived,
                copy_of(at),
            )
        for at in range(first, last):
            copy_of(at)(local[0].at[0]).wait()
        down = down_ref[first * rank : last * rank].T
        for distance in range(PLANE):
            product = jnp.dot(
                tokens[distance][...], down, preferred_element_type=jnp.float32
            ).T
            hot = hot_lanes((device ^ distance) * rows, rows, length_ref, index_ref)
            total = outs[distance][...] if first else jnp.zeros((rank, rows), jnp.float32)
            for at in range(first, last):
                piece = product[(at - first) * rank : (at - first + 1) * rank]
                total = jnp.where(hot == entries[at], piece, total)
            outs[distance][...] = total

    run(0, half)

    @pl.when(plan_ref[SECTIONS * hot_count] > half)
    def _():
        run(half, hot_count)


def finish_kernel(
    hot_count,
    plan_ref,
    length_ref,
    index_ref,
    base_ref,
    cosine_ref,
    sine_ref,
    slot_ref,
    *refs,
):
    partials = refs[:PLANE]
    ups = refs[PLANE : 2 * PLANE]
    out_ref, low_ref, rows_ref = refs[2 * PLANE :]
    count, part, key_width = ups[0].shape
    rows = base_ref.shape[0]
    device = lax.axis_index("seq")
    place = lax.rem(device, PLANE)
    total = partials[0][...]
    for distance in range(1, PLANE):
        total = total + partials[distance][...]
    low_ref[...] = total
    hot = hot_lanes(device * rows, rows, length_ref, index_ref)
    entries = [plan_ref[DEVICE_LISTS * hot_count + at] for at in range(count)]
    projected = base_ref[...]
    for distance in range(PLANE):
        first = pl.multiple_of((place ^ distance) * part, part)
        piece = low_ref[pl.ds(first, part), :]
        spread_rows = jnp.concatenate(
            [jnp.where(hot == entry, piece, 0.0) for entry in entries], axis=0
        ).astype(jnp.bfloat16)
        projected = projected + lax.dot_general(
            spread_rows,
            ups[distance][...].reshape(count * part, key_width),
            (((0,), (0,)), ((), ())),
            preferred_element_type=jnp.float32,
        )
    cosine = cosine_ref[...]
    sine = sine_ref[...]
    for head in range(key_width // HEAD):
        columns = slice(head * HEAD, (head + 1) * HEAD)
        values = projected[:, columns]
        turned = values * cosine + pltpu.roll(values, HEAD // 2, 1) * sine
        rows_ref[:, columns] = turned.astype(jnp.bfloat16)
    slots = lax.broadcasted_iota(jnp.int32, (out_ref.shape[0], rows), 0)
    placed = (slots == slot_ref[...]).astype(jnp.bfloat16)
    out_ref[...] = jnp.dot(
        placed, rows_ref[...], preferred_element_type=jnp.float32
    ).astype(jnp.bfloat16)


def turn_tables(positions):
    half_head = HEAD // 2
    frequencies = rope_theta ** (-(jnp.arange(half_head, dtype=jnp.float32) * 2.0) / HEAD)
    angles = positions.astype(jnp.float32)[:, None] * frequencies[None, :]
    cosine = jnp.cos(angles)
    sine = jnp.sin(angles)
    return (
        jnp.concatenate([cosine, cosine], axis=1),
        jnp.concatenate([-sine, sine], axis=1),
    )


def planes_outgoing(
    tokens,
    input_norm_scale,
    key_matrix,
    adapter_down_weight,
    adapter_up_weight,
    lengths,
    prompt_adapter_index,
    active_adapter_ids,
    positions,
    slot_index,
    out_rows,
):
    peer_count = PLANE * PLANES
    rows, width = tokens.shape
    quarter = width // PLANE
    adapter_device, rank, key_width = adapter_up_weight.shape
    part = rank // PLANE
    hot_count = active_adapter_ids.shape[0]
    prompt_index = prompt_adapter_index[:, 0]
    piece = jax.ShapeDtypeStruct((adapter_device, rank + part, quarter), jnp.bfloat16)
    packed = call(
        functools.partial(pack_kernel, quarter),
        [piece] * PLANE,
        [ANY, ANY],
        [ANY] * PLANE,
        [pltpu.SemaphoreType.DMA((2 * PLANE,))],
        60 * 1024 * 1024,
    )(jnp.swapaxes(adapter_down_weight, 1, 2), adapter_up_weight)
    local = [packed[0]] + [
        swap(packed[distance], distance, peer_count) for distance in range(1, PLANE)
    ]
    plan = call(
        functools.partial(plan_kernel, rows, adapter_device),
        jax.ShapeDtypeStruct((SECTIONS * hot_count + 2,), jnp.int32),
        [SMEM] * 3,
        SMEM,
    )(lengths, prompt_index, active_adapter_ids)
    block = rows // 4
    normed, *columns = pl.pallas_call(
        norm_kernel,
        grid=(4,),
        out_shape=[jax.ShapeDtypeStruct((rows, width), jnp.bfloat16)]
        + [jax.ShapeDtypeStruct((rows, quarter), jnp.bfloat16)] * PLANE,
        in_specs=[
            pl.BlockSpec((block, width), lambda at: (at, 0)),
            pl.BlockSpec((1, width), lambda at: (0, 0)),
        ],
        out_specs=[pl.BlockSpec((block, width), lambda at: (at, 0))]
        + [pl.BlockSpec((block, quarter), lambda at: (at, 0))] * PLANE,
        compiler_params=pltpu.CompilerParams(vmem_limit_bytes=VMEM_LIMIT),
    )(tokens, input_norm_scale.reshape(1, width))
    columns[1] = swap(columns[1], 1, peer_count)
    base = jnp.dot(normed, key_matrix, preferred_element_type=jnp.float32)
    cosine, sine = turn_tables(positions)

    def branch(slots, count):
        def run(plan, lengths, prompt_index, base, cosine, sine, slot_index, columns, local):
            sends = call(
                functools.partial(select_kernel, slots, hot_count, adapter_device),
                [
                    jax.ShapeDtypeStruct((slot, rank + part, quarter), jnp.bfloat16)
                    for slot in slots
                ],
                [SMEM] + [ANY] * PLANE,
                [ANY] * len(slots),
                [pltpu.SemaphoreType.DMA((sum(slots),))],
            )(plan, *local)
            *sends, third, fourth = lax.optimization_barrier((*sends, *columns[2:]))
            columns = columns[:2] + [third, fourth]
            arrived = [
                swap(send, (at + 1) * PLANE, peer_count) for at, send in enumerate(sends)
            ]
            tokens = columns[:2] + [
                swap(columns[distance], distance, peer_count) for distance in range(2, PLANE)
            ]
            ups = call(
                functools.partial(collect_kernel, rank, hot_count, adapter_device),
                [jax.ShapeDtypeStruct((count, part, key_width), jnp.bfloat16)] * PLANE,
                [SMEM] + [ANY] * (PLANE + PLANES - 1),
                [ANY] * PLANE,
                [pltpu.SemaphoreType.DMA((PLANE * count,))],
            )(plan, *local, *arrived)
            ups = [ups[0]] + [
                swap(ups[distance], distance, peer_count) for distance in range(1, PLANE)
            ]
            partials = call(
                functools.partial(partial_kernel, rank, hot_count, adapter_device),
                [jax.ShapeDtypeStruct((rank, rows), jnp.float32)] * PLANE,
                [SMEM] * 3 + [ANY] * (PLANE + PLANES - 1) + [VMEM] * PLANE,
                [VMEM] * PLANE,
                [
                    pltpu.VMEM((hot_count * rank, quarter), jnp.bfloat16),
                    pltpu.SemaphoreType.DMA((hot_count,)),
                ],
                flops=2 * hot_count * rank * width * rows,
                bytes_accessed=6 * 1024 * 1024,
            )(plan, lengths, prompt_index, *local, *arrived, *tokens)
            partials = [partials[0]] + [
                swap(partials[distance], distance, peer_count) for distance in range(1, PLANE)
            ]
            return call(
                functools.partial(finish_kernel, hot_count),
                jax.ShapeDtypeStruct((out_rows, key_width), jnp.bfloat16),
                [SMEM] * 3 + [VMEM] * (4 + 2 * PLANE),
                VMEM,
                [
                    pltpu.VMEM((rank, rows), jnp.float32),
                    pltpu.VMEM((rows, key_width), jnp.bfloat16),
                ],
                flops=2 * rows * key_width * (hot_count * rank + out_rows),
                bytes_accessed=6 * 1024 * 1024,
            )(
                plan,
                lengths,
                prompt_index,
                base,
                cosine,
                sine,
                slot_index.reshape(1, rows),
                *partials,
                *ups,
            )

        return run

    cases = [branch(slots, FEW) for slots in SLOT_CASES]
    cases.append(branch((hot_count,) * (PLANES - 1), hot_count))
    return lax.switch(
        plan[SECTIONS * hot_count + 1],
        cases,
        plan,
        lengths,
        prompt_index,
        base,
        cosine,
        sine,
        slot_index,
        columns,
        local,
    )


def gathered_outgoing(
    tokens,
    input_norm_scale,
    key_matrix,
    adapter_down_weight,
    adapter_up_weight,
    active_adapter_ids,
    positions,
    hot_slots,
    slot_index,
    out_rows,
):
    float_rows = tokens.astype(jnp.float32)
    inverse_rms = lax.rsqrt(jnp.mean(float_rows * float_rows, axis=1, keepdims=True) + norm_eps)
    normed = (float_rows * inverse_rms * input_norm_scale[None, :]).astype(jnp.bfloat16)
    adapter_device = adapter_down_weight.shape[0]
    down_list = []
    up_list = []
    for entry in range(active_adapter_ids.shape[0]):
        adapter = active_adapter_ids[entry]
        for weight, gathered in ((adapter_down_weight, down_list), (adapter_up_weight, up_list)):
            mine = lax.dynamic_index_in_dim(weight, adapter % adapter_device, 0, keepdims=False)
            gathered.append(spread(mine, "seq", adapter // adapter_device))
    down_matrices = jnp.concatenate(down_list, axis=1)
    up_matrices = jnp.concatenate(up_list, axis=0)
    base_proj = jnp.dot(normed, key_matrix, preferred_element_type=jnp.float32)
    low_rank = jnp.dot(normed, down_matrices, preferred_element_type=jnp.float32).astype(
        jnp.bfloat16
    )
    column_owned = (jnp.arange(down_matrices.shape[1], dtype=jnp.int32) // ADAPTER_RANK)[
        None, :
    ] == hot_slots[:, None]
    low_rank = jnp.where(column_owned, low_rank, jnp.zeros_like(low_rank))
    projected = base_proj + jnp.dot(low_rank, up_matrices, preferred_element_type=jnp.float32)
    key_rows = rotate(projected, positions).astype(jnp.bfloat16)
    return jnp.zeros((out_rows, key_rows.shape[1]), jnp.bfloat16).at[slot_index].set(key_rows)


def on_device(
    tokens,
    input_norm_scale,
    key_matrix,
    adapter_down_weight,
    adapter_up_weight,
    lengths,
    prompt_adapter_index,
    active_adapter_ids,
    token_cache_device,
):
    rows_dev = tokens.shape[0]
    peer_count = lax.axis_size("seq")
    slot_count = max(4, 2 * rows_dev // peer_count)
    key_width = key_matrix.shape[1]
    targets = token_cache_device[:, 0]
    row_order = jnp.arange(rows_dev, dtype=jnp.int32)
    earlier = row_order[None, :] < row_order[:, None]
    rank_within = jnp.sum(
        ((targets[:, None] == targets[None, :]) & earlier).astype(jnp.int32), axis=1
    )
    slot_index = targets * slot_count + rank_within
    positions, hot_slots = locate(
        lengths, prompt_adapter_index, lax.axis_index("seq") * rows_dev, rows_dev
    )
    out_rows = peer_count * slot_count
    if peer_count == PLANE * PLANES:
        outgoing = planes_outgoing(
            tokens,
            input_norm_scale,
            key_matrix,
            adapter_down_weight,
            adapter_up_weight,
            lengths,
            prompt_adapter_index,
            active_adapter_ids,
            positions,
            slot_index,
            out_rows,
        )
    else:
        outgoing = gathered_outgoing(
            tokens,
            input_norm_scale,
            key_matrix,
            adapter_down_weight,
            adapter_up_weight,
            active_adapter_ids,
            positions,
            hot_slots,
            slot_index,
            out_rows,
        )
    outgoing = outgoing.reshape(peer_count, slot_count, key_width)
    result = lax.all_to_all(outgoing, "seq", split_axis=0, concat_axis=0, tiled=True)
    return result.reshape(out_rows, key_width)


def solution(mesh):
    in_specs = (
        P(("groups", "seq"), None),
        P(),
        P(),
        P("seq", None, None),
        P("seq", None, None),
        P("groups"),
        P("groups", None),
        P("groups"),
        P(("groups", "seq"), None),
    )
    out_specs = P(("groups", "seq"), None)
    return jax.shard_map(
        on_device, mesh=mesh, in_specs=in_specs, out_specs=out_specs, check_vma=False
    )
```

```python
import functools

import jax
import jax.numpy as jnp
from jax import lax
from jax.experimental import pallas as pl
from jax.experimental.pallas import tpu as pltpu
from jax.sharding import PartitionSpec as P

HEAD = 128
ADAPTER_RANK = 64


rope_theta = 500000.0
norm_eps = 1e-05


def spread(array, axis, root):
    mine = lax.axis_index(axis) == root
    return lax.psum(jnp.where(mine, array, jnp.zeros_like(array)), axis)


def rotate(projected, positions):
    half_head = HEAD // 2
    frequencies = rope_theta ** (-(jnp.arange(half_head, dtype=jnp.float32) * 2.0) / HEAD)
    angles = positions.astype(jnp.float32)[:, None] * frequencies[None, :]
    cosine = jnp.cos(angles)[:, None, :]
    sine_table = jnp.sin(angles)[:, None, :]
    per_head = projected.reshape(projected.shape[0], -1, HEAD)
    first_half = per_head[..., :half_head]
    second_half = per_head[..., half_head:]
    turned = jnp.concatenate(
        [
            first_half * cosine - second_half * sine_table,
            second_half * cosine + first_half * sine_table,
        ],
        axis=-1,
    )
    return turned.reshape(projected.shape)


def locate(lengths, prompt_adapter_index, first_row, row_count):
    prompt_ends = jnp.cumsum(lengths)
    prompt_starts = prompt_ends - lengths
    row_ids = first_row + jnp.arange(row_count, dtype=jnp.int32)
    prompt_ids = jnp.sum((prompt_ends[None, :] <= row_ids[:, None]).astype(jnp.int32), axis=1)
    prompt_match = prompt_ids[:, None] == jnp.arange(lengths.shape[0], dtype=jnp.int32)[None, :]
    prompt_start = jnp.sum(jnp.where(prompt_match, prompt_starts[None, :], 0), axis=1)
    hot_slots = jnp.sum(jnp.where(prompt_match, prompt_adapter_index[:, 0][None, :], 0), axis=1)
    return (row_ids - prompt_start, hot_slots)


PLANE = 4
PLANES = 4
SLOT_CASES = ((2, 1, 1), (3, 2, 1), (3, 1, 2), (3, 2, 2), (3, 3, 1), (3, 1, 3), (4, 3, 3))
FEW = 4
ANY = pl.BlockSpec(memory_space=pl.ANY)
SMEM = pl.BlockSpec(memory_space=pltpu.SMEM)
VMEM = pl.BlockSpec(memory_space=pltpu.VMEM)
VMEM_LIMIT = 40 * 1024 * 1024


def swap(value, distance, peer_count):
    return lax.ppermute(value, "seq", [(i, i ^ distance) for i in range(peer_count)])


def call(kernel, out_shape, in_specs, out_specs, scratch=(), **cost):
    return pl.pallas_call(
        kernel,
        out_shape=out_shape,
        in_specs=in_specs,
        out_specs=out_specs,
        scratch_shapes=list(scratch),
        compiler_params=pltpu.CompilerParams(vmem_limit_bytes=VMEM_LIMIT),
        cost_estimate=pl.CostEstimate(transcendentals=0, **cost) if cost else None,
    )


FROM_KIND, FROM_SLOT, PLANE_LIST, DEVICE_LISTS, SECTIONS = 3, 4, 5, 6, 10


def bit_of(mask, entry):
    return lax.shift_right_logical(mask, entry) & 1


def plan_kernel(rows, adapter_device, length_ref, index_ref, id_ref, plan_ref):
    hot_count = id_ref.shape[0]
    device = lax.axis_index("seq")
    plane = lax.div(device, PLANE)
    place = device - plane * PLANE
    for at in range(FROM_KIND * hot_count):
        plan_ref[at] = 0
    for at in range(PLANE_LIST * hot_count, SECTIONS * hot_count):
        plan_ref[at] = -1
    devices = PLANE * PLANES
    uses = [jnp.int32(0)] * devices
    start = jnp.int32(0)
    for prompt in range(length_ref.shape[0]):
        end = start + length_ref[prompt]
        bit = lax.shift_left(jnp.int32(1), index_ref[prompt])
        for at in range(devices):
            hit = (start < (at + 1) * rows) & (end > at * rows)
            uses[at] = uses[at] | jnp.where(hit, bit, 0)
        start = end
    need = []
    for at in range(PLANES):
        mask = uses[at * PLANE]
        for inner in range(1, PLANE):
            mask = mask | uses[at * PLANE + inner]
        need.append(mask)

    def pick(masks, which):
        total = masks[0]
        for at in range(1, len(masks)):
            total = jnp.where(which == at, masks[at], total)
        return total

    def list_bits(section, mask):
        count = jnp.int32(0)
        for entry in range(hot_count):

            @pl.when(bit_of(mask, entry) == 1)
            def _():
                plan_ref[section * hot_count + count] = entry

            count = count + bit_of(mask, entry)
        return count

    owner_plane = []
    kind = []
    slot = []
    local = []
    for entry in range(hot_count):
        adapter = id_ref[entry]
        owner = lax.div(adapter, adapter_device)
        owner_plane.append(lax.div(owner, PLANE))
        local.append(
            ((owner - owner_plane[entry] * PLANE) ^ place) * adapter_device
            + adapter
            - owner * adapter_device
        )
        kind.append(jnp.int32(0))
        slot.append(local[entry])
    need_here = pick(need, plane)
    for distance in range(1, PLANES):
        other = plane ^ distance
        need_there = pick(need, other)
        sent = jnp.int32(0)
        taken = jnp.int32(0)
        for entry in range(hot_count):
            plan_ref[(distance - 1) * hot_count + sent] = local[entry]
            sent = sent + jnp.where(owner_plane[entry] == plane, bit_of(need_there, entry), 0)
            wanted = jnp.where(owner_plane[entry] == other, bit_of(need_here, entry), 0)
            kind[entry] = jnp.where(wanted == 1, distance, kind[entry])
            slot[entry] = jnp.where(wanted == 1, taken, slot[entry])
            taken = taken + wanted
    for entry in range(hot_count):
        plan_ref[FROM_KIND * hot_count + entry] = kind[entry]
        plan_ref[FROM_SLOT * hot_count + entry] = slot[entry]
    plan_ref[SECTIONS * hot_count] = list_bits(PLANE_LIST, need_here)
    for distance in range(PLANE):
        list_bits(DEVICE_LISTS + distance, pick(uses, device ^ distance))
    most = []
    for distance in range(1, PLANES):
        largest = jnp.int32(0)
        for at in range(PLANES):
            count = jnp.int32(0)
            for entry in range(hot_count):
                wanted = bit_of(need[at ^ distance], entry)
                count = count + jnp.where(owner_plane[entry] == at, wanted, 0)
            largest = jnp.maximum(largest, count)
        most.append(largest)
    few = jnp.bool_(True)
    for at in range(devices):
        count = jnp.int32(0)
        for entry in range(hot_count):
            count = count + bit_of(uses[at], entry)
        few = few & (count <= FEW)
    case = jnp.int32(len(SLOT_CASES))
    for at in reversed(range(len(SLOT_CASES))):
        fits = few
        for distance in range(PLANES - 1):
            fits = fits & (most[distance] <= SLOT_CASES[at][distance])
        case = jnp.where(fits, at, case)
    plan_ref[SECTIONS * hot_count + 1] = case


def norm_kernel(token_ref, scale_ref, out_ref, *quarter_refs):
    values = token_ref[...].astype(jnp.float32)
    inverse_rms = lax.rsqrt(jnp.mean(values * values, axis=1, keepdims=True) + norm_eps)
    out_ref[...] = (values * inverse_rms * scale_ref[...]).astype(jnp.bfloat16)
    place = lax.rem(lax.axis_index("seq"), PLANE)
    quarter = quarter_refs[0].shape[1]
    for distance in range(PLANE):
        first = pl.multiple_of((place ^ distance) * quarter, quarter)
        quarter_refs[distance][...] = out_ref[:, pl.ds(first, quarter)]


def pack_kernel(quarter, down_ref, up_ref, *refs):
    outs = refs[:PLANE]
    sems = refs[PLANE]
    place = lax.rem(lax.axis_index("seq"), PLANE)
    rank = down_ref.shape[1]
    part = rank // PLANE
    copies = []
    for distance in range(PLANE):
        other = place ^ distance
        columns = pl.ds(pl.multiple_of(other * quarter, quarter), quarter)
        copies.append(
            pltpu.make_async_copy(
                down_ref.at[:, :, columns],
                outs[distance].at[:, pl.ds(0, rank), :],
                sems.at[2 * distance],
            )
        )
        rows = pl.ds(pl.multiple_of(other * part, part), part)
        copies.append(
            pltpu.make_async_copy(
                up_ref.at[:, rows, :],
                outs[distance].at[:, pl.ds(rank, part), :],
                sems.at[2 * distance + 1],
            )
        )
    for copy in copies:
        copy.start()
    for copy in copies:
        copy.wait()


def select_kernel(slots, hot_count, adapter_device, plan_ref, *refs):
    local = refs[:PLANE]
    outs = refs[PLANE : PLANE + PLANES - 1]
    sems = refs[-1]
    waits = []
    for distance in range(1, PLANES):
        for slot in range(slots[distance - 1]):
            index = plan_ref[(distance - 1) * hot_count + slot]
            holder = lax.div(index, adapter_device)
            inner = index - holder * adapter_device
            target = outs[distance - 1].at[slot]
            sem = sems.at[len(waits)]
            for at in range(PLANE):

                @pl.when(holder == at)
                def _():
                    pltpu.make_async_copy(local[at].at[inner], target, sem).start()

            waits.append(pltpu.make_async_copy(local[0].at[0], target, sem))
    for wait in waits:
        wait.wait()


def start_rows(plan_ref, entry, hot_count, adapter_device, local, arrived, copy_of):
    kind = plan_ref[FROM_KIND * hot_count + entry]
    slot = plan_ref[FROM_SLOT * hot_count + entry]

    @pl.when(kind == 0)
    def _():
        holder = lax.div(slot, adapter_device)
        inner = slot - holder * adapter_device
        for at in range(PLANE):

            @pl.when(holder == at)
            def _():
                copy_of(local[at].at[inner]).start()

    for distance in range(1, PLANES):

        @pl.when(kind == distance)
        def _():
            copy_of(arrived[distance - 1].at[slot]).start()


def collect_kernel(rank, hot_count, adapter_device, plan_ref, *refs):
    local = refs[:PLANE]
    arrived = refs[PLANE : PLANE + PLANES - 1]
    outs = refs[PLANE + PLANES - 1 : -1]
    sems = refs[-1]
    count, part, _ = outs[0].shape
    waits = []
    for distance in range(PLANE):
        for at in range(count):
            entry = jnp.maximum(plan_ref[(DEVICE_LISTS + distance) * hot_count + at], 0)
            copy_of = lambda source, distance=distance, at=at: pltpu.make_async_copy(
                source.at[pl.ds(rank, part), :],
                outs[distance].at[at],
                sems.at[distance * count + at],
            )
            start_rows(plan_ref, entry, hot_count, adapter_device, local, arrived, copy_of)
            waits.append(copy_of(local[0].at[0]))
    for wait in waits:
        wait.wait()


def hot_lanes(first_row, rows, length_ref, index_ref):
    row_ids = first_row + lax.broadcasted_iota(jnp.int32, (1, rows), 1)
    hot = jnp.zeros((1, rows), jnp.int32)
    start = jnp.int32(0)
    for prompt in range(length_ref.shape[0]):
        end = start + length_ref[prompt]
        hot = jnp.where((row_ids >= start) & (row_ids < end), index_ref[prompt], hot)
        start = end
    return hot


def partial_kernel(rank, hot_count, adapter_device, plan_ref, length_ref, index_ref, *refs):
    local = refs[:PLANE]
    arrived = refs[PLANE : PLANE + PLANES - 1]
    refs = refs[PLANE + PLANES - 1 :]
    tokens = refs[:PLANE]
    outs = refs[PLANE : 2 * PLANE]
    down_ref, sems = refs[2 * PLANE :]
    device = lax.axis_index("seq")
    rows = tokens[0].shape[0]
    half = hot_count // 2
    entries = [plan_ref[PLANE_LIST * hot_count + at] for at in range(hot_count)]

    def copy_of(at):
        return lambda source: pltpu.make_async_copy(
            source.at[pl.ds(0, rank), :],
            down_ref.at[pl.ds(at * rank, rank), :],
            sems.at[at],
        )

    def run(first, last):
        for at in range(first, last):
            start_rows(
                plan_ref,
                jnp.maximum(entries[at], 0),
                hot_count,
                adapter_device,
                local,
                arrived,
                copy_of(at),
            )
        for at in range(first, last):
            copy_of(at)(local[0].at[0]).wait()
        down = down_ref[first * rank : last * rank].T
        for distance in range(PLANE):
            product = jnp.dot(
                tokens[distance][...], down, preferred_element_type=jnp.float32
            ).T
            hot = hot_lanes((device ^ distance) * rows, rows, length_ref, index_ref)
            total = outs[distance][...] if first else jnp.zeros((rank, rows), jnp.float32)
            for at in range(first, last):
                piece = product[(at - first) * rank : (at - first + 1) * rank]
                total = jnp.where(hot == entries[at], piece, total)
            outs[distance][...] = total

    run(0, half)

    @pl.when(plan_ref[SECTIONS * hot_count] > half)
    def _():
        run(half, hot_count)


def finish_kernel(
    hot_count,
    plan_ref,
    length_ref,
    index_ref,
    base_ref,
    cosine_ref,
    sine_ref,
    slot_ref,
    *refs,
):
    partials = refs[:PLANE]
    ups = refs[PLANE : 2 * PLANE]
    out_ref, low_ref, rows_ref = refs[2 * PLANE :]
    count, part, key_width = ups[0].shape
    rows = base_ref.shape[0]
    device = lax.axis_index("seq")
    place = lax.rem(device, PLANE)
    total = partials[0][...]
    for distance in range(1, PLANE):
        total = total + partials[distance][...]
    low_ref[...] = total
    hot = hot_lanes(device * rows, rows, length_ref, index_ref)
    entries = [plan_ref[DEVICE_LISTS * hot_count + at] for at in range(count)]
    projected = base_ref[...]
    for distance in range(PLANE):
        first = pl.multiple_of((place ^ distance) * part, part)
        piece = low_ref[pl.ds(first, part), :]
        spread_rows = jnp.concatenate(
            [jnp.where(hot == entry, piece, 0.0) for entry in entries], axis=0
        ).astype(jnp.bfloat16)
        projected = projected + lax.dot_general(
            spread_rows,
            ups[distance][...].reshape(count * part, key_width),
            (((0,), (0,)), ((), ())),
            preferred_element_type=jnp.float32,
        )
    cosine = cosine_ref[...]
    sine = sine_ref[...]
    for head in range(key_width // HEAD):
        columns = slice(head * HEAD, (head + 1) * HEAD)
        values = projected[:, columns]
        turned = values * cosine + pltpu.roll(values, HEAD // 2, 1) * sine
        rows_ref[:, columns] = turned.astype(jnp.bfloat16)
    slots = lax.broadcasted_iota(jnp.int32, (out_ref.shape[0], rows), 0)
    placed = (slots == slot_ref[...]).astype(jnp.bfloat16)
    out_ref[...] = jnp.dot(
        placed, rows_ref[...], preferred_element_type=jnp.float32
    ).astype(jnp.bfloat16)


def turn_tables(positions):
    half_head = HEAD // 2
    frequencies = rope_theta ** (-(jnp.arange(half_head, dtype=jnp.float32) * 2.0) / HEAD)
    angles = positions.astype(jnp.float32)[:, None] * frequencies[None, :]
    cosine = jnp.cos(angles)
    sine = jnp.sin(angles)
    return (
        jnp.concatenate([cosine, cosine], axis=1),
        jnp.concatenate([-sine, sine], axis=1),
    )


def planes_outgoing(
    tokens,
    input_norm_scale,
    key_matrix,
    adapter_down_weight,
    adapter_up_weight,
    lengths,
    prompt_adapter_index,
    active_adapter_ids,
    positions,
    slot_index,
    out_rows,
):
    peer_count = PLANE * PLANES
    rows, width = tokens.shape
    quarter = width // PLANE
    adapter_device, rank, key_width = adapter_up_weight.shape
    part = rank // PLANE
    hot_count = active_adapter_ids.shape[0]
    prompt_index = prompt_adapter_index[:, 0]
    piece = jax.ShapeDtypeStruct((adapter_device, rank + part, quarter), jnp.bfloat16)
    packed = call(
        functools.partial(pack_kernel, quarter),
        [piece] * PLANE,
        [ANY, ANY],
        [ANY] * PLANE,
        [pltpu.SemaphoreType.DMA((2 * PLANE,))],
    )(jnp.swapaxes(adapter_down_weight, 1, 2), adapter_up_weight)
    local = [packed[0]] + [
        swap(packed[distance], distance, peer_count) for distance in range(1, PLANE)
    ]
    plan = call(
        functools.partial(plan_kernel, rows, adapter_device),
        jax.ShapeDtypeStruct((SECTIONS * hot_count + 2,), jnp.int32),
        [SMEM] * 3,
        SMEM,
    )(lengths, prompt_index, active_adapter_ids)
    block = rows // 4
    normed, *columns = pl.pallas_call(
        norm_kernel,
        grid=(4,),
        out_shape=[jax.ShapeDtypeStruct((rows, width), jnp.bfloat16)]
        + [jax.ShapeDtypeStruct((rows, quarter), jnp.bfloat16)] * PLANE,
        in_specs=[
            pl.BlockSpec((block, width), lambda at: (at, 0)),
            pl.BlockSpec((1, width), lambda at: (0, 0)),
        ],
        out_specs=[pl.BlockSpec((block, width), lambda at: (at, 0))]
        + [pl.BlockSpec((block, quarter), lambda at: (at, 0))] * PLANE,
        compiler_params=pltpu.CompilerParams(vmem_limit_bytes=VMEM_LIMIT),
    )(tokens, input_norm_scale.reshape(1, width))
    columns[1] = swap(columns[1], 1, peer_count)
    base = jnp.dot(normed, key_matrix, preferred_element_type=jnp.float32)
    cosine, sine = turn_tables(positions)

    def branch(slots, count):
        def run(plan, lengths, prompt_index, base, cosine, sine, slot_index, columns, local):
            sends = call(
                functools.partial(select_kernel, slots, hot_count, adapter_device),
                [
                    jax.ShapeDtypeStruct((slot, rank + part, quarter), jnp.bfloat16)
                    for slot in slots
                ],
                [SMEM] + [ANY] * PLANE,
                [ANY] * len(slots),
                [pltpu.SemaphoreType.DMA((sum(slots),))],
            )(plan, *local)
            *sends, third, fourth = lax.optimization_barrier((*sends, *columns[2:]))
            columns = columns[:2] + [third, fourth]
            arrived = [
                swap(send, (at + 1) * PLANE, peer_count) for at, send in enumerate(sends)
            ]
            tokens = columns[:2] + [
                swap(columns[distance], distance, peer_count) for distance in range(2, PLANE)
            ]
            ups = call(
                functools.partial(collect_kernel, rank, hot_count, adapter_device),
                [jax.ShapeDtypeStruct((count, part, key_width), jnp.bfloat16)] * PLANE,
                [SMEM] + [ANY] * (PLANE + PLANES - 1),
                [ANY] * PLANE,
                [pltpu.SemaphoreType.DMA((PLANE * count,))],
            )(plan, *local, *arrived)
            ups = [ups[0]] + [
                swap(ups[distance], distance, peer_count) for distance in range(1, PLANE)
            ]
            partials = call(
                functools.partial(partial_kernel, rank, hot_count, adapter_device),
                [jax.ShapeDtypeStruct((rank, rows), jnp.float32)] * PLANE,
                [SMEM] * 3 + [ANY] * (PLANE + PLANES - 1) + [VMEM] * PLANE,
                [VMEM] * PLANE,
                [
                    pltpu.VMEM((hot_count * rank, quarter), jnp.bfloat16),
                    pltpu.SemaphoreType.DMA((hot_count,)),
                ],
                flops=2 * hot_count * rank * width * rows,
                bytes_accessed=40 * 1024 * 1024,
            )(plan, lengths, prompt_index, *local, *arrived, *tokens)
            partials = [partials[0]] + [
                swap(partials[distance], distance, peer_count) for distance in range(1, PLANE)
            ]
            return call(
                functools.partial(finish_kernel, hot_count),
                jax.ShapeDtypeStruct((out_rows, key_width), jnp.bfloat16),
                [SMEM] * 3 + [VMEM] * (4 + 2 * PLANE),
                VMEM,
                [
                    pltpu.VMEM((rank, rows), jnp.float32),
                    pltpu.VMEM((rows, key_width), jnp.bfloat16),
                ],
                flops=2 * rows * key_width * (hot_count * rank + out_rows),
                bytes_accessed=6 * 1024 * 1024,
            )(
                plan,
                lengths,
                prompt_index,
                base,
                cosine,
                sine,
                slot_index.reshape(1, rows),
                *partials,
                *ups,
            )

        return run

    cases = [branch(slots, FEW) for slots in SLOT_CASES]
    cases.append(branch((hot_count,) * (PLANES - 1), hot_count))
    return lax.switch(
        plan[SECTIONS * hot_count + 1],
        cases,
        plan,
        lengths,
        prompt_index,
        base,
        cosine,
        sine,
        slot_index,
        columns,
        local,
    )


def gathered_outgoing(
    tokens,
    input_norm_scale,
    key_matrix,
    adapter_down_weight,
    adapter_up_weight,
    active_adapter_ids,
    positions,
    hot_slots,
    slot_index,
    out_rows,
):
    float_rows = tokens.astype(jnp.float32)
    inverse_rms = lax.rsqrt(jnp.mean(float_rows * float_rows, axis=1, keepdims=True) + norm_eps)
    normed = (float_rows * inverse_rms * input_norm_scale[None, :]).astype(jnp.bfloat16)
    adapter_device = adapter_down_weight.shape[0]
    down_list = []
    up_list = []
    for entry in range(active_adapter_ids.shape[0]):
        adapter = active_adapter_ids[entry]
        for weight, gathered in ((adapter_down_weight, down_list), (adapter_up_weight, up_list)):
            mine = lax.dynamic_index_in_dim(weight, adapter % adapter_device, 0, keepdims=False)
            gathered.append(spread(mine, "seq", adapter // adapter_device))
    down_matrices = jnp.concatenate(down_list, axis=1)
    up_matrices = jnp.concatenate(up_list, axis=0)
    base_proj = jnp.dot(normed, key_matrix, preferred_element_type=jnp.float32)
    low_rank = jnp.dot(normed, down_matrices, preferred_element_type=jnp.float32).astype(
        jnp.bfloat16
    )
    column_owned = (jnp.arange(down_matrices.shape[1], dtype=jnp.int32) // ADAPTER_RANK)[
        None, :
    ] == hot_slots[:, None]
    low_rank = jnp.where(column_owned, low_rank, jnp.zeros_like(low_rank))
    projected = base_proj + jnp.dot(low_rank, up_matrices, preferred_element_type=jnp.float32)
    key_rows = rotate(projected, positions).astype(jnp.bfloat16)
    return jnp.zeros((out_rows, key_rows.shape[1]), jnp.bfloat16).at[slot_index].set(key_rows)


def on_device(
    tokens,
    input_norm_scale,
    key_matrix,
    adapter_down_weight,
    adapter_up_weight,
    lengths,
    prompt_adapter_index,
    active_adapter_ids,
    token_cache_device,
):
    rows_dev = tokens.shape[0]
    peer_count = lax.axis_size("seq")
    slot_count = max(4, 2 * rows_dev // peer_count)
    key_width = key_matrix.shape[1]
    targets = token_cache_device[:, 0]
    row_order = jnp.arange(rows_dev, dtype=jnp.int32)
    earlier = row_order[None, :] < row_order[:, None]
    rank_within = jnp.sum(
        ((targets[:, None] == targets[None, :]) & earlier).astype(jnp.int32), axis=1
    )
    slot_index = targets * slot_count + rank_within
    positions, hot_slots = locate(
        lengths, prompt_adapter_index, lax.axis_index("seq") * rows_dev, rows_dev
    )
    out_rows = peer_count * slot_count
    if peer_count == PLANE * PLANES:
        outgoing = planes_outgoing(
            tokens,
            input_norm_scale,
            key_matrix,
            adapter_down_weight,
            adapter_up_weight,
            lengths,
            prompt_adapter_index,
            active_adapter_ids,
            positions,
            slot_index,
            out_rows,
        )
    else:
        outgoing = gathered_outgoing(
            tokens,
            input_norm_scale,
            key_matrix,
            adapter_down_weight,
            adapter_up_weight,
            active_adapter_ids,
            positions,
            hot_slots,
            slot_index,
            out_rows,
        )
    outgoing = outgoing.reshape(peer_count, slot_count, key_width)
    result = lax.all_to_all(outgoing, "seq", split_axis=0, concat_axis=0, tiled=True)
    return result.reshape(out_rows, key_width)


def solution(mesh):
    in_specs = (
        P(("groups", "seq"), None),
        P(),
        P(),
        P("seq", None, None),
        P("seq", None, None),
        P("groups"),
        P("groups", None),
        P("groups"),
        P(("groups", "seq"), None),
    )
    out_specs = P(("groups", "seq"), None)
    return jax.shard_map(
        on_device, mesh=mesh, in_specs=in_specs, out_specs=out_specs, check_vma=False
    )
```

```python
import functools

import jax
import jax.numpy as jnp
from jax import lax
from jax.experimental import pallas as pl
from jax.experimental.pallas import tpu as pltpu
from jax.sharding import PartitionSpec as P

HEAD = 128
ADAPTER_RANK = 64


rope_theta = 500000.0
norm_eps = 1e-05


def spread(array, axis, root):
    mine = lax.axis_index(axis) == root
    return lax.psum(jnp.where(mine, array, jnp.zeros_like(array)), axis)


def rotate(projected, positions):
    half_head = HEAD // 2
    frequencies = rope_theta ** (-(jnp.arange(half_head, dtype=jnp.float32) * 2.0) / HEAD)
    angles = positions.astype(jnp.float32)[:, None] * frequencies[None, :]
    cosine = jnp.cos(angles)[:, None, :]
    sine_table = jnp.sin(angles)[:, None, :]
    per_head = projected.reshape(projected.shape[0], -1, HEAD)
    first_half = per_head[..., :half_head]
    second_half = per_head[..., half_head:]
    turned = jnp.concatenate(
        [
            first_half * cosine - second_half * sine_table,
            second_half * cosine + first_half * sine_table,
        ],
        axis=-1,
    )
    return turned.reshape(projected.shape)


def locate(lengths, prompt_adapter_index, first_row, row_count):
    prompt_ends = jnp.cumsum(lengths)
    prompt_starts = prompt_ends - lengths
    row_ids = first_row + jnp.arange(row_count, dtype=jnp.int32)
    prompt_ids = jnp.sum((prompt_ends[None, :] <= row_ids[:, None]).astype(jnp.int32), axis=1)
    prompt_match = prompt_ids[:, None] == jnp.arange(lengths.shape[0], dtype=jnp.int32)[None, :]
    prompt_start = jnp.sum(jnp.where(prompt_match, prompt_starts[None, :], 0), axis=1)
    hot_slots = jnp.sum(jnp.where(prompt_match, prompt_adapter_index[:, 0][None, :], 0), axis=1)
    return (row_ids - prompt_start, hot_slots)


PLANE = 4
PLANES = 4
SLOT_CASES = ((2, 1, 1), (3, 2, 1), (3, 1, 2), (3, 2, 2), (3, 3, 1), (3, 1, 3), (4, 3, 3))
FEW = 4
ANY = pl.BlockSpec(memory_space=pl.ANY)
SMEM = pl.BlockSpec(memory_space=pltpu.SMEM)
VMEM = pl.BlockSpec(memory_space=pltpu.VMEM)
VMEM_LIMIT = 40 * 1024 * 1024


def swap(value, distance, peer_count):
    return lax.ppermute(value, "seq", [(i, i ^ distance) for i in range(peer_count)])


def call(kernel, out_shape, in_specs, out_specs, scratch=(), **cost):
    return pl.pallas_call(
        kernel,
        out_shape=out_shape,
        in_specs=in_specs,
        out_specs=out_specs,
        scratch_shapes=list(scratch),
        compiler_params=pltpu.CompilerParams(vmem_limit_bytes=VMEM_LIMIT),
        cost_estimate=pl.CostEstimate(transcendentals=0, **cost) if cost else None,
    )


FROM_KIND, FROM_SLOT, PLANE_LIST, DEVICE_LISTS, SECTIONS = 3, 4, 5, 6, 10


def bit_of(mask, entry):
    return lax.shift_right_logical(mask, entry) & 1


def plan_kernel(rows, adapter_device, length_ref, index_ref, id_ref, plan_ref):
    hot_count = id_ref.shape[0]
    device = lax.axis_index("seq")
    plane = lax.div(device, PLANE)
    place = device - plane * PLANE
    for at in range(FROM_KIND * hot_count):
        plan_ref[at] = 0
    for at in range(PLANE_LIST * hot_count, SECTIONS * hot_count):
        plan_ref[at] = -1
    devices = PLANE * PLANES
    uses = [jnp.int32(0)] * devices
    start = jnp.int32(0)
    for prompt in range(length_ref.shape[0]):
        end = start + length_ref[prompt]
        bit = lax.shift_left(jnp.int32(1), index_ref[prompt])
        for at in range(devices):
            hit = (start < (at + 1) * rows) & (end > at * rows)
            uses[at] = uses[at] | jnp.where(hit, bit, 0)
        start = end
    need = []
    for at in range(PLANES):
        mask = uses[at * PLANE]
        for inner in range(1, PLANE):
            mask = mask | uses[at * PLANE + inner]
        need.append(mask)

    def pick(masks, which):
        total = masks[0]
        for at in range(1, len(masks)):
            total = jnp.where(which == at, masks[at], total)
        return total

    def list_bits(section, mask, values):
        count = jnp.int32(0)
        for entry in range(hot_count):

            @pl.when(bit_of(mask, entry) == 1)
            def _():
                plan_ref[section * hot_count + count] = values[entry]

            count = count + bit_of(mask, entry)
        return count

    owner_plane = []
    kind = []
    slot = []
    local = []
    for entry in range(hot_count):
        adapter = id_ref[entry]
        owner = lax.div(adapter, adapter_device)
        owner_plane.append(lax.div(owner, PLANE))
        local.append(
            ((owner - owner_plane[entry] * PLANE) ^ place) * adapter_device
            + adapter
            - owner * adapter_device
        )
        kind.append(jnp.int32(0))
        slot.append(local[entry])
    need_here = pick(need, plane)
    for distance in range(1, PLANES):
        other = plane ^ distance
        need_there = pick(need, other)
        sent = jnp.int32(0)
        taken = jnp.int32(0)
        for entry in range(hot_count):
            plan_ref[(distance - 1) * hot_count + sent] = local[entry]
            sent = sent + jnp.where(owner_plane[entry] == plane, bit_of(need_there, entry), 0)
            wanted = jnp.where(owner_plane[entry] == other, bit_of(need_here, entry), 0)
            kind[entry] = jnp.where(wanted == 1, distance, kind[entry])
            slot[entry] = jnp.where(wanted == 1, taken, slot[entry])
            taken = taken + wanted
    for entry in range(hot_count):
        plan_ref[FROM_KIND * hot_count + entry] = kind[entry]
        plan_ref[FROM_SLOT * hot_count + entry] = slot[entry]
    listed = [jnp.int32(0)]
    for entry in range(hot_count):
        listed.append(listed[entry] + bit_of(need_here, entry))
    plan_ref[SECTIONS * hot_count] = list_bits(
        PLANE_LIST, need_here, [jnp.int32(entry) for entry in range(hot_count)]
    )
    for distance in range(PLANE):
        list_bits(DEVICE_LISTS + distance, pick(uses, device ^ distance), listed)
    most = []
    for distance in range(1, PLANES):
        largest = jnp.int32(0)
        for at in range(PLANES):
            count = jnp.int32(0)
            for entry in range(hot_count):
                wanted = bit_of(need[at ^ distance], entry)
                count = count + jnp.where(owner_plane[entry] == at, wanted, 0)
            largest = jnp.maximum(largest, count)
        most.append(largest)
    few = jnp.bool_(True)
    for at in range(devices):
        count = jnp.int32(0)
        for entry in range(hot_count):
            count = count + bit_of(uses[at], entry)
        few = few & (count <= FEW)
    case = jnp.int32(len(SLOT_CASES))
    for at in reversed(range(len(SLOT_CASES))):
        fits = jnp.bool_(True)
        for distance in range(PLANES - 1):
            fits = fits & (most[distance] <= SLOT_CASES[at][distance])
        case = jnp.where(fits, at, case)
    plan_ref[SECTIONS * hot_count + 1] = case
    plan_ref[SECTIONS * hot_count + 2] = jnp.where(few, 1, 0)


def norm_kernel(token_ref, scale_ref, out_ref, *quarter_refs):
    values = token_ref[...].astype(jnp.float32)
    inverse_rms = lax.rsqrt(jnp.mean(values * values, axis=1, keepdims=True) + norm_eps)
    out_ref[...] = (values * inverse_rms * scale_ref[...]).astype(jnp.bfloat16)
    place = lax.rem(lax.axis_index("seq"), PLANE)
    quarter = quarter_refs[0].shape[1]
    for distance in range(PLANE):
        first = pl.multiple_of((place ^ distance) * quarter, quarter)
        quarter_refs[distance][...] = out_ref[:, pl.ds(first, quarter)]


def pack_kernel(quarter, down_ref, up_ref, *refs):
    outs = refs[:PLANE]
    sems = refs[PLANE]
    place = lax.rem(lax.axis_index("seq"), PLANE)
    rank = down_ref.shape[1]
    part = rank // PLANE
    copies = []
    for distance in range(PLANE):
        other = place ^ distance
        columns = pl.ds(pl.multiple_of(other * quarter, quarter), quarter)
        copies.append(
            pltpu.make_async_copy(
                down_ref.at[:, :, columns],
                outs[distance].at[:, pl.ds(0, rank), :],
                sems.at[2 * distance],
            )
        )
        rows = pl.ds(pl.multiple_of(other * part, part), part)
        copies.append(
            pltpu.make_async_copy(
                up_ref.at[:, rows, :],
                outs[distance].at[:, pl.ds(rank, part), :],
                sems.at[2 * distance + 1],
            )
        )
    for copy in copies:
        copy.start()
    for copy in copies:
        copy.wait()


def select_kernel(slots, hot_count, adapter_device, plan_ref, *refs):
    local = refs[:PLANE]
    outs = refs[PLANE : PLANE + PLANES - 1]
    sems = refs[-1]
    waits = []
    for distance in range(1, PLANES):
        for slot in range(slots[distance - 1]):
            index = plan_ref[(distance - 1) * hot_count + slot]
            holder = lax.div(index, adapter_device)
            inner = index - holder * adapter_device
            target = outs[distance - 1].at[slot]
            sem = sems.at[len(waits)]
            for at in range(PLANE):

                @pl.when(holder == at)
                def _():
                    pltpu.make_async_copy(local[at].at[inner], target, sem).start()

            waits.append(pltpu.make_async_copy(local[0].at[0], target, sem))
    for wait in waits:
        wait.wait()


def start_rows(plan_ref, entry, hot_count, adapter_device, local, arrived, copy_of):
    kind = plan_ref[FROM_KIND * hot_count + entry]
    slot = plan_ref[FROM_SLOT * hot_count + entry]

    @pl.when(kind == 0)
    def _():
        holder = lax.div(slot, adapter_device)
        inner = slot - holder * adapter_device
        for at in range(PLANE):

            @pl.when(holder == at)
            def _():
                copy_of(local[at].at[inner]).start()

    for distance in range(1, PLANES):

        @pl.when(kind == distance)
        def _():
            copy_of(arrived[distance - 1].at[slot]).start()


def collect_kernel(hot_count, adapter_device, plan_ref, *refs):
    local = refs[:PLANE]
    arrived = refs[PLANE : PLANE + PLANES - 1]
    out_ref, sems = refs[PLANE + PLANES - 1 :]
    used = plan_ref[SECTIONS * hot_count]

    def copy_of(at):
        return lambda source: pltpu.make_async_copy(source, out_ref.at[at], sems.at[at])

    for at in range(hot_count):

        @pl.when(at < used)
        def _():
            entry = plan_ref[PLANE_LIST * hot_count + at]
            start_rows(plan_ref, entry, hot_count, adapter_device, local, arrived, copy_of(at))

    for at in range(hot_count):

        @pl.when(at < used)
        def _():
            copy_of(at)(local[0].at[0]).wait()


def share_kernel(first, rank, hot_count, plan_ref, rows_ref, *outs):
    for distance in range(PLANE):
        for at in range(outs[0].shape[0]):
            listed = plan_ref[(DEVICE_LISTS + distance) * hot_count + first + at]
            outs[distance][at] = rows_ref[jnp.maximum(listed, 0), rank:, :]


def nothing_kernel(plan_ref, *outs):
    del plan_ref, outs


def hot_lanes(first_row, rows, length_ref, index_ref):
    row_ids = first_row + lax.broadcasted_iota(jnp.int32, (1, rows), 1)
    hot = jnp.zeros((1, rows), jnp.int32)
    start = jnp.int32(0)
    for prompt in range(length_ref.shape[0]):
        end = start + length_ref[prompt]
        hot = jnp.where((row_ids >= start) & (row_ids < end), index_ref[prompt], hot)
        start = end
    return hot


def partial_kernel(rank, hot_count, plan_ref, length_ref, index_ref, rows_ref, *refs):
    tokens = refs[:PLANE]
    outs = refs[PLANE:]
    device = lax.axis_index("seq")
    rows = tokens[0].shape[0]
    half = hot_count // 2

    def run(first, last):
        down = jnp.concatenate([rows_ref[at, :rank, :] for at in range(first, last)], axis=0).T
        for distance in range(PLANE):
            product = jnp.dot(
                tokens[distance][...], down, preferred_element_type=jnp.float32
            ).T
            hot = hot_lanes((device ^ distance) * rows, rows, length_ref, index_ref)
            total = outs[distance][...] if first else jnp.zeros((rank, rows), jnp.float32)
            for at in range(first, last):
                piece = product[(at - first) * rank : (at - first + 1) * rank]
                total = jnp.where(hot == plan_ref[PLANE_LIST * hot_count + at], piece, total)
            outs[distance][...] = total

    run(0, half)

    @pl.when(plan_ref[SECTIONS * hot_count] > half)
    def _():
        run(half, hot_count)


def finish_kernel(
    hot_count,
    plan_ref,
    length_ref,
    index_ref,
    base_ref,
    cosine_ref,
    sine_ref,
    slot_ref,
    *refs,
):
    partials = refs[:PLANE]
    ups = refs[PLANE : 2 * PLANE]
    more = refs[2 * PLANE : 3 * PLANE]
    out_ref, low_ref, sum_ref, rows_ref = refs[3 * PLANE :]
    few, part, key_width = ups[0].shape
    rows = base_ref.shape[0]
    device = lax.axis_index("seq")
    place = lax.rem(device, PLANE)
    total = partials[0][...]
    for distance in range(1, PLANE):
        total = total + partials[distance][...]
    low_ref[...] = total
    hot = hot_lanes(device * rows, rows, length_ref, index_ref)

    def adapted(held, first_entry):
        entries = []
        for at in range(first_entry, first_entry + held[0].shape[0]):
            listed = plan_ref[DEVICE_LISTS * hot_count + at]
            entry = plan_ref[PLANE_LIST * hot_count + jnp.maximum(listed, 0)]
            entries.append(jnp.where(listed >= 0, entry, -1))
        result = None
        for distance in range(PLANE):
            first = pl.multiple_of((place ^ distance) * part, part)
            piece = low_ref[pl.ds(first, part), :]
            spread_rows = jnp.concatenate(
                [jnp.where(hot == entry, piece, 0.0) for entry in entries], axis=0
            ).astype(jnp.bfloat16)
            product = lax.dot_general(
                spread_rows,
                held[distance][...].reshape(len(entries) * part, key_width),
                (((0,), (0,)), ((), ())),
                preferred_element_type=jnp.float32,
            )
            result = product if result is None else result + product
        return result

    sum_ref[...] = base_ref[...] + adapted(ups, 0)

    @pl.when(plan_ref[SECTIONS * hot_count + 2] == 0)
    def _():
        sum_ref[...] += adapted(more, few)

    projected = sum_ref[...]
    cosine = cosine_ref[...]
    sine = sine_ref[...]
    for head in range(key_width // HEAD):
        columns = slice(head * HEAD, (head + 1) * HEAD)
        values = projected[:, columns]
        turned = values * cosine + pltpu.roll(values, HEAD // 2, 1) * sine
        rows_ref[:, columns] = turned.astype(jnp.bfloat16)
    slots = lax.broadcasted_iota(jnp.int32, (out_ref.shape[0], rows), 0)
    placed = (slots == slot_ref[...]).astype(jnp.bfloat16)
    out_ref[...] = jnp.dot(
        placed, rows_ref[...], preferred_element_type=jnp.float32
    ).astype(jnp.bfloat16)


def turn_tables(positions):
    half_head = HEAD // 2
    frequencies = rope_theta ** (-(jnp.arange(half_head, dtype=jnp.float32) * 2.0) / HEAD)
    angles = positions.astype(jnp.float32)[:, None] * frequencies[None, :]
    cosine = jnp.cos(angles)
    sine = jnp.sin(angles)
    return (
        jnp.concatenate([cosine, cosine], axis=1),
        jnp.concatenate([-sine, sine], axis=1),
    )


def planes_outgoing(
    tokens,
    input_norm_scale,
    key_matrix,
    adapter_down_weight,
    adapter_up_weight,
    lengths,
    prompt_adapter_index,
    active_adapter_ids,
    positions,
    slot_index,
    out_rows,
):
    peer_count = PLANE * PLANES
    rows, width = tokens.shape
    quarter = width // PLANE
    adapter_device, rank, key_width = adapter_up_weight.shape
    part = rank // PLANE
    hot_count = active_adapter_ids.shape[0]
    prompt_index = prompt_adapter_index[:, 0]
    piece = jax.ShapeDtypeStruct((adapter_device, rank + part, quarter), jnp.bfloat16)
    packed = call(
        functools.partial(pack_kernel, quarter),
        [piece] * PLANE,
        [ANY, ANY],
        [ANY] * PLANE,
        [pltpu.SemaphoreType.DMA((2 * PLANE,))],
    )(jnp.swapaxes(adapter_down_weight, 1, 2), adapter_up_weight)
    local = [packed[0]] + [
        swap(packed[distance], distance, peer_count) for distance in range(1, PLANE)
    ]
    plan = call(
        functools.partial(plan_kernel, rows, adapter_device),
        jax.ShapeDtypeStruct((SECTIONS * hot_count + 3,), jnp.int32),
        [SMEM] * 3,
        SMEM,
    )(lengths, prompt_index, active_adapter_ids)
    block = rows // 4
    normed, *columns = pl.pallas_call(
        norm_kernel,
        grid=(4,),
        out_shape=[jax.ShapeDtypeStruct((rows, width), jnp.bfloat16)]
        + [jax.ShapeDtypeStruct((rows, quarter), jnp.bfloat16)] * PLANE,
        in_specs=[
            pl.BlockSpec((block, width), lambda at: (at, 0)),
            pl.BlockSpec((1, width), lambda at: (0, 0)),
        ],
        out_specs=[pl.BlockSpec((block, width), lambda at: (at, 0))]
        + [pl.BlockSpec((block, quarter), lambda at: (at, 0))] * PLANE,
        compiler_params=pltpu.CompilerParams(vmem_limit_bytes=VMEM_LIMIT),
    )(tokens, input_norm_scale.reshape(1, width))
    base = jnp.dot(normed, key_matrix, preferred_element_type=jnp.float32)
    cosine, sine = turn_tables(positions)
    *local, third, fourth = lax.optimization_barrier((*local, *columns[2:]))
    columns = [
        columns[0],
        swap(columns[1], 1, peer_count),
        swap(third, 2, peer_count),
        swap(fourth, 3, peer_count),
    ]

    def branch(slots):
        def run(plan, *local):
            sends = call(
                functools.partial(select_kernel, slots, hot_count, adapter_device),
                [
                    jax.ShapeDtypeStruct((slot, rank + part, quarter), jnp.bfloat16)
                    for slot in slots
                ],
                [SMEM] + [ANY] * PLANE,
                [ANY] * len(slots),
                [pltpu.SemaphoreType.DMA((sum(slots),))],
            )(plan, *local)
            arrived = [
                swap(send, (at + 1) * PLANE, peer_count) for at, send in enumerate(sends)
            ]
            return call(
                functools.partial(collect_kernel, hot_count, adapter_device),
                jax.ShapeDtypeStruct((hot_count, rank + part, quarter), jnp.bfloat16),
                [SMEM] + [ANY] * (PLANE + PLANES - 1),
                ANY,
                [pltpu.SemaphoreType.DMA((hot_count,))],
            )(plan, *local, *arrived)

        return run

    cases = [branch(slots) for slots in SLOT_CASES + ((hot_count,) * (PLANES - 1),)]
    used_rows = lax.switch(plan[SECTIONS * hot_count + 1], cases, plan, *local)

    def share(first, count):
        def run(plan, used_rows):
            parts = call(
                functools.partial(share_kernel, first, rank, hot_count),
                [jax.ShapeDtypeStruct((count, part, key_width), jnp.bfloat16)] * PLANE,
                [SMEM, VMEM],
                [VMEM] * PLANE,
            )(plan, used_rows)
            return [parts[0]] + [
                swap(parts[distance], distance, peer_count) for distance in range(1, PLANE)
            ]

        return run

    def no_more(plan, used_rows):
        del used_rows
        empty = call(
            nothing_kernel,
            [jax.ShapeDtypeStruct((hot_count - FEW, part, key_width), jnp.bfloat16)] * PLANE,
            [SMEM],
            [VMEM] * PLANE,
        )(plan)
        return list(empty)

    ups = share(0, FEW)(plan, used_rows)
    partials = call(
        functools.partial(partial_kernel, rank, hot_count),
        [jax.ShapeDtypeStruct((rank, rows), jnp.float32)] * PLANE,
        [SMEM] * 3 + [VMEM] * (1 + PLANE),
        [VMEM] * PLANE,
        flops=2 * hot_count * rank * width * rows,
        bytes_accessed=40 * 1024 * 1024,
    )(plan, lengths, prompt_index, used_rows, *columns)
    partials = [partials[0]] + [
        swap(partials[distance], distance, peer_count) for distance in range(1, PLANE)
    ]
    more = lax.cond(
        plan[SECTIONS * hot_count + 2] == 1,
        no_more,
        share(FEW, hot_count - FEW),
        plan,
        used_rows,
    )
    return call(
        functools.partial(finish_kernel, hot_count),
        jax.ShapeDtypeStruct((out_rows, key_width), jnp.bfloat16),
        [SMEM] * 3 + [VMEM] * (4 + 3 * PLANE),
        VMEM,
        [
            pltpu.VMEM((rank, rows), jnp.float32),
            pltpu.VMEM((rows, key_width), jnp.float32),
            pltpu.VMEM((rows, key_width), jnp.bfloat16),
        ],
        flops=2 * rows * key_width * (hot_count * rank + out_rows),
        bytes_accessed=6 * 1024 * 1024,
    )(
        plan,
        lengths,
        prompt_index,
        base,
        cosine,
        sine,
        slot_index.reshape(1, rows),
        *partials,
        *ups,
        *more,
    )


def gathered_outgoing(
    tokens,
    input_norm_scale,
    key_matrix,
    adapter_down_weight,
    adapter_up_weight,
    active_adapter_ids,
    positions,
    hot_slots,
    slot_index,
    out_rows,
):
    float_rows = tokens.astype(jnp.float32)
    inverse_rms = lax.rsqrt(jnp.mean(float_rows * float_rows, axis=1, keepdims=True) + norm_eps)
    normed = (float_rows * inverse_rms * input_norm_scale[None, :]).astype(jnp.bfloat16)
    adapter_device = adapter_down_weight.shape[0]
    down_list = []
    up_list = []
    for entry in range(active_adapter_ids.shape[0]):
        adapter = active_adapter_ids[entry]
        for weight, gathered in ((adapter_down_weight, down_list), (adapter_up_weight, up_list)):
            mine = lax.dynamic_index_in_dim(weight, adapter % adapter_device, 0, keepdims=False)
            gathered.append(spread(mine, "seq", adapter // adapter_device))
    down_matrices = jnp.concatenate(down_list, axis=1)
    up_matrices = jnp.concatenate(up_list, axis=0)
    base_proj = jnp.dot(normed, key_matrix, preferred_element_type=jnp.float32)
    low_rank = jnp.dot(normed, down_matrices, preferred_element_type=jnp.float32).astype(
        jnp.bfloat16
    )
    column_owned = (jnp.arange(down_matrices.shape[1], dtype=jnp.int32) // ADAPTER_RANK)[
        None, :
    ] == hot_slots[:, None]
    low_rank = jnp.where(column_owned, low_rank, jnp.zeros_like(low_rank))
    projected = base_proj + jnp.dot(low_rank, up_matrices, preferred_element_type=jnp.float32)
    key_rows = rotate(projected, positions).astype(jnp.bfloat16)
    return jnp.zeros((out_rows, key_rows.shape[1]), jnp.bfloat16).at[slot_index].set(key_rows)


def on_device(
    tokens,
    input_norm_scale,
    key_matrix,
    adapter_down_weight,
    adapter_up_weight,
    lengths,
    prompt_adapter_index,
    active_adapter_ids,
    token_cache_device,
):
    rows_dev = tokens.shape[0]
    peer_count = lax.axis_size("seq")
    slot_count = max(4, 2 * rows_dev // peer_count)
    key_width = key_matrix.shape[1]
    targets = token_cache_device[:, 0]
    row_order = jnp.arange(rows_dev, dtype=jnp.int32)
    earlier = row_order[None, :] < row_order[:, None]
    rank_within = jnp.sum(
        ((targets[:, None] == targets[None, :]) & earlier).astype(jnp.int32), axis=1
    )
    slot_index = targets * slot_count + rank_within
    positions, hot_slots = locate(
        lengths, prompt_adapter_index, lax.axis_index("seq") * rows_dev, rows_dev
    )
    out_rows = peer_count * slot_count
    if peer_count == PLANE * PLANES:
        outgoing = planes_outgoing(
            tokens,
            input_norm_scale,
            key_matrix,
            adapter_down_weight,
            adapter_up_weight,
            lengths,
            prompt_adapter_index,
            active_adapter_ids,
            positions,
            slot_index,
            out_rows,
        )
    else:
        outgoing = gathered_outgoing(
            tokens,
            input_norm_scale,
            key_matrix,
            adapter_down_weight,
            adapter_up_weight,
            active_adapter_ids,
            positions,
            hot_slots,
            slot_index,
            out_rows,
        )
    outgoing = outgoing.reshape(peer_count, slot_count, key_width)
    result = lax.all_to_all(outgoing, "seq", split_axis=0, concat_axis=0, tiled=True)
    return result.reshape(out_rows, key_width)


def solution(mesh):
    in_specs = (
        P(("groups", "seq"), None),
        P(),
        P(),
        P("seq", None, None),
        P("seq", None, None),
        P("groups"),
        P("groups", None),
        P("groups"),
        P(("groups", "seq"), None),
    )
    out_specs = P(("groups", "seq"), None)
    return jax.shard_map(
        on_device, mesh=mesh, in_specs=in_specs, out_specs=out_specs, check_vma=False
    )
```

```python
import functools

import jax
import jax.numpy as jnp
from jax import lax
from jax.experimental import pallas as pl
from jax.experimental.pallas import tpu as pltpu
from jax.sharding import PartitionSpec as P

HEAD = 128
ADAPTER_RANK = 64


rope_theta = 500000.0
norm_eps = 1e-05


def spread(array, axis, root):
    mine = lax.axis_index(axis) == root
    return lax.psum(jnp.where(mine, array, jnp.zeros_like(array)), axis)


def rotate(projected, positions):
    half_head = HEAD // 2
    frequencies = rope_theta ** (-(jnp.arange(half_head, dtype=jnp.float32) * 2.0) / HEAD)
    angles = positions.astype(jnp.float32)[:, None] * frequencies[None, :]
    cosine = jnp.cos(angles)[:, None, :]
    sine_table = jnp.sin(angles)[:, None, :]
    per_head = projected.reshape(projected.shape[0], -1, HEAD)
    first_half = per_head[..., :half_head]
    second_half = per_head[..., half_head:]
    turned = jnp.concatenate(
        [
            first_half * cosine - second_half * sine_table,
            second_half * cosine + first_half * sine_table,
        ],
        axis=-1,
    )
    return turned.reshape(projected.shape)


def locate(lengths, prompt_adapter_index, first_row, row_count):
    prompt_ends = jnp.cumsum(lengths)
    prompt_starts = prompt_ends - lengths
    row_ids = first_row + jnp.arange(row_count, dtype=jnp.int32)
    prompt_ids = jnp.sum((prompt_ends[None, :] <= row_ids[:, None]).astype(jnp.int32), axis=1)
    prompt_match = prompt_ids[:, None] == jnp.arange(lengths.shape[0], dtype=jnp.int32)[None, :]
    prompt_start = jnp.sum(jnp.where(prompt_match, prompt_starts[None, :], 0), axis=1)
    hot_slots = jnp.sum(jnp.where(prompt_match, prompt_adapter_index[:, 0][None, :], 0), axis=1)
    return (row_ids - prompt_start, hot_slots)


PLANE = 4
PLANES = 4
SLOT_CASES = ((2, 1, 1), (3, 2, 1), (3, 1, 2), (3, 2, 2), (3, 3, 1), (3, 1, 3), (4, 3, 3))
FEW = 4
ANY = pl.BlockSpec(memory_space=pl.ANY)
SMEM = pl.BlockSpec(memory_space=pltpu.SMEM)
VMEM = pl.BlockSpec(memory_space=pltpu.VMEM)
VMEM_LIMIT = 40 * 1024 * 1024


def swap(value, distance, peer_count):
    return lax.ppermute(value, "seq", [(i, i ^ distance) for i in range(peer_count)])


def call(kernel, out_shape, in_specs, out_specs, scratch=(), **cost):
    return pl.pallas_call(
        kernel,
        out_shape=out_shape,
        in_specs=in_specs,
        out_specs=out_specs,
        scratch_shapes=list(scratch),
        compiler_params=pltpu.CompilerParams(vmem_limit_bytes=VMEM_LIMIT),
        cost_estimate=pl.CostEstimate(transcendentals=0, **cost) if cost else None,
    )


FROM_KIND, FROM_SLOT, PLANE_LIST, DEVICE_LISTS, SECTIONS = 3, 4, 5, 6, 10


def bit_of(mask, entry):
    return lax.shift_right_logical(mask, entry) & 1


def plan_kernel(rows, adapter_device, length_ref, index_ref, id_ref, plan_ref):
    hot_count = id_ref.shape[0]
    device = lax.axis_index("seq")
    plane = lax.div(device, PLANE)
    place = device - plane * PLANE
    for at in range(FROM_KIND * hot_count):
        plan_ref[at] = 0
    for at in range(PLANE_LIST * hot_count, SECTIONS * hot_count):
        plan_ref[at] = -1
    devices = PLANE * PLANES
    uses = [jnp.int32(0)] * devices
    start = jnp.int32(0)
    for prompt in range(length_ref.shape[0]):
        end = start + length_ref[prompt]
        bit = lax.shift_left(jnp.int32(1), index_ref[prompt])
        plan_ref[SECTIONS * hot_count + 3 + 2 * prompt] = end
        plan_ref[SECTIONS * hot_count + 4 + 2 * prompt] = index_ref[prompt]
        for at in range(devices):
            hit = (start < (at + 1) * rows) & (end > at * rows)
            uses[at] = uses[at] | jnp.where(hit, bit, 0)
        start = end
    need = []
    for at in range(PLANES):
        mask = uses[at * PLANE]
        for inner in range(1, PLANE):
            mask = mask | uses[at * PLANE + inner]
        need.append(mask)

    def pick(masks, which):
        total = masks[0]
        for at in range(1, len(masks)):
            total = jnp.where(which == at, masks[at], total)
        return total

    def list_bits(section, mask, values):
        count = jnp.int32(0)
        for entry in range(hot_count):

            @pl.when(bit_of(mask, entry) == 1)
            def _():
                plan_ref[section * hot_count + count] = values[entry]

            count = count + bit_of(mask, entry)
        return count

    owner_plane = []
    kind = []
    slot = []
    local = []
    for entry in range(hot_count):
        adapter = id_ref[entry]
        owner = lax.div(adapter, adapter_device)
        owner_plane.append(lax.div(owner, PLANE))
        local.append(
            ((owner - owner_plane[entry] * PLANE) ^ place) * adapter_device
            + adapter
            - owner * adapter_device
        )
        kind.append(jnp.int32(0))
        slot.append(local[entry])
    need_here = pick(need, plane)
    for distance in range(1, PLANES):
        other = plane ^ distance
        need_there = pick(need, other)
        sent = jnp.int32(0)
        taken = jnp.int32(0)
        for entry in range(hot_count):
            plan_ref[(distance - 1) * hot_count + sent] = local[entry]
            sent = sent + jnp.where(owner_plane[entry] == plane, bit_of(need_there, entry), 0)
            wanted = jnp.where(owner_plane[entry] == other, bit_of(need_here, entry), 0)
            kind[entry] = jnp.where(wanted == 1, distance, kind[entry])
            slot[entry] = jnp.where(wanted == 1, taken, slot[entry])
            taken = taken + wanted
    for entry in range(hot_count):
        plan_ref[FROM_KIND * hot_count + entry] = kind[entry]
        plan_ref[FROM_SLOT * hot_count + entry] = slot[entry]
    listed = [jnp.int32(0)]
    for entry in range(hot_count):
        listed.append(listed[entry] + bit_of(need_here, entry))
    plan_ref[SECTIONS * hot_count] = list_bits(
        PLANE_LIST, need_here, [jnp.int32(entry) for entry in range(hot_count)]
    )
    for distance in range(PLANE):
        list_bits(DEVICE_LISTS + distance, pick(uses, device ^ distance), listed)
    most = []
    for distance in range(1, PLANES):
        largest = jnp.int32(0)
        for at in range(PLANES):
            count = jnp.int32(0)
            for entry in range(hot_count):
                wanted = bit_of(need[at ^ distance], entry)
                count = count + jnp.where(owner_plane[entry] == at, wanted, 0)
            largest = jnp.maximum(largest, count)
        most.append(largest)
    few = jnp.bool_(True)
    for at in range(devices):
        count = jnp.int32(0)
        for entry in range(hot_count):
            count = count + bit_of(uses[at], entry)
        few = few & (count <= FEW)
    case = jnp.int32(len(SLOT_CASES))
    for at in reversed(range(len(SLOT_CASES))):
        fits = jnp.bool_(True)
        for distance in range(PLANES - 1):
            fits = fits & (most[distance] <= SLOT_CASES[at][distance])
        case = jnp.where(fits, at, case)
    plan_ref[SECTIONS * hot_count + 1] = case
    plan_ref[SECTIONS * hot_count + 2] = jnp.where(few, 1, 0)


def norm_kernel(token_ref, scale_ref, out_ref, *quarter_refs):
    values = token_ref[...].astype(jnp.float32)
    inverse_rms = lax.rsqrt(jnp.mean(values * values, axis=1, keepdims=True) + norm_eps)
    out_ref[...] = (values * inverse_rms * scale_ref[...]).astype(jnp.bfloat16)
    place = lax.rem(lax.axis_index("seq"), PLANE)
    quarter = quarter_refs[0].shape[1]
    for distance in range(PLANE):
        first = pl.multiple_of((place ^ distance) * quarter, quarter)
        quarter_refs[distance][...] = out_ref[:, pl.ds(first, quarter)]


def pack_kernel(quarter, down_ref, up_ref, *refs):
    outs = refs[:PLANE]
    sems = refs[PLANE]
    place = lax.rem(lax.axis_index("seq"), PLANE)
    rank = down_ref.shape[1]
    part = rank // PLANE
    copies = []
    for distance in range(PLANE):
        other = place ^ distance
        columns = pl.ds(pl.multiple_of(other * quarter, quarter), quarter)
        copies.append(
            pltpu.make_async_copy(
                down_ref.at[:, :, columns],
                outs[distance].at[:, pl.ds(0, rank), :],
                sems.at[2 * distance],
            )
        )
        rows = pl.ds(pl.multiple_of(other * part, part), part)
        copies.append(
            pltpu.make_async_copy(
                up_ref.at[:, rows, :],
                outs[distance].at[:, pl.ds(rank, part), :],
                sems.at[2 * distance + 1],
            )
        )
    for copy in copies:
        copy.start()
    for copy in copies:
        copy.wait()


def select_kernel(slots, hot_count, adapter_device, plan_ref, *refs):
    local = refs[:PLANE]
    outs = refs[PLANE : PLANE + PLANES - 1]
    sems = refs[-1]
    waits = []
    for distance in range(1, PLANES):
        for slot in range(slots[distance - 1]):
            index = plan_ref[(distance - 1) * hot_count + slot]
            holder = lax.div(index, adapter_device)
            inner = index - holder * adapter_device
            target = outs[distance - 1].at[slot]
            sem = sems.at[len(waits)]
            for at in range(PLANE):

                @pl.when(holder == at)
                def _():
                    pltpu.make_async_copy(local[at].at[inner], target, sem).start()

            waits.append(pltpu.make_async_copy(local[0].at[0], target, sem))
    for wait in waits:
        wait.wait()


def start_rows(plan_ref, entry, hot_count, adapter_device, local, arrived, copy_of):
    kind = plan_ref[FROM_KIND * hot_count + entry]
    slot = plan_ref[FROM_SLOT * hot_count + entry]

    @pl.when(kind == 0)
    def _():
        holder = lax.div(slot, adapter_device)
        inner = slot - holder * adapter_device
        for at in range(PLANE):

            @pl.when(holder == at)
            def _():
                copy_of(local[at].at[inner]).start()

    for distance in range(1, PLANES):

        @pl.when(kind == distance)
        def _():
            copy_of(arrived[distance - 1].at[slot]).start()


def share_rows(first, rank, hot_count, plan_ref, rows_ref, outs):
    for distance in range(PLANE):
        for at in range(outs[0].shape[0]):
            listed = plan_ref[(DEVICE_LISTS + distance) * hot_count + first + at]
            outs[distance][at] = rows_ref[jnp.maximum(listed, 0), rank:, :]


def share_kernel(first, rank, hot_count, plan_ref, rows_ref, *outs):
    share_rows(first, rank, hot_count, plan_ref, rows_ref, outs)


def collect_kernel(rank, hot_count, adapter_device, plan_ref, *refs):
    local = refs[:PLANE]
    arrived = refs[PLANE : PLANE + PLANES - 1]
    out_ref, *shares, sems = refs[PLANE + PLANES - 1 :]
    used = plan_ref[SECTIONS * hot_count]

    def copy_of(at):
        return lambda source: pltpu.make_async_copy(source, out_ref.at[at], sems.at[at])

    for at in range(hot_count):

        @pl.when(at < used)
        def _():
            entry = plan_ref[PLANE_LIST * hot_count + at]
            start_rows(plan_ref, entry, hot_count, adapter_device, local, arrived, copy_of(at))

    for at in range(hot_count):

        @pl.when(at < used)
        def _():
            copy_of(at)(local[0].at[0]).wait()

    share_rows(0, rank, hot_count, plan_ref, out_ref, shares)


def nothing_kernel(plan_ref, *outs):
    del plan_ref, outs


def hot_lanes(first_row, rows, hot_count, plan_ref):
    row_ids = first_row + lax.broadcasted_iota(jnp.int32, (1, rows), 1)
    hot = jnp.zeros((1, rows), jnp.int32)
    start = jnp.int32(0)
    for at in range(SECTIONS * hot_count + 3, plan_ref.shape[0], 2):
        end = plan_ref[at]
        hot = jnp.where((row_ids >= start) & (row_ids < end), plan_ref[at + 1], hot)
        start = end
    return hot


def partial_kernel(rank, hot_count, plan_ref, rows_ref, *refs):
    tokens = refs[:PLANE]
    outs = refs[PLANE:]
    device = lax.axis_index("seq")
    rows = tokens[0].shape[0]
    half = hot_count // 2

    def run(first, last):
        down = jnp.concatenate([rows_ref[at, :rank, :] for at in range(first, last)], axis=0).T
        for distance in range(PLANE):
            product = jnp.dot(
                tokens[distance][...], down, preferred_element_type=jnp.float32
            ).T
            hot = hot_lanes((device ^ distance) * rows, rows, hot_count, plan_ref)
            total = outs[distance][...] if first else jnp.zeros((rank, rows), jnp.float32)
            for at in range(first, last):
                piece = product[(at - first) * rank : (at - first + 1) * rank]
                total = jnp.where(hot == plan_ref[PLANE_LIST * hot_count + at], piece, total)
            outs[distance][...] = total

    run(0, half)

    @pl.when(plan_ref[SECTIONS * hot_count] > half)
    def _():
        run(half, hot_count)


def finish_kernel(
    hot_count,
    plan_ref,
    base_ref,
    cosine_ref,
    sine_ref,
    slot_ref,
    *refs,
):
    partials = refs[:PLANE]
    ups = refs[PLANE : 2 * PLANE]
    more = refs[2 * PLANE : 3 * PLANE]
    out_ref, low_ref, sum_ref, rows_ref = refs[3 * PLANE :]
    few, part, key_width = ups[0].shape
    rows = base_ref.shape[0]
    device = lax.axis_index("seq")
    place = lax.rem(device, PLANE)
    total = partials[0][...]
    for distance in range(1, PLANE):
        total = total + partials[distance][...]
    low_ref[...] = total
    hot = hot_lanes(device * rows, rows, hot_count, plan_ref)

    def adapted(held, first_entry):
        entries = []
        for at in range(first_entry, first_entry + held[0].shape[0]):
            listed = plan_ref[DEVICE_LISTS * hot_count + at]
            entry = plan_ref[PLANE_LIST * hot_count + jnp.maximum(listed, 0)]
            entries.append(jnp.where(listed >= 0, entry, -1))
        result = None
        for distance in range(PLANE):
            first = pl.multiple_of((place ^ distance) * part, part)
            piece = low_ref[pl.ds(first, part), :]
            spread_rows = jnp.concatenate(
                [jnp.where(hot == entry, piece, 0.0) for entry in entries], axis=0
            ).astype(jnp.bfloat16)
            product = lax.dot_general(
                spread_rows,
                held[distance][...].reshape(len(entries) * part, key_width),
                (((0,), (0,)), ((), ())),
                preferred_element_type=jnp.float32,
            )
            result = product if result is None else result + product
        return result

    sum_ref[...] = base_ref[...] + adapted(ups, 0)

    @pl.when(plan_ref[SECTIONS * hot_count + 2] == 0)
    def _():
        sum_ref[...] += adapted(more, few)

    projected = sum_ref[...]
    cosine = cosine_ref[...]
    sine = sine_ref[...]
    for head in range(key_width // HEAD):
        columns = slice(head * HEAD, (head + 1) * HEAD)
        values = projected[:, columns]
        turned = values * cosine + pltpu.roll(values, HEAD // 2, 1) * sine
        rows_ref[:, columns] = turned.astype(jnp.bfloat16)
    slots = lax.broadcasted_iota(jnp.int32, (out_ref.shape[0], rows), 0)
    placed = (slots == slot_ref[...]).astype(jnp.bfloat16)
    out_ref[...] = jnp.dot(
        placed, rows_ref[...], preferred_element_type=jnp.float32
    ).astype(jnp.bfloat16)


def turn_tables(positions):
    half_head = HEAD // 2
    frequencies = rope_theta ** (-(jnp.arange(half_head, dtype=jnp.float32) * 2.0) / HEAD)
    angles = positions.astype(jnp.float32)[:, None] * frequencies[None, :]
    cosine = jnp.cos(angles)
    sine = jnp.sin(angles)
    return (
        jnp.concatenate([cosine, cosine], axis=1),
        jnp.concatenate([-sine, sine], axis=1),
    )


def planes_outgoing(
    tokens,
    input_norm_scale,
    key_matrix,
    adapter_down_weight,
    adapter_up_weight,
    lengths,
    prompt_adapter_index,
    active_adapter_ids,
    positions,
    slot_index,
    out_rows,
):
    peer_count = PLANE * PLANES
    rows, width = tokens.shape
    quarter = width // PLANE
    adapter_device, rank, key_width = adapter_up_weight.shape
    part = rank // PLANE
    hot_count = active_adapter_ids.shape[0]
    prompt_index = prompt_adapter_index[:, 0]
    piece = jax.ShapeDtypeStruct((adapter_device, rank + part, quarter), jnp.bfloat16)
    packed = call(
        functools.partial(pack_kernel, quarter),
        [piece] * PLANE,
        [ANY, ANY],
        [ANY] * PLANE,
        [pltpu.SemaphoreType.DMA((2 * PLANE,))],
    )(jnp.swapaxes(adapter_down_weight, 1, 2), adapter_up_weight)
    packed = list(packed)
    local = [packed[0]] + [
        swap(packed[distance], distance, peer_count) for distance in range(1, PLANE)
    ]
    plan = call(
        functools.partial(plan_kernel, rows, adapter_device),
        jax.ShapeDtypeStruct((SECTIONS * hot_count + 3 + 2 * lengths.shape[0],), jnp.int32),
        [SMEM] * 3,
        SMEM,
    )(lengths, prompt_index, active_adapter_ids)
    tokens, packed[0] = lax.optimization_barrier((tokens, packed[0]))
    local[0] = packed[0]
    block = rows // 4
    normed, *columns = pl.pallas_call(
        norm_kernel,
        grid=(4,),
        out_shape=[jax.ShapeDtypeStruct((rows, width), jnp.bfloat16)]
        + [jax.ShapeDtypeStruct((rows, quarter), jnp.bfloat16)] * PLANE,
        in_specs=[
            pl.BlockSpec((block, width), lambda at: (at, 0)),
            pl.BlockSpec((1, width), lambda at: (0, 0)),
        ],
        out_specs=[pl.BlockSpec((block, width), lambda at: (at, 0))]
        + [pl.BlockSpec((block, quarter), lambda at: (at, 0))] * PLANE,
        compiler_params=pltpu.CompilerParams(vmem_limit_bytes=VMEM_LIMIT),
    )(tokens, input_norm_scale.reshape(1, width))
    base = jnp.dot(normed, key_matrix, preferred_element_type=jnp.float32)
    cosine, sine = turn_tables(positions)
    second = swap(columns[1], 1, peer_count)
    plan, base, cosine, sine, slot_index, second = lax.optimization_barrier(
        (plan, base, cosine, sine, slot_index, second)
    )

    def branch(slots):
        def run(plan, third, fourth, *local):
            sends = call(
                functools.partial(select_kernel, slots, hot_count, adapter_device),
                [
                    jax.ShapeDtypeStruct((slot, rank + part, quarter), jnp.bfloat16)
                    for slot in slots
                ],
                [SMEM] + [ANY] * PLANE,
                [ANY] * len(slots),
                [pltpu.SemaphoreType.DMA((sum(slots),))],
            )(plan, *local)
            *sends, third, fourth = lax.optimization_barrier((*sends, third, fourth))
            arrived = [
                swap(send, (at + 1) * PLANE, peer_count) for at, send in enumerate(sends)
            ]
            third = swap(third, 2, peer_count)
            fourth = swap(fourth, 3, peer_count)
            collected = call(
                functools.partial(collect_kernel, rank, hot_count, adapter_device),
                [jax.ShapeDtypeStruct((hot_count, rank + part, quarter), jnp.bfloat16)]
                + [jax.ShapeDtypeStruct((FEW, part, key_width), jnp.bfloat16)] * PLANE,
                [SMEM] + [ANY] * (PLANE + PLANES - 1),
                [VMEM] * (1 + PLANE),
                [pltpu.SemaphoreType.DMA((hot_count,))],
            )(plan, *local, *arrived)
            return (third, fourth, *collected)

        return run

    cases = [branch(slots) for slots in SLOT_CASES + ((hot_count,) * (PLANES - 1),)]
    third, fourth, used_rows, *ups = lax.switch(
        plan[SECTIONS * hot_count + 1], cases, plan, columns[2], columns[3], *local
    )

    def share(parts):
        return [parts[0]] + [
            swap(parts[distance], distance, peer_count) for distance in range(1, PLANE)
        ]

    def more_ups(plan, used_rows):
        return share(
            call(
                functools.partial(share_kernel, FEW, rank, hot_count),
                [jax.ShapeDtypeStruct((hot_count - FEW, part, key_width), jnp.bfloat16)] * PLANE,
                [SMEM, VMEM],
                [VMEM] * PLANE,
            )(plan, used_rows)
        )

    def no_more(plan, used_rows):
        del used_rows
        empty = call(
            nothing_kernel,
            [jax.ShapeDtypeStruct((hot_count - FEW, part, key_width), jnp.bfloat16)] * PLANE,
            [SMEM],
            [VMEM] * PLANE,
        )(plan)
        return list(empty)

    ups = share(ups)
    sums = call(
        functools.partial(partial_kernel, rank, hot_count),
        [jax.ShapeDtypeStruct((rank, rows), jnp.float32)] * PLANE,
        [SMEM] + [VMEM] * (1 + PLANE),
        [VMEM] * PLANE,
        flops=2 * hot_count * rank * width * rows,
        bytes_accessed=40 * 1024 * 1024,
    )(plan, used_rows, columns[0], second, third, fourth)
    partials = share(sums)
    late_plan, late_rows, _ = lax.optimization_barrier((plan, used_rows, sums[0]))
    more = lax.cond(
        late_plan[SECTIONS * hot_count + 2] == 1, no_more, more_ups, late_plan, late_rows
    )
    return call(
        functools.partial(finish_kernel, hot_count),
        jax.ShapeDtypeStruct((out_rows, key_width), jnp.bfloat16),
        [SMEM] + [VMEM] * (4 + 3 * PLANE),
        VMEM,
        [
            pltpu.VMEM((rank, rows), jnp.float32),
            pltpu.VMEM((rows, key_width), jnp.float32),
            pltpu.VMEM((rows, key_width), jnp.bfloat16),
        ],
        flops=2 * rows * key_width * (hot_count * rank + out_rows),
        bytes_accessed=6 * 1024 * 1024,
    )(
        plan,
        base,
        cosine,
        sine,
        slot_index.reshape(1, rows),
        *partials,
        *ups,
        *more,
    )


def gathered_outgoing(
    tokens,
    input_norm_scale,
    key_matrix,
    adapter_down_weight,
    adapter_up_weight,
    active_adapter_ids,
    positions,
    hot_slots,
    slot_index,
    out_rows,
):
    float_rows = tokens.astype(jnp.float32)
    inverse_rms = lax.rsqrt(jnp.mean(float_rows * float_rows, axis=1, keepdims=True) + norm_eps)
    normed = (float_rows * inverse_rms * input_norm_scale[None, :]).astype(jnp.bfloat16)
    adapter_device = adapter_down_weight.shape[0]
    down_list = []
    up_list = []
    for entry in range(active_adapter_ids.shape[0]):
        adapter = active_adapter_ids[entry]
        for weight, gathered in ((adapter_down_weight, down_list), (adapter_up_weight, up_list)):
            mine = lax.dynamic_index_in_dim(weight, adapter % adapter_device, 0, keepdims=False)
            gathered.append(spread(mine, "seq", adapter // adapter_device))
    down_matrices = jnp.concatenate(down_list, axis=1)
    up_matrices = jnp.concatenate(up_list, axis=0)
    base_proj = jnp.dot(normed, key_matrix, preferred_element_type=jnp.float32)
    low_rank = jnp.dot(normed, down_matrices, preferred_element_type=jnp.float32).astype(
        jnp.bfloat16
    )
    column_owned = (jnp.arange(down_matrices.shape[1], dtype=jnp.int32) // ADAPTER_RANK)[
        None, :
    ] == hot_slots[:, None]
    low_rank = jnp.where(column_owned, low_rank, jnp.zeros_like(low_rank))
    projected = base_proj + jnp.dot(low_rank, up_matrices, preferred_element_type=jnp.float32)
    key_rows = rotate(projected, positions).astype(jnp.bfloat16)
    return jnp.zeros((out_rows, key_rows.shape[1]), jnp.bfloat16).at[slot_index].set(key_rows)


def on_device(
    tokens,
    input_norm_scale,
    key_matrix,
    adapter_down_weight,
    adapter_up_weight,
    lengths,
    prompt_adapter_index,
    active_adapter_ids,
    token_cache_device,
):
    rows_dev = tokens.shape[0]
    peer_count = lax.axis_size("seq")
    slot_count = max(4, 2 * rows_dev // peer_count)
    key_width = key_matrix.shape[1]
    targets = token_cache_device[:, 0]
    row_order = jnp.arange(rows_dev, dtype=jnp.int32)
    earlier = row_order[None, :] < row_order[:, None]
    rank_within = jnp.sum(
        ((targets[:, None] == targets[None, :]) & earlier).astype(jnp.int32), axis=1
    )
    slot_index = targets * slot_count + rank_within
    positions, hot_slots = locate(
        lengths, prompt_adapter_index, lax.axis_index("seq") * rows_dev, rows_dev
    )
    out_rows = peer_count * slot_count
    if peer_count == PLANE * PLANES:
        outgoing = planes_outgoing(
            tokens,
            input_norm_scale,
            key_matrix,
            adapter_down_weight,
            adapter_up_weight,
            lengths,
            prompt_adapter_index,
            active_adapter_ids,
            positions,
            slot_index,
            out_rows,
        )
    else:
        outgoing = gathered_outgoing(
            tokens,
            input_norm_scale,
            key_matrix,
            adapter_down_weight,
            adapter_up_weight,
            active_adapter_ids,
            positions,
            hot_slots,
            slot_index,
            out_rows,
        )
    outgoing = outgoing.reshape(peer_count, slot_count, key_width)
    result = lax.all_to_all(outgoing, "seq", split_axis=0, concat_axis=0, tiled=True)
    return result.reshape(out_rows, key_width)


def solution(mesh):
    in_specs = (
        P(("groups", "seq"), None),
        P(),
        P(),
        P("seq", None, None),
        P("seq", None, None),
        P("groups"),
        P("groups", None),
        P("groups"),
        P(("groups", "seq"), None),
    )
    out_specs = P(("groups", "seq"), None)
    return jax.shard_map(
        on_device, mesh=mesh, in_specs=in_specs, out_specs=out_specs, check_vma=False
    )
```

```python
import functools

import jax
import jax.numpy as jnp
from jax import lax
from jax.experimental import pallas as pl
from jax.experimental.pallas import tpu as pltpu
from jax.sharding import PartitionSpec as P

HEAD = 128
ADAPTER_RANK = 64


rope_theta = 500000.0
norm_eps = 1e-05


def spread(array, axis, root):
    mine = lax.axis_index(axis) == root
    return lax.psum(jnp.where(mine, array, jnp.zeros_like(array)), axis)


def rotate(projected, positions):
    half_head = HEAD // 2
    frequencies = rope_theta ** (-(jnp.arange(half_head, dtype=jnp.float32) * 2.0) / HEAD)
    angles = positions.astype(jnp.float32)[:, None] * frequencies[None, :]
    cosine = jnp.cos(angles)[:, None, :]
    sine_table = jnp.sin(angles)[:, None, :]
    per_head = projected.reshape(projected.shape[0], -1, HEAD)
    first_half = per_head[..., :half_head]
    second_half = per_head[..., half_head:]
    turned = jnp.concatenate(
        [
            first_half * cosine - second_half * sine_table,
            second_half * cosine + first_half * sine_table,
        ],
        axis=-1,
    )
    return turned.reshape(projected.shape)


def locate(lengths, prompt_adapter_index, first_row, row_count):
    prompt_ends = jnp.cumsum(lengths)
    prompt_starts = prompt_ends - lengths
    row_ids = first_row + jnp.arange(row_count, dtype=jnp.int32)
    prompt_ids = jnp.sum((prompt_ends[None, :] <= row_ids[:, None]).astype(jnp.int32), axis=1)
    prompt_match = prompt_ids[:, None] == jnp.arange(lengths.shape[0], dtype=jnp.int32)[None, :]
    prompt_start = jnp.sum(jnp.where(prompt_match, prompt_starts[None, :], 0), axis=1)
    hot_slots = jnp.sum(jnp.where(prompt_match, prompt_adapter_index[:, 0][None, :], 0), axis=1)
    return (row_ids - prompt_start, hot_slots)


PLANE = 4
PLANES = 4
SLOT_CASES = ((2, 1, 1), (3, 2, 1), (3, 1, 2), (3, 2, 2), (3, 3, 1), (3, 1, 3), (4, 3, 3))
FEW = 3
ANY = pl.BlockSpec(memory_space=pl.ANY)
SMEM = pl.BlockSpec(memory_space=pltpu.SMEM)
VMEM = pl.BlockSpec(memory_space=pltpu.VMEM)
VMEM_LIMIT = 40 * 1024 * 1024


def swap(value, distance, peer_count):
    return lax.ppermute(value, "seq", [(i, i ^ distance) for i in range(peer_count)])


def call(kernel, out_shape, in_specs, out_specs, scratch=(), **cost):
    return pl.pallas_call(
        kernel,
        out_shape=out_shape,
        in_specs=in_specs,
        out_specs=out_specs,
        scratch_shapes=list(scratch),
        compiler_params=pltpu.CompilerParams(vmem_limit_bytes=VMEM_LIMIT),
        cost_estimate=pl.CostEstimate(transcendentals=0, **cost) if cost else None,
    )


FROM_KIND, FROM_SLOT, PLANE_LIST, DEVICE_LISTS, SECTIONS = 3, 4, 5, 6, 10


def bit_of(mask, entry):
    return lax.shift_right_logical(mask, entry) & 1


def plan_kernel(rows, adapter_device, length_ref, index_ref, id_ref, plan_ref):
    hot_count = id_ref.shape[0]
    device = lax.axis_index("seq")
    plane = lax.div(device, PLANE)
    place = device - plane * PLANE
    for at in range(FROM_KIND * hot_count):
        plan_ref[at] = 0
    for at in range(PLANE_LIST * hot_count, SECTIONS * hot_count):
        plan_ref[at] = -1
    devices = PLANE * PLANES
    uses = [jnp.int32(0)] * devices
    start = jnp.int32(0)
    for prompt in range(length_ref.shape[0]):
        end = start + length_ref[prompt]
        bit = lax.shift_left(jnp.int32(1), index_ref[prompt])
        plan_ref[SECTIONS * hot_count + 3 + 2 * prompt] = end
        plan_ref[SECTIONS * hot_count + 4 + 2 * prompt] = index_ref[prompt]
        for at in range(devices):
            hit = (start < (at + 1) * rows) & (end > at * rows)
            uses[at] = uses[at] | jnp.where(hit, bit, 0)
        start = end
    need = []
    for at in range(PLANES):
        mask = uses[at * PLANE]
        for inner in range(1, PLANE):
            mask = mask | uses[at * PLANE + inner]
        need.append(mask)

    def pick(masks, which):
        total = masks[0]
        for at in range(1, len(masks)):
            total = jnp.where(which == at, masks[at], total)
        return total

    def list_bits(section, mask, values):
        count = jnp.int32(0)
        for entry in range(hot_count):

            @pl.when(bit_of(mask, entry) == 1)
            def _():
                plan_ref[section * hot_count + count] = values[entry]

            count = count + bit_of(mask, entry)
        return count

    owner_plane = []
    kind = []
    slot = []
    local = []
    for entry in range(hot_count):
        adapter = id_ref[entry]
        owner = lax.div(adapter, adapter_device)
        owner_plane.append(lax.div(owner, PLANE))
        local.append(
            ((owner - owner_plane[entry] * PLANE) ^ place) * adapter_device
            + adapter
            - owner * adapter_device
        )
        kind.append(jnp.int32(0))
        slot.append(local[entry])
    need_here = pick(need, plane)
    for distance in range(1, PLANES):
        other = plane ^ distance
        need_there = pick(need, other)
        sent = jnp.int32(0)
        taken = jnp.int32(0)
        for entry in range(hot_count):
            plan_ref[(distance - 1) * hot_count + sent] = local[entry]
            sent = sent + jnp.where(owner_plane[entry] == plane, bit_of(need_there, entry), 0)
            wanted = jnp.where(owner_plane[entry] == other, bit_of(need_here, entry), 0)
            kind[entry] = jnp.where(wanted == 1, distance, kind[entry])
            slot[entry] = jnp.where(wanted == 1, taken, slot[entry])
            taken = taken + wanted
    for entry in range(hot_count):
        plan_ref[FROM_KIND * hot_count + entry] = kind[entry]
        plan_ref[FROM_SLOT * hot_count + entry] = slot[entry]
    listed = [jnp.int32(0)]
    for entry in range(hot_count):
        listed.append(listed[entry] + bit_of(need_here, entry))
    plan_ref[SECTIONS * hot_count] = list_bits(
        PLANE_LIST, need_here, [jnp.int32(entry) for entry in range(hot_count)]
    )
    for distance in range(PLANE):
        list_bits(DEVICE_LISTS + distance, pick(uses, device ^ distance), listed)
    most = []
    for distance in range(1, PLANES):
        largest = jnp.int32(0)
        for at in range(PLANES):
            count = jnp.int32(0)
            for entry in range(hot_count):
                wanted = bit_of(need[at ^ distance], entry)
                count = count + jnp.where(owner_plane[entry] == at, wanted, 0)
            largest = jnp.maximum(largest, count)
        most.append(largest)
    few = jnp.bool_(True)
    for at in range(devices):
        count = jnp.int32(0)
        for entry in range(hot_count):
            count = count + bit_of(uses[at], entry)
        few = few & (count <= FEW)
    case = jnp.int32(len(SLOT_CASES))
    for at in reversed(range(len(SLOT_CASES))):
        fits = few
        for distance in range(PLANES - 1):
            fits = fits & (most[distance] <= SLOT_CASES[at][distance])
        case = jnp.where(fits, at, case)
    plan_ref[SECTIONS * hot_count + 1] = case
    plan_ref[SECTIONS * hot_count + 2] = jnp.where(few, 1, 0)


def norm_kernel(token_ref, scale_ref, out_ref, *quarter_refs):
    values = token_ref[...].astype(jnp.float32)
    inverse_rms = lax.rsqrt(jnp.mean(values * values, axis=1, keepdims=True) + norm_eps)
    out_ref[...] = (values * inverse_rms * scale_ref[...]).astype(jnp.bfloat16)
    place = lax.rem(lax.axis_index("seq"), PLANE)
    quarter = quarter_refs[0].shape[1]
    for distance in range(PLANE):
        first = pl.multiple_of((place ^ distance) * quarter, quarter)
        quarter_refs[distance][...] = out_ref[:, pl.ds(first, quarter)]


def pack_kernel(quarter, down_ref, up_ref, *refs):
    outs = refs[:PLANE]
    sems = refs[PLANE]
    place = lax.rem(lax.axis_index("seq"), PLANE)
    rank = down_ref.shape[1]
    part = rank // PLANE
    copies = []
    for distance in range(PLANE):
        other = place ^ distance
        columns = pl.ds(pl.multiple_of(other * quarter, quarter), quarter)
        copies.append(
            pltpu.make_async_copy(
                down_ref.at[:, :, columns],
                outs[distance].at[:, pl.ds(0, rank), :],
                sems.at[2 * distance],
            )
        )
        rows = pl.ds(pl.multiple_of(other * part, part), part)
        copies.append(
            pltpu.make_async_copy(
                up_ref.at[:, rows, :],
                outs[distance].at[:, pl.ds(rank, part), :],
                sems.at[2 * distance + 1],
            )
        )
    for copy in copies:
        copy.start()
    for copy in copies:
        copy.wait()


def select_kernel(slots, hot_count, adapter_device, plan_ref, *refs):
    local = refs[:PLANE]
    outs = refs[PLANE : PLANE + PLANES - 1]
    sems = refs[-1]
    waits = []
    for distance in range(1, PLANES):
        for slot in range(slots[distance - 1]):
            index = plan_ref[(distance - 1) * hot_count + slot]
            holder = lax.div(index, adapter_device)
            inner = index - holder * adapter_device
            target = outs[distance - 1].at[slot]
            sem = sems.at[len(waits)]
            for at in range(PLANE):

                @pl.when(holder == at)
                def _():
                    pltpu.make_async_copy(local[at].at[inner], target, sem).start()

            waits.append(pltpu.make_async_copy(local[0].at[0], target, sem))
    for wait in waits:
        wait.wait()


def start_rows(plan_ref, entry, hot_count, adapter_device, local, arrived, copy_of):
    kind = plan_ref[FROM_KIND * hot_count + entry]
    slot = plan_ref[FROM_SLOT * hot_count + entry]

    @pl.when(kind == 0)
    def _():
        holder = lax.div(slot, adapter_device)
        inner = slot - holder * adapter_device
        for at in range(PLANE):

            @pl.when(holder == at)
            def _():
                copy_of(local[at].at[inner]).start()

    for distance in range(1, PLANES):

        @pl.when(kind == distance)
        def _():
            copy_of(arrived[distance - 1].at[slot]).start()


def share_rows(first, count, rank, hot_count, plan_ref, rows_ref, outs):
    for distance in range(PLANE):
        for at in range(count):
            listed = plan_ref[(DEVICE_LISTS + distance) * hot_count + first + at]
            outs[distance][at] = rows_ref[jnp.maximum(listed, 0), rank:, :]


def share_kernel(first, rank, hot_count, plan_ref, rows_ref, *outs):
    share_rows(first, outs[0].shape[0], rank, hot_count, plan_ref, rows_ref, outs)


def collect_kernel(hot_count, adapter_device, plan_ref, *refs):
    local = refs[:PLANE]
    arrived = refs[PLANE : PLANE + PLANES - 1]
    out_ref, sems = refs[PLANE + PLANES - 1], refs[-1]
    used = plan_ref[SECTIONS * hot_count]

    def copy_of(at):
        return lambda source: pltpu.make_async_copy(source, out_ref.at[at], sems.at[at])

    for at in range(hot_count):

        @pl.when(at < used)
        def _():
            entry = plan_ref[PLANE_LIST * hot_count + at]
            start_rows(plan_ref, entry, hot_count, adapter_device, local, arrived, copy_of(at))

    for at in range(hot_count):

        @pl.when(at < used)
        def _():
            copy_of(at)(local[0].at[0]).wait()


def hot_lanes(first_row, rows, hot_count, plan_ref):
    row_ids = first_row + lax.broadcasted_iota(jnp.int32, (1, rows), 1)
    hot = jnp.zeros((1, rows), jnp.int32)
    start = jnp.int32(0)
    for at in range(SECTIONS * hot_count + 3, plan_ref.shape[0], 2):
        end = plan_ref[at]
        hot = jnp.where((row_ids >= start) & (row_ids < end), plan_ref[at + 1], hot)
        start = end
    return hot


def partial_kernel(rank, hot_count, plan_ref, rows_ref, *refs):
    tokens = refs[:PLANE]
    outs = refs[PLANE : 2 * PLANE]
    sums = refs[2 * PLANE]
    device = lax.axis_index("seq")
    rows = tokens[0].shape[0]
    half = hot_count // 2
    part = rank // PLANE
    share_rows(0, FEW, rank, hot_count, plan_ref, rows_ref, outs)

    def run(first, last):
        down = jnp.concatenate([rows_ref[at, :rank, :] for at in range(first, last)], axis=0).T
        for distance in range(PLANE):
            product = jnp.dot(
                tokens[distance][...], down, preferred_element_type=jnp.float32
            ).T
            hot = hot_lanes((device ^ distance) * rows, rows, hot_count, plan_ref)
            total = sums[distance] if first else jnp.zeros((rank, rows), jnp.float32)
            for at in range(first, last):
                piece = product[(at - first) * rank : (at - first + 1) * rank]
                total = jnp.where(hot == plan_ref[PLANE_LIST * hot_count + at], piece, total)
            sums[distance] = total

    run(0, half)

    @pl.when(plan_ref[SECTIONS * hot_count] > half)
    def _():
        run(half, hot_count)

    for distance in range(PLANE):
        for at in range(PLANE):
            total = sums[distance, at * part : (at + 1) * part]
            high = total.astype(jnp.bfloat16)
            low = (total - high.astype(jnp.float32)).astype(jnp.bfloat16)
            outs[distance][FEW, :, at * rows : (at + 1) * rows] = high
            outs[distance][FEW + 1, :, at * rows : (at + 1) * rows] = low


def finish_kernel(
    hot_count,
    plan_ref,
    base_ref,
    cosine_ref,
    sine_ref,
    slot_ref,
    *refs,
):
    shared = refs[:PLANE]
    more = refs[PLANE : 2 * PLANE]
    out_ref, low_ref, sum_ref, rows_ref = refs[2 * PLANE :]
    _, part, key_width = shared[0].shape
    rows = base_ref.shape[0]
    device = lax.axis_index("seq")
    place = lax.rem(device, PLANE)
    for at in range(PLANE):
        total = jnp.zeros((part, rows), jnp.float32)
        for distance in range(PLANE):
            for term in (FEW, FEW + 1):
                total = total + shared[distance][term, :, at * rows : (at + 1) * rows].astype(
                    jnp.float32
                )
        low_ref[at * part : (at + 1) * part] = total
    hot = hot_lanes(device * rows, rows, hot_count, plan_ref)

    def adapted(held, first_entry, count):
        entries = []
        for at in range(first_entry, first_entry + count):
            listed = plan_ref[DEVICE_LISTS * hot_count + at]
            entry = plan_ref[PLANE_LIST * hot_count + jnp.maximum(listed, 0)]
            entries.append(jnp.where(listed >= 0, entry, -1))
        result = None
        for distance in range(PLANE):
            first = pl.multiple_of((place ^ distance) * part, part)
            piece = low_ref[pl.ds(first, part), :]
            spread_rows = jnp.concatenate(
                [jnp.where(hot == entry, piece, 0.0) for entry in entries], axis=0
            ).astype(jnp.bfloat16)
            product = lax.dot_general(
                spread_rows,
                held[distance][:count].reshape(count * part, key_width),
                (((0,), (0,)), ((), ())),
                preferred_element_type=jnp.float32,
            )
            result = product if result is None else result + product
        return result

    sum_ref[...] = base_ref[...] + adapted(shared, 0, FEW)

    @pl.when(plan_ref[SECTIONS * hot_count + 2] == 0)
    def _():
        sum_ref[...] += adapted(more, FEW, hot_count - FEW)

    projected = sum_ref[...]
    cosine = cosine_ref[...]
    sine = sine_ref[...]
    for head in range(key_width // HEAD):
        columns = slice(head * HEAD, (head + 1) * HEAD)
        values = projected[:, columns]
        turned = values * cosine + pltpu.roll(values, HEAD // 2, 1) * sine
        rows_ref[:, columns] = turned.astype(jnp.bfloat16)
    slots = lax.broadcasted_iota(jnp.int32, (out_ref.shape[0], rows), 0)
    placed = (slots == slot_ref[...]).astype(jnp.bfloat16)
    out_ref[...] = jnp.dot(
        placed, rows_ref[...], preferred_element_type=jnp.float32
    ).astype(jnp.bfloat16)


def turn_tables(positions):
    half_head = HEAD // 2
    frequencies = rope_theta ** (-(jnp.arange(half_head, dtype=jnp.float32) * 2.0) / HEAD)
    angles = positions.astype(jnp.float32)[:, None] * frequencies[None, :]
    cosine = jnp.cos(angles)
    sine = jnp.sin(angles)
    return (
        jnp.concatenate([cosine, cosine], axis=1),
        jnp.concatenate([-sine, sine], axis=1),
    )


def planes_outgoing(
    tokens,
    input_norm_scale,
    key_matrix,
    adapter_down_weight,
    adapter_up_weight,
    lengths,
    prompt_adapter_index,
    active_adapter_ids,
    positions,
    slot_index,
    out_rows,
):
    peer_count = PLANE * PLANES
    rows, width = tokens.shape
    quarter = width // PLANE
    adapter_device, rank, key_width = adapter_up_weight.shape
    part = rank // PLANE
    hot_count = active_adapter_ids.shape[0]
    prompt_index = prompt_adapter_index[:, 0]
    piece = jax.ShapeDtypeStruct((adapter_device, rank + part, quarter), jnp.bfloat16)
    packed = call(
        functools.partial(pack_kernel, quarter),
        [piece] * PLANE,
        [ANY, ANY],
        [ANY] * PLANE,
        [pltpu.SemaphoreType.DMA((2 * PLANE,))],
    )(jnp.swapaxes(adapter_down_weight, 1, 2), adapter_up_weight)
    local = [packed[0]] + [
        swap(packed[distance], distance, peer_count) for distance in range(1, PLANE)
    ]
    plan = call(
        functools.partial(plan_kernel, rows, adapter_device),
        jax.ShapeDtypeStruct((SECTIONS * hot_count + 3 + 2 * lengths.shape[0],), jnp.int32),
        [SMEM] * 3,
        SMEM,
    )(lengths, prompt_index, active_adapter_ids)
    tokens, local[1] = lax.optimization_barrier((tokens, local[1]))
    block = rows // 4
    normed, *columns = pl.pallas_call(
        norm_kernel,
        grid=(4,),
        out_shape=[jax.ShapeDtypeStruct((rows, width), jnp.bfloat16)]
        + [jax.ShapeDtypeStruct((rows, quarter), jnp.bfloat16)] * PLANE,
        in_specs=[
            pl.BlockSpec((block, width), lambda at: (at, 0)),
            pl.BlockSpec((1, width), lambda at: (0, 0)),
        ],
        out_specs=[pl.BlockSpec((block, width), lambda at: (at, 0))]
        + [pl.BlockSpec((block, quarter), lambda at: (at, 0))] * PLANE,
        compiler_params=pltpu.CompilerParams(vmem_limit_bytes=VMEM_LIMIT),
    )(tokens, input_norm_scale.reshape(1, width))
    base = jnp.dot(normed, key_matrix, preferred_element_type=jnp.float32)
    cosine, sine = turn_tables(positions)
    second = swap(columns[1], 1, peer_count)
    plan, base, cosine, sine, slot_index, second = lax.optimization_barrier(
        (plan, base, cosine, sine, slot_index, second)
    )

    rest = jax.ShapeDtypeStruct((hot_count - FEW, part, key_width), jnp.bfloat16)

    def share(parts):
        return [parts[0]] + [
            swap(parts[distance], distance, peer_count) for distance in range(1, PLANE)
        ]

    def branch(slots):
        def run(plan, third, fourth, *local):
            sends = call(
                functools.partial(select_kernel, slots, hot_count, adapter_device),
                [
                    jax.ShapeDtypeStruct((slot, rank + part, quarter), jnp.bfloat16)
                    for slot in slots
                ],
                [SMEM] + [ANY] * PLANE,
                [ANY] * len(slots),
                [pltpu.SemaphoreType.DMA((sum(slots),))],
            )(plan, *local)
            *sends, third, fourth = lax.optimization_barrier((*sends, third, fourth))
            arrived = [
                swap(send, (at + 1) * PLANE, peer_count) for at, send in enumerate(sends)
            ]
            third = swap(third, 2, peer_count)
            fourth = swap(fourth, 3, peer_count)
            collected, *more = call(
                functools.partial(collect_kernel, hot_count, adapter_device),
                [jax.ShapeDtypeStruct((hot_count, rank + part, quarter), jnp.bfloat16)]
                + ([] if slots[0] == hot_count else [rest] * PLANE),
                [SMEM] + [ANY] * (PLANE + PLANES - 1),
                [VMEM] * (1 if slots[0] == hot_count else 1 + PLANE),
                [pltpu.SemaphoreType.DMA((hot_count,))],
            )(plan, *local, *arrived)
            if not more:
                more = share(
                    call(
                        functools.partial(share_kernel, FEW, rank, hot_count),
                        [rest] * PLANE,
                        [SMEM, VMEM],
                        [VMEM] * PLANE,
                    )(plan, collected)
                )
            return (third, fourth, collected, *more)

        return run

    cases = [branch(slots) for slots in SLOT_CASES + ((hot_count,) * (PLANES - 1),)]
    third, fourth, used_rows, *more = lax.switch(
        plan[SECTIONS * hot_count + 1], cases, plan, columns[2], columns[3], *local
    )

    shared = share(
        call(
            functools.partial(partial_kernel, rank, hot_count),
            [jax.ShapeDtypeStruct((FEW + 2, part, key_width), jnp.bfloat16)] * PLANE,
            [SMEM] + [VMEM] * (1 + PLANE),
            [VMEM] * PLANE,
            [pltpu.VMEM((PLANE, rank, rows), jnp.float32)],
            flops=2 * hot_count * rank * width * rows,
            bytes_accessed=6 * 1024 * 1024,
        )(plan, used_rows, columns[0], second, third, fourth)
    )
    return call(
        functools.partial(finish_kernel, hot_count),
        jax.ShapeDtypeStruct((out_rows, key_width), jnp.bfloat16),
        [SMEM] + [VMEM] * (4 + 2 * PLANE),
        VMEM,
        [
            pltpu.VMEM((rank, rows), jnp.float32),
            pltpu.VMEM((rows, key_width), jnp.float32),
            pltpu.VMEM((rows, key_width), jnp.bfloat16),
        ],
        flops=2 * rows * key_width * (hot_count * rank + out_rows),
        bytes_accessed=6 * 1024 * 1024,
    )(
        plan,
        base,
        cosine,
        sine,
        slot_index.reshape(1, rows),
        *shared,
        *more,
    )


def gathered_outgoing(
    tokens,
    input_norm_scale,
    key_matrix,
    adapter_down_weight,
    adapter_up_weight,
    active_adapter_ids,
    positions,
    hot_slots,
    slot_index,
    out_rows,
):
    float_rows = tokens.astype(jnp.float32)
    inverse_rms = lax.rsqrt(jnp.mean(float_rows * float_rows, axis=1, keepdims=True) + norm_eps)
    normed = (float_rows * inverse_rms * input_norm_scale[None, :]).astype(jnp.bfloat16)
    adapter_device = adapter_down_weight.shape[0]
    down_list = []
    up_list = []
    for entry in range(active_adapter_ids.shape[0]):
        adapter = active_adapter_ids[entry]
        for weight, gathered in ((adapter_down_weight, down_list), (adapter_up_weight, up_list)):
            mine = lax.dynamic_index_in_dim(weight, adapter % adapter_device, 0, keepdims=False)
            gathered.append(spread(mine, "seq", adapter // adapter_device))
    down_matrices = jnp.concatenate(down_list, axis=1)
    up_matrices = jnp.concatenate(up_list, axis=0)
    base_proj = jnp.dot(normed, key_matrix, preferred_element_type=jnp.float32)
    low_rank = jnp.dot(normed, down_matrices, preferred_element_type=jnp.float32).astype(
        jnp.bfloat16
    )
    column_owned = (jnp.arange(down_matrices.shape[1], dtype=jnp.int32) // ADAPTER_RANK)[
        None, :
    ] == hot_slots[:, None]
    low_rank = jnp.where(column_owned, low_rank, jnp.zeros_like(low_rank))
    projected = base_proj + jnp.dot(low_rank, up_matrices, preferred_element_type=jnp.float32)
    key_rows = rotate(projected, positions).astype(jnp.bfloat16)
    return jnp.zeros((out_rows, key_rows.shape[1]), jnp.bfloat16).at[slot_index].set(key_rows)


def on_device(
    tokens,
    input_norm_scale,
    key_matrix,
    adapter_down_weight,
    adapter_up_weight,
    lengths,
    prompt_adapter_index,
    active_adapter_ids,
    token_cache_device,
):
    rows_dev = tokens.shape[0]
    peer_count = lax.axis_size("seq")
    slot_count = max(4, 2 * rows_dev // peer_count)
    key_width = key_matrix.shape[1]
    targets = token_cache_device[:, 0]
    row_order = jnp.arange(rows_dev, dtype=jnp.int32)
    earlier = row_order[None, :] < row_order[:, None]
    rank_within = jnp.sum(
        ((targets[:, None] == targets[None, :]) & earlier).astype(jnp.int32), axis=1
    )
    slot_index = targets * slot_count + rank_within
    positions, hot_slots = locate(
        lengths, prompt_adapter_index, lax.axis_index("seq") * rows_dev, rows_dev
    )
    out_rows = peer_count * slot_count
    if peer_count == PLANE * PLANES:
        outgoing = planes_outgoing(
            tokens,
            input_norm_scale,
            key_matrix,
            adapter_down_weight,
            adapter_up_weight,
            lengths,
            prompt_adapter_index,
            active_adapter_ids,
            positions,
            slot_index,
            out_rows,
        )
    else:
        outgoing = gathered_outgoing(
            tokens,
            input_norm_scale,
            key_matrix,
            adapter_down_weight,
            adapter_up_weight,
            active_adapter_ids,
            positions,
            hot_slots,
            slot_index,
            out_rows,
        )
    outgoing = outgoing.reshape(peer_count, slot_count, key_width)
    result = lax.all_to_all(outgoing, "seq", split_axis=0, concat_axis=0, tiled=True)
    return result.reshape(out_rows, key_width)


def solution(mesh):
    in_specs = (
        P(("groups", "seq"), None),
        P(),
        P(),
        P("seq", None, None),
        P("seq", None, None),
        P("groups"),
        P("groups", None),
        P("groups"),
        P(("groups", "seq"), None),
    )
    out_specs = P(("groups", "seq"), None)
    return jax.shard_map(
        on_device, mesh=mesh, in_specs=in_specs, out_specs=out_specs, check_vma=False
    )
```

```python
import functools

import jax
import jax.numpy as jnp
from jax import lax
from jax.experimental import pallas as pl
from jax.experimental.pallas import tpu as pltpu
from jax.sharding import PartitionSpec as P

HEAD = 128
ADAPTER_RANK = 64


rope_theta = 500000.0
norm_eps = 1e-05


def spread(array, axis, root):
    mine = lax.axis_index(axis) == root
    return lax.psum(jnp.where(mine, array, jnp.zeros_like(array)), axis)


def rotate(projected, positions):
    half_head = HEAD // 2
    frequencies = rope_theta ** (-(jnp.arange(half_head, dtype=jnp.float32) * 2.0) / HEAD)
    angles = positions.astype(jnp.float32)[:, None] * frequencies[None, :]
    cosine = jnp.cos(angles)[:, None, :]
    sine_table = jnp.sin(angles)[:, None, :]
    per_head = projected.reshape(projected.shape[0], -1, HEAD)
    first_half = per_head[..., :half_head]
    second_half = per_head[..., half_head:]
    turned = jnp.concatenate(
        [
            first_half * cosine - second_half * sine_table,
            second_half * cosine + first_half * sine_table,
        ],
        axis=-1,
    )
    return turned.reshape(projected.shape)


def locate(lengths, prompt_adapter_index, first_row, row_count):
    prompt_ends = jnp.cumsum(lengths)
    prompt_starts = prompt_ends - lengths
    row_ids = first_row + jnp.arange(row_count, dtype=jnp.int32)
    prompt_ids = jnp.sum((prompt_ends[None, :] <= row_ids[:, None]).astype(jnp.int32), axis=1)
    prompt_match = prompt_ids[:, None] == jnp.arange(lengths.shape[0], dtype=jnp.int32)[None, :]
    prompt_start = jnp.sum(jnp.where(prompt_match, prompt_starts[None, :], 0), axis=1)
    hot_slots = jnp.sum(jnp.where(prompt_match, prompt_adapter_index[:, 0][None, :], 0), axis=1)
    return (row_ids - prompt_start, hot_slots)


PLANE = 4
PLANES = 4
SLOT_CASES = (
    (2, 1, 1),
    (3, 2, 1),
    (3, 1, 2),
    (3, 2, 2),
    (3, 3, 1),
    (3, 1, 3),
    (4, 3, 2),
    (4, 2, 3),
    (4, 4, 1),
    (4, 1, 4),
    (4, 3, 3),
)
FEW = 3
ANY = pl.BlockSpec(memory_space=pl.ANY)
SMEM = pl.BlockSpec(memory_space=pltpu.SMEM)
VMEM = pl.BlockSpec(memory_space=pltpu.VMEM)
VMEM_LIMIT = 40 * 1024 * 1024


def swap(value, distance, peer_count):
    return lax.ppermute(value, "seq", [(i, i ^ distance) for i in range(peer_count)])


def call(kernel, out_shape, in_specs, out_specs, scratch=(), **cost):
    return pl.pallas_call(
        kernel,
        out_shape=out_shape,
        in_specs=in_specs,
        out_specs=out_specs,
        scratch_shapes=list(scratch),
        compiler_params=pltpu.CompilerParams(vmem_limit_bytes=VMEM_LIMIT),
        cost_estimate=pl.CostEstimate(transcendentals=0, **cost) if cost else None,
    )


FROM_KIND, FROM_SLOT, PLANE_LIST, DEVICE_LISTS, SECTIONS = 3, 4, 5, 6, 10


def bit_of(mask, entry):
    return lax.shift_right_logical(mask, entry) & 1


def plan_kernel(rows, adapter_device, length_ref, index_ref, id_ref, plan_ref):
    hot_count = id_ref.shape[0]
    device = lax.axis_index("seq")
    plane = lax.div(device, PLANE)
    place = device - plane * PLANE
    for at in range(FROM_KIND * hot_count):
        plan_ref[at] = 0
    for at in range(PLANE_LIST * hot_count, SECTIONS * hot_count):
        plan_ref[at] = -1
    devices = PLANE * PLANES
    uses = [jnp.int32(0)] * devices
    start = jnp.int32(0)
    for prompt in range(length_ref.shape[0]):
        end = start + length_ref[prompt]
        bit = lax.shift_left(jnp.int32(1), index_ref[prompt])
        plan_ref[SECTIONS * hot_count + 3 + 2 * prompt] = end
        plan_ref[SECTIONS * hot_count + 4 + 2 * prompt] = index_ref[prompt]
        for at in range(devices):
            hit = (start < (at + 1) * rows) & (end > at * rows)
            uses[at] = uses[at] | jnp.where(hit, bit, 0)
        start = end
    need = []
    for at in range(PLANES):
        mask = uses[at * PLANE]
        for inner in range(1, PLANE):
            mask = mask | uses[at * PLANE + inner]
        need.append(mask)

    def pick(masks, which):
        total = masks[0]
        for at in range(1, len(masks)):
            total = jnp.where(which == at, masks[at], total)
        return total

    def list_bits(section, mask, values):
        count = jnp.int32(0)
        for entry in range(hot_count):

            @pl.when(bit_of(mask, entry) == 1)
            def _():
                plan_ref[section * hot_count + count] = values[entry]

            count = count + bit_of(mask, entry)
        return count

    owner_plane = []
    kind = []
    slot = []
    local = []
    for entry in range(hot_count):
        adapter = id_ref[entry]
        owner = lax.div(adapter, adapter_device)
        owner_plane.append(lax.div(owner, PLANE))
        local.append(
            ((owner - owner_plane[entry] * PLANE) ^ place) * adapter_device
            + adapter
            - owner * adapter_device
        )
        kind.append(jnp.int32(0))
        slot.append(local[entry])
    need_here = pick(need, plane)
    for distance in range(1, PLANES):
        other = plane ^ distance
        need_there = pick(need, other)
        sent = jnp.int32(0)
        taken = jnp.int32(0)
        for entry in range(hot_count):
            plan_ref[(distance - 1) * hot_count + sent] = local[entry]
            sent = sent + jnp.where(owner_plane[entry] == plane, bit_of(need_there, entry), 0)
            wanted = jnp.where(owner_plane[entry] == other, bit_of(need_here, entry), 0)
            kind[entry] = jnp.where(wanted == 1, distance, kind[entry])
            slot[entry] = jnp.where(wanted == 1, taken, slot[entry])
            taken = taken + wanted
    for entry in range(hot_count):
        plan_ref[FROM_KIND * hot_count + entry] = kind[entry]
        plan_ref[FROM_SLOT * hot_count + entry] = slot[entry]
    listed = [jnp.int32(0)]
    for entry in range(hot_count):
        listed.append(listed[entry] + bit_of(need_here, entry))
    plan_ref[SECTIONS * hot_count] = list_bits(
        PLANE_LIST, need_here, [jnp.int32(entry) for entry in range(hot_count)]
    )
    for distance in range(PLANE):
        list_bits(DEVICE_LISTS + distance, pick(uses, device ^ distance), listed)
    most = []
    for distance in range(1, PLANES):
        largest = jnp.int32(0)
        for at in range(PLANES):
            count = jnp.int32(0)
            for entry in range(hot_count):
                wanted = bit_of(need[at ^ distance], entry)
                count = count + jnp.where(owner_plane[entry] == at, wanted, 0)
            largest = jnp.maximum(largest, count)
        most.append(largest)
    few = jnp.bool_(True)
    for at in range(devices):
        count = jnp.int32(0)
        for entry in range(hot_count):
            count = count + bit_of(uses[at], entry)
        few = few & (count <= FEW)
    case = jnp.int32(len(SLOT_CASES))
    for at in reversed(range(len(SLOT_CASES))):
        fits = few
        for distance in range(PLANES - 1):
            fits = fits & (most[distance] <= SLOT_CASES[at][distance])
        case = jnp.where(fits, at, case)
    plan_ref[SECTIONS * hot_count + 1] = case
    plan_ref[SECTIONS * hot_count + 2] = jnp.where(few, 1, 0)


def norm_kernel(token_ref, scale_ref, out_ref, *quarter_refs):
    values = token_ref[...].astype(jnp.float32)
    inverse_rms = lax.rsqrt(jnp.mean(values * values, axis=1, keepdims=True) + norm_eps)
    out_ref[...] = (values * inverse_rms * scale_ref[...]).astype(jnp.bfloat16)
    place = lax.rem(lax.axis_index("seq"), PLANE)
    quarter = quarter_refs[0].shape[1]
    for distance in range(PLANE):
        first = pl.multiple_of((place ^ distance) * quarter, quarter)
        quarter_refs[distance][...] = out_ref[:, pl.ds(first, quarter)]


def pack_kernel(quarter, down_ref, up_ref, *refs):
    outs = refs[:PLANE]
    sems = refs[PLANE]
    place = lax.rem(lax.axis_index("seq"), PLANE)
    rank = down_ref.shape[1]
    part = rank // PLANE
    copies = []
    for distance in range(PLANE):
        other = place ^ distance
        columns = pl.ds(pl.multiple_of(other * quarter, quarter), quarter)
        copies.append(
            pltpu.make_async_copy(
                down_ref.at[:, :, columns],
                outs[distance].at[:, pl.ds(0, rank), :],
                sems.at[2 * distance],
            )
        )
        rows = pl.ds(pl.multiple_of(other * part, part), part)
        copies.append(
            pltpu.make_async_copy(
                up_ref.at[:, rows, :],
                outs[distance].at[:, pl.ds(rank, part), :],
                sems.at[2 * distance + 1],
            )
        )
    for copy in copies:
        copy.start()
    for copy in copies:
        copy.wait()


def select_kernel(slots, hot_count, adapter_device, plan_ref, *refs):
    local = refs[:PLANE]
    outs = refs[PLANE:]
    for distance in range(1, PLANES):
        for slot in range(slots[distance - 1]):
            index = plan_ref[(distance - 1) * hot_count + slot]
            holder = lax.div(index, adapter_device)
            inner = index - holder * adapter_device
            for at in range(PLANE):

                @pl.when(holder == at)
                def _():
                    outs[distance - 1][slot] = local[at][inner]


def share_rows(first, count, rank, hot_count, plan_ref, rows_ref, outs):
    for distance in range(PLANE):
        for at in range(count):
            listed = plan_ref[(DEVICE_LISTS + distance) * hot_count + first + at]
            outs[distance][at] = rows_ref[jnp.maximum(listed, 0), rank:, :]


def share_kernel(first, rank, hot_count, plan_ref, rows_ref, *outs):
    share_rows(first, outs[0].shape[0], rank, hot_count, plan_ref, rows_ref, outs)


def collect_kernel(hot_count, adapter_device, plan_ref, *refs):
    local = refs[:PLANE]
    arrived = refs[PLANE : PLANE + PLANES - 1]
    out_ref = refs[PLANE + PLANES - 1]
    used = plan_ref[SECTIONS * hot_count]
    for place in range(hot_count):

        @pl.when(place < used)
        def _():
            entry = plan_ref[PLANE_LIST * hot_count + place]
            kind = plan_ref[FROM_KIND * hot_count + entry]
            slot = plan_ref[FROM_SLOT * hot_count + entry]

            @pl.when(kind == 0)
            def _():
                holder = lax.div(slot, adapter_device)
                inner = slot - holder * adapter_device
                for at in range(PLANE):

                    @pl.when(holder == at)
                    def _():
                        out_ref[place] = local[at][inner]

            for distance in range(1, PLANES):

                @pl.when(kind == distance)
                def _():
                    out_ref[place] = arrived[distance - 1][slot]


def hot_lanes(first_row, rows, hot_count, plan_ref):
    row_ids = first_row + lax.broadcasted_iota(jnp.int32, (1, rows), 1)
    hot = jnp.zeros((1, rows), jnp.int32)
    start = jnp.int32(0)
    for at in range(SECTIONS * hot_count + 3, plan_ref.shape[0], 2):
        end = plan_ref[at]
        hot = jnp.where((row_ids >= start) & (row_ids < end), plan_ref[at + 1], hot)
        start = end
    return hot


def partial_kernel(rank, hot_count, plan_ref, rows_ref, *refs):
    tokens = refs[:PLANE]
    outs = refs[PLANE : 2 * PLANE]
    sums = refs[2 * PLANE]
    device = lax.axis_index("seq")
    rows = tokens[0].shape[0]
    half = hot_count // 2
    part = rank // PLANE
    share_rows(0, FEW, rank, hot_count, plan_ref, rows_ref, outs)

    def run(first, last):
        down = jnp.concatenate([rows_ref[at, :rank, :] for at in range(first, last)], axis=0).T
        for distance in range(PLANE):
            product = jnp.dot(
                tokens[distance][...], down, preferred_element_type=jnp.float32
            ).T
            hot = hot_lanes((device ^ distance) * rows, rows, hot_count, plan_ref)
            total = sums[distance] if first else jnp.zeros((rank, rows), jnp.float32)
            for at in range(first, last):
                piece = product[(at - first) * rank : (at - first + 1) * rank]
                total = jnp.where(hot == plan_ref[PLANE_LIST * hot_count + at], piece, total)
            sums[distance] = total

    run(0, half)

    @pl.when(plan_ref[SECTIONS * hot_count] > half)
    def _():
        run(half, hot_count)

    for distance in range(PLANE):
        for at in range(PLANE):
            total = sums[distance, at * part : (at + 1) * part]
            high = total.astype(jnp.bfloat16)
            low = (total - high.astype(jnp.float32)).astype(jnp.bfloat16)
            outs[distance][FEW, :, at * rows : (at + 1) * rows] = high
            outs[distance][FEW + 1, :, at * rows : (at + 1) * rows] = low


def finish_kernel(
    hot_count,
    plan_ref,
    base_ref,
    cosine_ref,
    sine_ref,
    slot_ref,
    *refs,
):
    shared = refs[:PLANE]
    more = refs[PLANE : 2 * PLANE]
    out_ref, low_ref, sum_ref, rows_ref = refs[2 * PLANE :]
    _, part, key_width = shared[0].shape
    rows = base_ref.shape[0]
    device = lax.axis_index("seq")
    place = lax.rem(device, PLANE)
    for at in range(PLANE):
        total = jnp.zeros((part, rows), jnp.float32)
        for distance in range(PLANE):
            for term in (FEW, FEW + 1):
                total = total + shared[distance][term, :, at * rows : (at + 1) * rows].astype(
                    jnp.float32
                )
        low_ref[at * part : (at + 1) * part] = total
    hot = hot_lanes(device * rows, rows, hot_count, plan_ref)

    def adapted(held, first_entry, count):
        entries = []
        for at in range(first_entry, first_entry + count):
            listed = plan_ref[DEVICE_LISTS * hot_count + at]
            entry = plan_ref[PLANE_LIST * hot_count + jnp.maximum(listed, 0)]
            entries.append(jnp.where(listed >= 0, entry, -1))
        result = None
        for distance in range(PLANE):
            first = pl.multiple_of((place ^ distance) * part, part)
            piece = low_ref[pl.ds(first, part), :]
            spread_rows = jnp.concatenate(
                [jnp.where(hot == entry, piece, 0.0) for entry in entries], axis=0
            ).astype(jnp.bfloat16)
            product = lax.dot_general(
                spread_rows,
                held[distance][:count].reshape(count * part, key_width),
                (((0,), (0,)), ((), ())),
                preferred_element_type=jnp.float32,
            )
            result = product if result is None else result + product
        return result

    sum_ref[...] = base_ref[...] + adapted(shared, 0, FEW)

    @pl.when(plan_ref[SECTIONS * hot_count + 2] == 0)
    def _():
        sum_ref[...] += adapted(more, FEW, hot_count - FEW)

    projected = sum_ref[...]
    cosine = cosine_ref[...]
    sine = sine_ref[...]
    for head in range(key_width // HEAD):
        columns = slice(head * HEAD, (head + 1) * HEAD)
        values = projected[:, columns]
        turned = values * cosine + pltpu.roll(values, HEAD // 2, 1) * sine
        rows_ref[:, columns] = turned.astype(jnp.bfloat16)
    slots = lax.broadcasted_iota(jnp.int32, (out_ref.shape[0], rows), 0)
    placed = (slots == slot_ref[...]).astype(jnp.bfloat16)
    out_ref[...] = jnp.dot(
        placed, rows_ref[...], preferred_element_type=jnp.float32
    ).astype(jnp.bfloat16)


def turn_tables(positions):
    half_head = HEAD // 2
    frequencies = rope_theta ** (-(jnp.arange(half_head, dtype=jnp.float32) * 2.0) / HEAD)
    angles = positions.astype(jnp.float32)[:, None] * frequencies[None, :]
    cosine = jnp.cos(angles)
    sine = jnp.sin(angles)
    return (
        jnp.concatenate([cosine, cosine], axis=1),
        jnp.concatenate([-sine, sine], axis=1),
    )


def planes_outgoing(
    tokens,
    input_norm_scale,
    key_matrix,
    adapter_down_weight,
    adapter_up_weight,
    lengths,
    prompt_adapter_index,
    active_adapter_ids,
    positions,
    slot_index,
    out_rows,
):
    peer_count = PLANE * PLANES
    rows, width = tokens.shape
    quarter = width // PLANE
    adapter_device, rank, key_width = adapter_up_weight.shape
    part = rank // PLANE
    hot_count = active_adapter_ids.shape[0]
    prompt_index = prompt_adapter_index[:, 0]
    piece = jax.ShapeDtypeStruct((adapter_device, rank + part, quarter), jnp.bfloat16)
    packed = call(
        functools.partial(pack_kernel, quarter),
        [piece] * PLANE,
        [ANY, ANY],
        [ANY] * PLANE,
        [pltpu.SemaphoreType.DMA((2 * PLANE,))],
    )(jnp.swapaxes(adapter_down_weight, 1, 2), adapter_up_weight)
    local = [packed[0]] + [
        swap(packed[distance], distance, peer_count) for distance in range(1, PLANE)
    ]
    plan = call(
        functools.partial(plan_kernel, rows, adapter_device),
        jax.ShapeDtypeStruct((SECTIONS * hot_count + 3 + 2 * lengths.shape[0],), jnp.int32),
        [SMEM] * 3,
        SMEM,
    )(lengths, prompt_index, active_adapter_ids)
    tokens, local[1] = lax.optimization_barrier((tokens, local[1]))
    block = rows // 4
    normed, *columns = pl.pallas_call(
        norm_kernel,
        grid=(4,),
        out_shape=[jax.ShapeDtypeStruct((rows, width), jnp.bfloat16)]
        + [jax.ShapeDtypeStruct((rows, quarter), jnp.bfloat16)] * PLANE,
        in_specs=[
            pl.BlockSpec((block, width), lambda at: (at, 0)),
            pl.BlockSpec((1, width), lambda at: (0, 0)),
        ],
        out_specs=[pl.BlockSpec((block, width), lambda at: (at, 0))]
        + [pl.BlockSpec((block, quarter), lambda at: (at, 0))] * PLANE,
        compiler_params=pltpu.CompilerParams(vmem_limit_bytes=VMEM_LIMIT),
    )(tokens, input_norm_scale.reshape(1, width))
    second = swap(columns[1], 1, peer_count)
    plan, positions, slot_index, second = lax.optimization_barrier(
        (plan, positions, slot_index, second)
    )

    rest = jax.ShapeDtypeStruct((hot_count - FEW, part, key_width), jnp.bfloat16)

    def share(parts):
        return [parts[0]] + [
            swap(parts[distance], distance, peer_count) for distance in range(1, PLANE)
        ]

    def branch(slots):
        def run(plan, third, fourth, *local):
            sends = call(
                functools.partial(select_kernel, slots, hot_count, adapter_device),
                [
                    jax.ShapeDtypeStruct((slot, rank + part, quarter), jnp.bfloat16)
                    for slot in slots
                ],
                [SMEM] + [VMEM] * PLANE,
                [VMEM] * len(slots),
            )(plan, *local)
            *sends, third, fourth = lax.optimization_barrier((*sends, third, fourth))
            arrived = [
                swap(send, (at + 1) * PLANE, peer_count) for at, send in enumerate(sends)
            ]
            third = swap(third, 2, peer_count)
            fourth = swap(fourth, 3, peer_count)
            collected, *more = call(
                functools.partial(collect_kernel, hot_count, adapter_device),
                [jax.ShapeDtypeStruct((hot_count, rank + part, quarter), jnp.bfloat16)]
                + ([] if slots[0] == hot_count else [rest] * PLANE),
                [SMEM] + [VMEM] * (PLANE + PLANES - 1),
                [VMEM] * (1 if slots[0] == hot_count else 1 + PLANE),
            )(plan, *local, *arrived)
            if not more:
                more = share(
                    call(
                        functools.partial(share_kernel, FEW, rank, hot_count),
                        [rest] * PLANE,
                        [SMEM, VMEM],
                        [VMEM] * PLANE,
                    )(plan, collected)
                )
            return (third, fourth, collected, *more)

        return run

    cases = [branch(slots) for slots in SLOT_CASES + ((hot_count,) * (PLANES - 1),)]
    third, fourth, used_rows, *more = lax.switch(
        plan[SECTIONS * hot_count + 1], cases, plan, columns[2], columns[3], *local
    )

    shared = call(
        functools.partial(partial_kernel, rank, hot_count),
        [jax.ShapeDtypeStruct((FEW + 2, part, key_width), jnp.bfloat16)] * PLANE,
        [SMEM] + [VMEM] * (1 + PLANE),
        [VMEM] * PLANE,
        [pltpu.VMEM((PLANE, rank, rows), jnp.float32)],
        flops=2 * hot_count * rank * width * rows,
        bytes_accessed=6 * 1024 * 1024,
    )(plan, used_rows, columns[0], second, third, fourth)
    normed, positions, own = lax.optimization_barrier((normed, positions, shared[0]))
    shared = share([own, *shared[1:]])
    base = jnp.dot(normed, key_matrix, preferred_element_type=jnp.float32)
    cosine, sine = turn_tables(positions)
    return call(
        functools.partial(finish_kernel, hot_count),
        jax.ShapeDtypeStruct((out_rows, key_width), jnp.bfloat16),
        [SMEM] + [VMEM] * (4 + 2 * PLANE),
        VMEM,
        [
            pltpu.VMEM((rank, rows), jnp.float32),
            pltpu.VMEM((rows, key_width), jnp.float32),
            pltpu.VMEM((rows, key_width), jnp.bfloat16),
        ],
        flops=2 * rows * key_width * (hot_count * rank + out_rows),
        bytes_accessed=6 * 1024 * 1024,
    )(
        plan,
        base,
        cosine,
        sine,
        slot_index.reshape(1, rows),
        *shared,
        *more,
    )


def gathered_outgoing(
    tokens,
    input_norm_scale,
    key_matrix,
    adapter_down_weight,
    adapter_up_weight,
    active_adapter_ids,
    positions,
    hot_slots,
    slot_index,
    out_rows,
):
    float_rows = tokens.astype(jnp.float32)
    inverse_rms = lax.rsqrt(jnp.mean(float_rows * float_rows, axis=1, keepdims=True) + norm_eps)
    normed = (float_rows * inverse_rms * input_norm_scale[None, :]).astype(jnp.bfloat16)
    adapter_device = adapter_down_weight.shape[0]
    down_list = []
    up_list = []
    for entry in range(active_adapter_ids.shape[0]):
        adapter = active_adapter_ids[entry]
        for weight, gathered in ((adapter_down_weight, down_list), (adapter_up_weight, up_list)):
            mine = lax.dynamic_index_in_dim(weight, adapter % adapter_device, 0, keepdims=False)
            gathered.append(spread(mine, "seq", adapter // adapter_device))
    down_matrices = jnp.concatenate(down_list, axis=1)
    up_matrices = jnp.concatenate(up_list, axis=0)
    base_proj = jnp.dot(normed, key_matrix, preferred_element_type=jnp.float32)
    low_rank = jnp.dot(normed, down_matrices, preferred_element_type=jnp.float32).astype(
        jnp.bfloat16
    )
    column_owned = (jnp.arange(down_matrices.shape[1], dtype=jnp.int32) // ADAPTER_RANK)[
        None, :
    ] == hot_slots[:, None]
    low_rank = jnp.where(column_owned, low_rank, jnp.zeros_like(low_rank))
    projected = base_proj + jnp.dot(low_rank, up_matrices, preferred_element_type=jnp.float32)
    key_rows = rotate(projected, positions).astype(jnp.bfloat16)
    return jnp.zeros((out_rows, key_rows.shape[1]), jnp.bfloat16).at[slot_index].set(key_rows)


def on_device(
    tokens,
    input_norm_scale,
    key_matrix,
    adapter_down_weight,
    adapter_up_weight,
    lengths,
    prompt_adapter_index,
    active_adapter_ids,
    token_cache_device,
):
    rows_dev = tokens.shape[0]
    peer_count = lax.axis_size("seq")
    slot_count = max(4, 2 * rows_dev // peer_count)
    key_width = key_matrix.shape[1]
    targets = token_cache_device[:, 0]
    row_order = jnp.arange(rows_dev, dtype=jnp.int32)
    earlier = row_order[None, :] < row_order[:, None]
    rank_within = jnp.sum(
        ((targets[:, None] == targets[None, :]) & earlier).astype(jnp.int32), axis=1
    )
    slot_index = targets * slot_count + rank_within
    positions, hot_slots = locate(
        lengths, prompt_adapter_index, lax.axis_index("seq") * rows_dev, rows_dev
    )
    out_rows = peer_count * slot_count
    if peer_count == PLANE * PLANES:
        outgoing = planes_outgoing(
            tokens,
            input_norm_scale,
            key_matrix,
            adapter_down_weight,
            adapter_up_weight,
            lengths,
            prompt_adapter_index,
            active_adapter_ids,
            positions,
            slot_index,
            out_rows,
        )
    else:
        outgoing = gathered_outgoing(
            tokens,
            input_norm_scale,
            key_matrix,
            adapter_down_weight,
            adapter_up_weight,
            active_adapter_ids,
            positions,
            hot_slots,
            slot_index,
            out_rows,
        )
    outgoing = outgoing.reshape(peer_count, slot_count, key_width)
    result = lax.all_to_all(outgoing, "seq", split_axis=0, concat_axis=0, tiled=True)
    return result.reshape(out_rows, key_width)


def solution(mesh):
    in_specs = (
        P(("groups", "seq"), None),
        P(),
        P(),
        P("seq", None, None),
        P("seq", None, None),
        P("groups"),
        P("groups", None),
        P("groups"),
        P(("groups", "seq"), None),
    )
    out_specs = P(("groups", "seq"), None)
    return jax.shard_map(
        on_device, mesh=mesh, in_specs=in_specs, out_specs=out_specs, check_vma=False
    )
```

```python
import functools

import jax
import jax.numpy as jnp
from jax import lax
from jax.experimental import pallas as pl
from jax.experimental.pallas import tpu as pltpu
from jax.sharding import PartitionSpec as P

HEAD = 128
ADAPTER_RANK = 64


rope_theta = 500000.0
norm_eps = 1e-05


def spread(array, axis, root):
    mine = lax.axis_index(axis) == root
    return lax.psum(jnp.where(mine, array, jnp.zeros_like(array)), axis)


def rotate(projected, positions):
    half_head = HEAD // 2
    frequencies = rope_theta ** (-(jnp.arange(half_head, dtype=jnp.float32) * 2.0) / HEAD)
    angles = positions.astype(jnp.float32)[:, None] * frequencies[None, :]
    cosine = jnp.cos(angles)[:, None, :]
    sine_table = jnp.sin(angles)[:, None, :]
    per_head = projected.reshape(projected.shape[0], -1, HEAD)
    first_half = per_head[..., :half_head]
    second_half = per_head[..., half_head:]
    turned = jnp.concatenate(
        [
            first_half * cosine - second_half * sine_table,
            second_half * cosine + first_half * sine_table,
        ],
        axis=-1,
    )
    return turned.reshape(projected.shape)


def locate(lengths, prompt_adapter_index, first_row, row_count):
    prompt_ends = jnp.cumsum(lengths)
    prompt_starts = prompt_ends - lengths
    row_ids = first_row + jnp.arange(row_count, dtype=jnp.int32)
    prompt_ids = jnp.sum((prompt_ends[None, :] <= row_ids[:, None]).astype(jnp.int32), axis=1)
    prompt_match = prompt_ids[:, None] == jnp.arange(lengths.shape[0], dtype=jnp.int32)[None, :]
    prompt_start = jnp.sum(jnp.where(prompt_match, prompt_starts[None, :], 0), axis=1)
    hot_slots = jnp.sum(jnp.where(prompt_match, prompt_adapter_index[:, 0][None, :], 0), axis=1)
    return (row_ids - prompt_start, hot_slots)


PLANE = 4
PLANES = 4
SLOT_CASES = (
    (2, 1, 1),
    (3, 2, 1),
    (3, 1, 2),
    (3, 2, 2),
    (3, 3, 1),
    (3, 1, 3),
    (4, 3, 2),
    (4, 2, 3),
    (4, 4, 1),
    (4, 1, 4),
    (4, 3, 3),
)
FEW = 3
ANY = pl.BlockSpec(memory_space=pl.ANY)
SMEM = pl.BlockSpec(memory_space=pltpu.SMEM)
VMEM = pl.BlockSpec(memory_space=pltpu.VMEM)
VMEM_LIMIT = 40 * 1024 * 1024


def swap(value, distance, peer_count):
    return lax.ppermute(value, "seq", [(i, i ^ distance) for i in range(peer_count)])


def call(kernel, out_shape, in_specs, out_specs, scratch=(), **cost):
    return pl.pallas_call(
        kernel,
        out_shape=out_shape,
        in_specs=in_specs,
        out_specs=out_specs,
        scratch_shapes=list(scratch),
        compiler_params=pltpu.CompilerParams(vmem_limit_bytes=VMEM_LIMIT),
        cost_estimate=pl.CostEstimate(transcendentals=0, **cost) if cost else None,
    )


FROM_KIND, FROM_SLOT, PLANE_LIST, DEVICE_LISTS, SECTIONS = 3, 4, 5, 6, 10


def bit_of(mask, entry):
    return lax.shift_right_logical(mask, entry) & 1


def plan_kernel(rows, adapter_device, length_ref, index_ref, id_ref, plan_ref):
    hot_count = id_ref.shape[0]
    device = lax.axis_index("seq")
    plane = lax.div(device, PLANE)
    place = device - plane * PLANE
    for at in range(FROM_KIND * hot_count):
        plan_ref[at] = 0
    for at in range(PLANE_LIST * hot_count, SECTIONS * hot_count):
        plan_ref[at] = -1
    devices = PLANE * PLANES
    uses = [jnp.int32(0)] * devices
    start = jnp.int32(0)
    for prompt in range(length_ref.shape[0]):
        end = start + length_ref[prompt]
        bit = lax.shift_left(jnp.int32(1), index_ref[prompt])
        plan_ref[SECTIONS * hot_count + 3 + 2 * prompt] = end
        plan_ref[SECTIONS * hot_count + 4 + 2 * prompt] = index_ref[prompt]
        for at in range(devices):
            hit = (start < (at + 1) * rows) & (end > at * rows)
            uses[at] = uses[at] | jnp.where(hit, bit, 0)
        start = end
    need = []
    for at in range(PLANES):
        mask = uses[at * PLANE]
        for inner in range(1, PLANE):
            mask = mask | uses[at * PLANE + inner]
        need.append(mask)

    def pick(masks, which):
        total = masks[0]
        for at in range(1, len(masks)):
            total = jnp.where(which == at, masks[at], total)
        return total

    def list_bits(section, mask, values):
        count = jnp.int32(0)
        for entry in range(hot_count):

            @pl.when(bit_of(mask, entry) == 1)
            def _():
                plan_ref[section * hot_count + count] = values[entry]

            count = count + bit_of(mask, entry)
        return count

    owner_plane = []
    kind = []
    slot = []
    local = []
    for entry in range(hot_count):
        adapter = id_ref[entry]
        owner = lax.div(adapter, adapter_device)
        owner_plane.append(lax.div(owner, PLANE))
        local.append(
            ((owner - owner_plane[entry] * PLANE) ^ place) * adapter_device
            + adapter
            - owner * adapter_device
        )
        kind.append(jnp.int32(0))
        slot.append(local[entry])
    need_here = pick(need, plane)
    for distance in range(1, PLANES):
        other = plane ^ distance
        need_there = pick(need, other)
        sent = jnp.int32(0)
        taken = jnp.int32(0)
        for entry in range(hot_count):
            plan_ref[(distance - 1) * hot_count + sent] = local[entry]
            sent = sent + jnp.where(owner_plane[entry] == plane, bit_of(need_there, entry), 0)
            wanted = jnp.where(owner_plane[entry] == other, bit_of(need_here, entry), 0)
            kind[entry] = jnp.where(wanted == 1, distance, kind[entry])
            slot[entry] = jnp.where(wanted == 1, taken, slot[entry])
            taken = taken + wanted
    for entry in range(hot_count):
        plan_ref[FROM_KIND * hot_count + entry] = kind[entry]
        plan_ref[FROM_SLOT * hot_count + entry] = slot[entry]
    listed = [jnp.int32(0)]
    for entry in range(hot_count):
        listed.append(listed[entry] + bit_of(need_here, entry))
    plan_ref[SECTIONS * hot_count] = list_bits(
        PLANE_LIST, need_here, [jnp.int32(entry) for entry in range(hot_count)]
    )
    for distance in range(PLANE):
        list_bits(DEVICE_LISTS + distance, pick(uses, device ^ distance), listed)
    most = []
    for distance in range(1, PLANES):
        largest = jnp.int32(0)
        for at in range(PLANES):
            count = jnp.int32(0)
            for entry in range(hot_count):
                wanted = bit_of(need[at ^ distance], entry)
                count = count + jnp.where(owner_plane[entry] == at, wanted, 0)
            largest = jnp.maximum(largest, count)
        most.append(largest)
    few = jnp.bool_(True)
    for at in range(devices):
        count = jnp.int32(0)
        for entry in range(hot_count):
            count = count + bit_of(uses[at], entry)
        few = few & (count <= FEW)
    case = jnp.int32(len(SLOT_CASES))
    for at in reversed(range(len(SLOT_CASES))):
        fits = few
        for distance in range(PLANES - 1):
            fits = fits & (most[distance] <= SLOT_CASES[at][distance])
        case = jnp.where(fits, at, case)
    plan_ref[SECTIONS * hot_count + 1] = case
    plan_ref[SECTIONS * hot_count + 2] = jnp.where(few, 1, 0)


def norm_kernel(token_ref, scale_ref, out_ref, *quarter_refs):
    values = token_ref[...].astype(jnp.float32)
    inverse_rms = lax.rsqrt(jnp.mean(values * values, axis=1, keepdims=True) + norm_eps)
    out_ref[...] = (values * inverse_rms * scale_ref[...]).astype(jnp.bfloat16)
    place = lax.rem(lax.axis_index("seq"), PLANE)
    quarter = quarter_refs[0].shape[1]
    for distance in range(PLANE):
        first = pl.multiple_of((place ^ distance) * quarter, quarter)
        quarter_refs[distance][...] = out_ref[:, pl.ds(first, quarter)]


def pack_kernel(quarter, down_ref, up_ref, *refs):
    outs = refs[:PLANE]
    sems = refs[PLANE]
    place = lax.rem(lax.axis_index("seq"), PLANE)
    rank = down_ref.shape[1]
    part = rank // PLANE
    copies = []
    for distance in range(PLANE):
        other = place ^ distance
        columns = pl.ds(pl.multiple_of(other * quarter, quarter), quarter)
        copies.append(
            pltpu.make_async_copy(
                down_ref.at[:, :, columns],
                outs[distance].at[:, pl.ds(0, rank), :],
                sems.at[2 * distance],
            )
        )
        rows = pl.ds(pl.multiple_of(other * part, part), part)
        copies.append(
            pltpu.make_async_copy(
                up_ref.at[:, rows, :],
                outs[distance].at[:, pl.ds(rank, part), :],
                sems.at[2 * distance + 1],
            )
        )
    for copy in copies:
        copy.start()
    for copy in copies:
        copy.wait()


def select_kernel(slots, hot_count, adapter_device, plan_ref, *refs):
    local = refs[:PLANE]
    outs = refs[PLANE:]
    for distance in range(1, PLANES):
        for slot in range(slots[distance - 1]):
            index = plan_ref[(distance - 1) * hot_count + slot]
            holder = lax.div(index, adapter_device)
            inner = index - holder * adapter_device
            for at in range(PLANE):

                @pl.when(holder == at)
                def _():
                    outs[distance - 1][slot] = local[at][inner]


def share_rows(first, count, rank, hot_count, plan_ref, rows_ref, outs):
    for distance in range(PLANE):
        for at in range(count):
            listed = plan_ref[(DEVICE_LISTS + distance) * hot_count + first + at]
            outs[distance][at] = rows_ref[jnp.maximum(listed, 0), rank:, :]


def share_kernel(first, rank, hot_count, plan_ref, rows_ref, *outs):
    share_rows(first, outs[0].shape[0], rank, hot_count, plan_ref, rows_ref, outs)


def collect_kernel(hot_count, adapter_device, plan_ref, *refs):
    local = refs[:PLANE]
    arrived = refs[PLANE : PLANE + PLANES - 1]
    out_ref, sems = refs[PLANE + PLANES - 1], refs[-1]
    used = plan_ref[SECTIONS * hot_count]

    def copy_of(place, source):
        return pltpu.make_async_copy(source, out_ref.at[place], sems.at[place])

    for place in range(hot_count):

        @pl.when(place < used)
        def _():
            entry = plan_ref[PLANE_LIST * hot_count + place]
            kind = plan_ref[FROM_KIND * hot_count + entry]
            slot = plan_ref[FROM_SLOT * hot_count + entry]

            @pl.when(kind == 0)
            def _():
                holder = lax.div(slot, adapter_device)
                inner = slot - holder * adapter_device
                for at in range(PLANE):

                    @pl.when(holder == at)
                    def _():
                        copy_of(place, local[at].at[inner]).start()

            for distance in range(1, PLANES):

                @pl.when(kind == distance)
                def _():
                    copy_of(place, arrived[distance - 1].at[slot]).start()

    for place in range(hot_count):

        @pl.when(place < used)
        def _():
            copy_of(place, local[0].at[0]).wait()


def hot_lanes(first_row, rows, hot_count, plan_ref):
    row_ids = first_row + lax.broadcasted_iota(jnp.int32, (1, rows), 1)
    hot = jnp.zeros((1, rows), jnp.int32)
    start = jnp.int32(0)
    for at in range(SECTIONS * hot_count + 3, plan_ref.shape[0], 2):
        end = plan_ref[at]
        hot = jnp.where((row_ids >= start) & (row_ids < end), plan_ref[at + 1], hot)
        start = end
    return hot


def partial_kernel(rank, hot_count, plan_ref, rows_ref, *refs):
    tokens = refs[:PLANE]
    outs = refs[PLANE : 2 * PLANE]
    sums = refs[2 * PLANE]
    device = lax.axis_index("seq")
    rows = tokens[0].shape[0]
    half = hot_count // 2
    part = rank // PLANE
    share_rows(0, FEW, rank, hot_count, plan_ref, rows_ref, outs)

    def run(first, last):
        down = jnp.concatenate([rows_ref[at, :rank, :] for at in range(first, last)], axis=0).T
        for distance in range(PLANE):
            product = jnp.dot(
                tokens[distance][...], down, preferred_element_type=jnp.float32
            ).T
            hot = hot_lanes((device ^ distance) * rows, rows, hot_count, plan_ref)
            total = sums[distance] if first else jnp.zeros((rank, rows), jnp.float32)
            for at in range(first, last):
                piece = product[(at - first) * rank : (at - first + 1) * rank]
                total = jnp.where(hot == plan_ref[PLANE_LIST * hot_count + at], piece, total)
            sums[distance] = total

    run(0, half)

    @pl.when(plan_ref[SECTIONS * hot_count] > half)
    def _():
        run(half, hot_count)

    for distance in range(PLANE):
        for at in range(PLANE):
            total = sums[distance, at * part : (at + 1) * part]
            high = total.astype(jnp.bfloat16)
            low = (total - high.astype(jnp.float32)).astype(jnp.bfloat16)
            outs[distance][FEW, :, at * rows : (at + 1) * rows] = high
            outs[distance][FEW + 1, :, at * rows : (at + 1) * rows] = low


def finish_kernel(
    hot_count,
    plan_ref,
    base_ref,
    cosine_ref,
    sine_ref,
    slot_ref,
    *refs,
):
    shared = refs[:PLANE]
    more = refs[PLANE : 2 * PLANE]
    out_ref, low_ref, sum_ref, rows_ref, more_ref, sems = refs[2 * PLANE :]
    _, part, key_width = shared[0].shape
    rows = base_ref.shape[0]
    device = lax.axis_index("seq")
    place = lax.rem(device, PLANE)
    for at in range(PLANE):
        total = jnp.zeros((part, rows), jnp.float32)
        for distance in range(PLANE):
            for term in (FEW, FEW + 1):
                total = total + shared[distance][term, :, at * rows : (at + 1) * rows].astype(
                    jnp.float32
                )
        low_ref[at * part : (at + 1) * part] = total
    hot = hot_lanes(device * rows, rows, hot_count, plan_ref)

    def adapted(held, first_entry, count):
        entries = []
        for at in range(first_entry, first_entry + count):
            listed = plan_ref[DEVICE_LISTS * hot_count + at]
            entry = plan_ref[PLANE_LIST * hot_count + jnp.maximum(listed, 0)]
            entries.append(jnp.where(listed >= 0, entry, -1))
        result = None
        for distance in range(PLANE):
            first = pl.multiple_of((place ^ distance) * part, part)
            piece = low_ref[pl.ds(first, part), :]
            spread_rows = jnp.concatenate(
                [jnp.where(hot == entry, piece, 0.0) for entry in entries], axis=0
            ).astype(jnp.bfloat16)
            product = lax.dot_general(
                spread_rows,
                held[distance][:count].reshape(count * part, key_width),
                (((0,), (0,)), ((), ())),
                preferred_element_type=jnp.float32,
            )
            result = product if result is None else result + product
        return result

    sum_ref[...] = base_ref[...] + adapted(shared, 0, FEW)

    @pl.when(plan_ref[SECTIONS * hot_count + 2] == 0)
    def _():
        copies = [
            pltpu.make_async_copy(more[at], more_ref.at[at], sems.at[at]) for at in range(PLANE)
        ]
        for copy in copies:
            copy.start()
        for copy in copies:
            copy.wait()
        sum_ref[...] += adapted(
            [more_ref.at[at] for at in range(PLANE)], FEW, hot_count - FEW
        )

    projected = sum_ref[...]
    cosine = cosine_ref[...]
    sine = sine_ref[...]
    for head in range(key_width // HEAD):
        columns = slice(head * HEAD, (head + 1) * HEAD)
        values = projected[:, columns]
        turned = values * cosine + pltpu.roll(values, HEAD // 2, 1) * sine
        rows_ref[:, columns] = turned.astype(jnp.bfloat16)
    slots = lax.broadcasted_iota(jnp.int32, (out_ref.shape[0], rows), 0)
    placed = (slots == slot_ref[...]).astype(jnp.bfloat16)
    out_ref[...] = jnp.dot(
        placed, rows_ref[...], preferred_element_type=jnp.float32
    ).astype(jnp.bfloat16)


def turn_tables(positions):
    half_head = HEAD // 2
    frequencies = rope_theta ** (-(jnp.arange(half_head, dtype=jnp.float32) * 2.0) / HEAD)
    angles = positions.astype(jnp.float32)[:, None] * frequencies[None, :]
    cosine = jnp.cos(angles)
    sine = jnp.sin(angles)
    return (
        jnp.concatenate([cosine, cosine], axis=1),
        jnp.concatenate([-sine, sine], axis=1),
    )


def planes_outgoing(
    tokens,
    input_norm_scale,
    key_matrix,
    adapter_down_weight,
    adapter_up_weight,
    lengths,
    prompt_adapter_index,
    active_adapter_ids,
    positions,
    slot_index,
    out_rows,
):
    peer_count = PLANE * PLANES
    rows, width = tokens.shape
    quarter = width // PLANE
    adapter_device, rank, key_width = adapter_up_weight.shape
    part = rank // PLANE
    hot_count = active_adapter_ids.shape[0]
    prompt_index = prompt_adapter_index[:, 0]
    piece = jax.ShapeDtypeStruct((adapter_device, rank + part, quarter), jnp.bfloat16)
    packed = call(
        functools.partial(pack_kernel, quarter),
        [piece] * PLANE,
        [ANY, ANY],
        [ANY] * PLANE,
        [pltpu.SemaphoreType.DMA((2 * PLANE,))],
    )(jnp.swapaxes(adapter_down_weight, 1, 2), adapter_up_weight)
    local = [packed[0]] + [
        swap(packed[distance], distance, peer_count) for distance in range(1, PLANE)
    ]
    plan = call(
        functools.partial(plan_kernel, rows, adapter_device),
        jax.ShapeDtypeStruct((SECTIONS * hot_count + 3 + 2 * lengths.shape[0],), jnp.int32),
        [SMEM] * 3,
        SMEM,
    )(lengths, prompt_index, active_adapter_ids)
    tokens, local[1] = lax.optimization_barrier((tokens, local[1]))
    block = rows // 4
    normed, *columns = pl.pallas_call(
        norm_kernel,
        grid=(4,),
        out_shape=[jax.ShapeDtypeStruct((rows, width), jnp.bfloat16)]
        + [jax.ShapeDtypeStruct((rows, quarter), jnp.bfloat16)] * PLANE,
        in_specs=[
            pl.BlockSpec((block, width), lambda at: (at, 0)),
            pl.BlockSpec((1, width), lambda at: (0, 0)),
        ],
        out_specs=[pl.BlockSpec((block, width), lambda at: (at, 0))]
        + [pl.BlockSpec((block, quarter), lambda at: (at, 0))] * PLANE,
        compiler_params=pltpu.CompilerParams(vmem_limit_bytes=VMEM_LIMIT),
    )(tokens, input_norm_scale.reshape(1, width))
    second = swap(columns[1], 1, peer_count)
    plan, positions, slot_index, second = lax.optimization_barrier(
        (plan, positions, slot_index, second)
    )

    rest = jax.ShapeDtypeStruct((hot_count - FEW, part, key_width), jnp.bfloat16)

    def share(parts):
        return [parts[0]] + [
            swap(parts[distance], distance, peer_count) for distance in range(1, PLANE)
        ]

    def branch(slots):
        def run(plan, third, fourth, *local):
            sends = call(
                functools.partial(select_kernel, slots, hot_count, adapter_device),
                [
                    jax.ShapeDtypeStruct((slot, rank + part, quarter), jnp.bfloat16)
                    for slot in slots
                ],
                [SMEM] + [VMEM] * PLANE,
                [VMEM] * len(slots),
            )(plan, *local)
            *sends, third, fourth = lax.optimization_barrier((*sends, third, fourth))
            if sum(slots) > 4:
                third = swap(third, 2, peer_count)
                fourth = swap(fourth, 3, peer_count)
            arrived = [
                swap(send, (at + 1) * PLANE, peer_count) for at, send in enumerate(sends)
            ]
            if sum(slots) <= 4:
                third = swap(third, 2, peer_count)
                fourth = swap(fourth, 3, peer_count)
            collected, *more = call(
                functools.partial(collect_kernel, hot_count, adapter_device),
                [jax.ShapeDtypeStruct((hot_count, rank + part, quarter), jnp.bfloat16)]
                + ([] if slots[0] == hot_count else [rest] * PLANE),
                [SMEM] + [ANY] * (PLANE + PLANES - 1),
                [VMEM] + [ANY] * (0 if slots[0] == hot_count else PLANE),
                [pltpu.SemaphoreType.DMA((hot_count,))],
            )(plan, *local, *arrived)
            if not more:
                more = share(
                    call(
                        functools.partial(share_kernel, FEW, rank, hot_count),
                        [rest] * PLANE,
                        [SMEM, VMEM],
                        [VMEM] * PLANE,
                    )(plan, collected)
                )
            return (third, fourth, collected, *more)

        return run

    cases = [branch(slots) for slots in SLOT_CASES + ((hot_count,) * (PLANES - 1),)]
    third, fourth, used_rows, *more = lax.switch(
        plan[SECTIONS * hot_count + 1], cases, plan, columns[2], columns[3], *local
    )

    shared = call(
        functools.partial(partial_kernel, rank, hot_count),
        [jax.ShapeDtypeStruct((FEW + 2, part, key_width), jnp.bfloat16)] * PLANE,
        [SMEM] + [VMEM] * (1 + PLANE),
        [VMEM] * PLANE,
        [pltpu.VMEM((PLANE, rank, rows), jnp.float32)],
        flops=2 * hot_count * rank * width * rows,
        bytes_accessed=6 * 1024 * 1024,
    )(plan, used_rows, columns[0], second, third, fourth)
    normed, positions, own = lax.optimization_barrier((normed, positions, shared[0]))
    shared = share([own, *shared[1:]])
    base = jnp.dot(normed, key_matrix, preferred_element_type=jnp.float32)
    cosine, sine = turn_tables(positions)
    return call(
        functools.partial(finish_kernel, hot_count),
        jax.ShapeDtypeStruct((out_rows, key_width), jnp.bfloat16),
        [SMEM] + [VMEM] * (4 + PLANE) + [ANY] * PLANE,
        VMEM,
        [
            pltpu.VMEM((rank, rows), jnp.float32),
            pltpu.VMEM((rows, key_width), jnp.float32),
            pltpu.VMEM((rows, key_width), jnp.bfloat16),
            pltpu.VMEM((PLANE, *rest.shape), jnp.bfloat16),
            pltpu.SemaphoreType.DMA((PLANE,)),
        ],
        flops=2 * rows * key_width * (hot_count * rank + out_rows),
        bytes_accessed=6 * 1024 * 1024,
    )(
        plan,
        base,
        cosine,
        sine,
        slot_index.reshape(1, rows),
        *shared,
        *more,
    )


def gathered_outgoing(
    tokens,
    input_norm_scale,
    key_matrix,
    adapter_down_weight,
    adapter_up_weight,
    active_adapter_ids,
    positions,
    hot_slots,
    slot_index,
    out_rows,
):
    float_rows = tokens.astype(jnp.float32)
    inverse_rms = lax.rsqrt(jnp.mean(float_rows * float_rows, axis=1, keepdims=True) + norm_eps)
    normed = (float_rows * inverse_rms * input_norm_scale[None, :]).astype(jnp.bfloat16)
    adapter_device = adapter_down_weight.shape[0]
    down_list = []
    up_list = []
    for entry in range(active_adapter_ids.shape[0]):
        adapter = active_adapter_ids[entry]
        for weight, gathered in ((adapter_down_weight, down_list), (adapter_up_weight, up_list)):
            mine = lax.dynamic_index_in_dim(weight, adapter % adapter_device, 0, keepdims=False)
            gathered.append(spread(mine, "seq", adapter // adapter_device))
    down_matrices = jnp.concatenate(down_list, axis=1)
    up_matrices = jnp.concatenate(up_list, axis=0)
    base_proj = jnp.dot(normed, key_matrix, preferred_element_type=jnp.float32)
    low_rank = jnp.dot(normed, down_matrices, preferred_element_type=jnp.float32).astype(
        jnp.bfloat16
    )
    column_owned = (jnp.arange(down_matrices.shape[1], dtype=jnp.int32) // ADAPTER_RANK)[
        None, :
    ] == hot_slots[:, None]
    low_rank = jnp.where(column_owned, low_rank, jnp.zeros_like(low_rank))
    projected = base_proj + jnp.dot(low_rank, up_matrices, preferred_element_type=jnp.float32)
    key_rows = rotate(projected, positions).astype(jnp.bfloat16)
    return jnp.zeros((out_rows, key_rows.shape[1]), jnp.bfloat16).at[slot_index].set(key_rows)


def on_device(
    tokens,
    input_norm_scale,
    key_matrix,
    adapter_down_weight,
    adapter_up_weight,
    lengths,
    prompt_adapter_index,
    active_adapter_ids,
    token_cache_device,
):
    rows_dev = tokens.shape[0]
    peer_count = lax.axis_size("seq")
    slot_count = max(4, 2 * rows_dev // peer_count)
    key_width = key_matrix.shape[1]
    targets = token_cache_device[:, 0]
    row_order = jnp.arange(rows_dev, dtype=jnp.int32)
    earlier = row_order[None, :] < row_order[:, None]
    rank_within = jnp.sum(
        ((targets[:, None] == targets[None, :]) & earlier).astype(jnp.int32), axis=1
    )
    slot_index = targets * slot_count + rank_within
    positions, hot_slots = locate(
        lengths, prompt_adapter_index, lax.axis_index("seq") * rows_dev, rows_dev
    )
    out_rows = peer_count * slot_count
    if peer_count == PLANE * PLANES:
        outgoing = planes_outgoing(
            tokens,
            input_norm_scale,
            key_matrix,
            adapter_down_weight,
            adapter_up_weight,
            lengths,
            prompt_adapter_index,
            active_adapter_ids,
            positions,
            slot_index,
            out_rows,
        )
    else:
        outgoing = gathered_outgoing(
            tokens,
            input_norm_scale,
            key_matrix,
            adapter_down_weight,
            adapter_up_weight,
            active_adapter_ids,
            positions,
            hot_slots,
            slot_index,
            out_rows,
        )
    outgoing = outgoing.reshape(peer_count, slot_count, key_width)
    result = lax.all_to_all(outgoing, "seq", split_axis=0, concat_axis=0, tiled=True)
    return result.reshape(out_rows, key_width)


def solution(mesh):
    in_specs = (
        P(("groups", "seq"), None),
        P(),
        P(),
        P("seq", None, None),
        P("seq", None, None),
        P("groups"),
        P("groups", None),
        P("groups"),
        P(("groups", "seq"), None),
    )
    out_specs = P(("groups", "seq"), None)
    return jax.shard_map(
        on_device, mesh=mesh, in_specs=in_specs, out_specs=out_specs, check_vma=False
    )
```

```python
import functools

import jax
import jax.numpy as jnp
from jax import lax
from jax.experimental import pallas as pl
from jax.experimental.pallas import tpu as pltpu
from jax.sharding import PartitionSpec as P

HEAD = 128
ADAPTER_RANK = 64


rope_theta = 500000.0
norm_eps = 1e-05


def spread(array, axis, root):
    mine = lax.axis_index(axis) == root
    return lax.psum(jnp.where(mine, array, jnp.zeros_like(array)), axis)


def rotate(projected, positions):
    half_head = HEAD // 2
    frequencies = rope_theta ** (-(jnp.arange(half_head, dtype=jnp.float32) * 2.0) / HEAD)
    angles = positions.astype(jnp.float32)[:, None] * frequencies[None, :]
    cosine = jnp.cos(angles)[:, None, :]
    sine_table = jnp.sin(angles)[:, None, :]
    per_head = projected.reshape(projected.shape[0], -1, HEAD)
    first_half = per_head[..., :half_head]
    second_half = per_head[..., half_head:]
    turned = jnp.concatenate(
        [
            first_half * cosine - second_half * sine_table,
            second_half * cosine + first_half * sine_table,
        ],
        axis=-1,
    )
    return turned.reshape(projected.shape)


def locate(lengths, prompt_adapter_index, first_row, row_count):
    prompt_ends = jnp.cumsum(lengths)
    prompt_starts = prompt_ends - lengths
    row_ids = first_row + jnp.arange(row_count, dtype=jnp.int32)
    prompt_ids = jnp.sum((prompt_ends[None, :] <= row_ids[:, None]).astype(jnp.int32), axis=1)
    prompt_match = prompt_ids[:, None] == jnp.arange(lengths.shape[0], dtype=jnp.int32)[None, :]
    prompt_start = jnp.sum(jnp.where(prompt_match, prompt_starts[None, :], 0), axis=1)
    hot_slots = jnp.sum(jnp.where(prompt_match, prompt_adapter_index[:, 0][None, :], 0), axis=1)
    return (row_ids - prompt_start, hot_slots)


PLANE = 4
PLANES = 4
SLOT_CASES = (
    (2, 1, 1),
    (3, 2, 1),
    (3, 1, 2),
    (3, 2, 2),
    (3, 3, 1),
    (3, 1, 3),
    (4, 3, 2),
    (4, 2, 3),
    (4, 4, 1),
    (4, 1, 4),
    (4, 3, 3),
)
FEW = 3
ANY = pl.BlockSpec(memory_space=pl.ANY)
SMEM = pl.BlockSpec(memory_space=pltpu.SMEM)
VMEM = pl.BlockSpec(memory_space=pltpu.VMEM)
VMEM_LIMIT = 40 * 1024 * 1024


def swap(value, distance, peer_count):
    return lax.ppermute(value, "seq", [(i, i ^ distance) for i in range(peer_count)])


def call(kernel, out_shape, in_specs, out_specs, scratch=(), **cost):
    return pl.pallas_call(
        kernel,
        out_shape=out_shape,
        in_specs=in_specs,
        out_specs=out_specs,
        scratch_shapes=list(scratch),
        compiler_params=pltpu.CompilerParams(vmem_limit_bytes=VMEM_LIMIT),
        cost_estimate=pl.CostEstimate(transcendentals=0, **cost) if cost else None,
    )


FROM_KIND, FROM_SLOT, PLANE_LIST, DEVICE_LISTS, SECTIONS = 3, 4, 5, 6, 10


def bit_of(mask, entry):
    return lax.shift_right_logical(mask, entry) & 1


def plan_kernel(rows, adapter_device, length_ref, index_ref, id_ref, plan_ref):
    hot_count = id_ref.shape[0]
    device = lax.axis_index("seq")
    plane = lax.div(device, PLANE)
    place = device - plane * PLANE
    for at in range(FROM_KIND * hot_count):
        plan_ref[at] = 0
    for at in range(PLANE_LIST * hot_count, SECTIONS * hot_count):
        plan_ref[at] = -1
    devices = PLANE * PLANES
    uses = [jnp.int32(0)] * devices
    start = jnp.int32(0)
    for prompt in range(length_ref.shape[0]):
        end = start + length_ref[prompt]
        bit = lax.shift_left(jnp.int32(1), index_ref[prompt])
        plan_ref[SECTIONS * hot_count + 3 + 2 * prompt] = end
        plan_ref[SECTIONS * hot_count + 4 + 2 * prompt] = index_ref[prompt]
        for at in range(devices):
            hit = (start < (at + 1) * rows) & (end > at * rows)
            uses[at] = uses[at] | jnp.where(hit, bit, 0)
        start = end
    need = []
    for at in range(PLANES):
        mask = uses[at * PLANE]
        for inner in range(1, PLANE):
            mask = mask | uses[at * PLANE + inner]
        need.append(mask)

    def pick(masks, which):
        total = masks[0]
        for at in range(1, len(masks)):
            total = jnp.where(which == at, masks[at], total)
        return total

    def list_bits(section, mask, values):
        count = jnp.int32(0)
        for entry in range(hot_count):

            @pl.when(bit_of(mask, entry) == 1)
            def _():
                plan_ref[section * hot_count + count] = values[entry]

            count = count + bit_of(mask, entry)
        return count

    owner_plane = []
    kind = []
    slot = []
    local = []
    for entry in range(hot_count):
        adapter = id_ref[entry]
        owner = lax.div(adapter, adapter_device)
        owner_plane.append(lax.div(owner, PLANE))
        local.append(
            ((owner - owner_plane[entry] * PLANE) ^ place) * adapter_device
            + adapter
            - owner * adapter_device
        )
        kind.append(jnp.int32(0))
        slot.append(local[entry])
    need_here = pick(need, plane)
    for distance in range(1, PLANES):
        other = plane ^ distance
        need_there = pick(need, other)
        sent = jnp.int32(0)
        taken = jnp.int32(0)
        for entry in range(hot_count):
            plan_ref[(distance - 1) * hot_count + sent] = local[entry]
            sent = sent + jnp.where(owner_plane[entry] == plane, bit_of(need_there, entry), 0)
            wanted = jnp.where(owner_plane[entry] == other, bit_of(need_here, entry), 0)
            kind[entry] = jnp.where(wanted == 1, distance, kind[entry])
            slot[entry] = jnp.where(wanted == 1, taken, slot[entry])
            taken = taken + wanted
    for entry in range(hot_count):
        plan_ref[FROM_KIND * hot_count + entry] = kind[entry]
        plan_ref[FROM_SLOT * hot_count + entry] = slot[entry]
    listed = [jnp.int32(0)]
    for entry in range(hot_count):
        listed.append(listed[entry] + bit_of(need_here, entry))
    plan_ref[SECTIONS * hot_count] = list_bits(
        PLANE_LIST, need_here, [jnp.int32(entry) for entry in range(hot_count)]
    )
    for distance in range(PLANE):
        list_bits(DEVICE_LISTS + distance, pick(uses, device ^ distance), listed)
    most = []
    for distance in range(1, PLANES):
        largest = jnp.int32(0)
        for at in range(PLANES):
            count = jnp.int32(0)
            for entry in range(hot_count):
                wanted = bit_of(need[at ^ distance], entry)
                count = count + jnp.where(owner_plane[entry] == at, wanted, 0)
            largest = jnp.maximum(largest, count)
        most.append(largest)
    few = jnp.bool_(True)
    for at in range(devices):
        count = jnp.int32(0)
        for entry in range(hot_count):
            count = count + bit_of(uses[at], entry)
        few = few & (count <= FEW)
    case = jnp.int32(len(SLOT_CASES))
    for at in reversed(range(len(SLOT_CASES))):
        fits = few
        for distance in range(PLANES - 1):
            fits = fits & (most[distance] <= SLOT_CASES[at][distance])
        case = jnp.where(fits, at, case)
    plan_ref[SECTIONS * hot_count + 1] = case
    plan_ref[SECTIONS * hot_count + 2] = jnp.where(few, 1, 0)


def norm_kernel(token_ref, scale_ref, out_ref, *quarter_refs):
    values = token_ref[...].astype(jnp.float32)
    inverse_rms = lax.rsqrt(jnp.mean(values * values, axis=1, keepdims=True) + norm_eps)
    out_ref[...] = (values * inverse_rms * scale_ref[...]).astype(jnp.bfloat16)
    place = lax.rem(lax.axis_index("seq"), PLANE)
    quarter = quarter_refs[0].shape[1]
    for distance in range(PLANE):
        first = pl.multiple_of((place ^ distance) * quarter, quarter)
        quarter_refs[distance][...] = out_ref[:, pl.ds(first, quarter)]


def pack_kernel(quarter, down_ref, up_ref, *refs):
    outs = refs[:PLANE]
    sems = refs[PLANE]
    place = lax.rem(lax.axis_index("seq"), PLANE)
    rank = down_ref.shape[1]
    part = rank // PLANE
    copies = []
    for distance in range(PLANE):
        other = place ^ distance
        columns = pl.ds(pl.multiple_of(other * quarter, quarter), quarter)
        copies.append(
            pltpu.make_async_copy(
                down_ref.at[:, :, columns],
                outs[distance].at[:, pl.ds(0, rank), :],
                sems.at[2 * distance],
            )
        )
        rows = pl.ds(pl.multiple_of(other * part, part), part)
        copies.append(
            pltpu.make_async_copy(
                up_ref.at[:, rows, :],
                outs[distance].at[:, pl.ds(rank, part), :],
                sems.at[2 * distance + 1],
            )
        )
    for copy in copies:
        copy.start()
    for copy in copies:
        copy.wait()


def select_kernel(slots, hot_count, adapter_device, plan_ref, *refs):
    local = refs[:PLANE]
    outs = refs[PLANE:]
    for distance in range(1, PLANES):
        for slot in range(slots[distance - 1]):
            index = plan_ref[(distance - 1) * hot_count + slot]
            holder = lax.div(index, adapter_device)
            inner = index - holder * adapter_device
            for at in range(PLANE):

                @pl.when(holder == at)
                def _():
                    outs[distance - 1][slot] = local[at][inner]


def share_rows(first, count, rank, hot_count, plan_ref, rows_ref, outs):
    for distance in range(PLANE):
        for at in range(count):
            listed = plan_ref[(DEVICE_LISTS + distance) * hot_count + first + at]
            outs[distance][at] = rows_ref[jnp.maximum(listed, 0), rank:, :]


def share_kernel(first, rank, hot_count, plan_ref, rows_ref, *outs):
    share_rows(first, outs[0].shape[0], rank, hot_count, plan_ref, rows_ref, outs)


def collect_kernel(hot_count, adapter_device, plan_ref, *refs):
    local = refs[:PLANE]
    arrived = refs[PLANE : PLANE + PLANES - 1]
    out_ref, sems = refs[PLANE + PLANES - 1], refs[-1]
    used = plan_ref[SECTIONS * hot_count]

    def copy_of(place, source):
        return pltpu.make_async_copy(source, out_ref.at[place], sems.at[place])

    for place in range(hot_count):

        @pl.when(place < used)
        def _():
            entry = plan_ref[PLANE_LIST * hot_count + place]
            kind = plan_ref[FROM_KIND * hot_count + entry]
            slot = plan_ref[FROM_SLOT * hot_count + entry]

            @pl.when(kind == 0)
            def _():
                holder = lax.div(slot, adapter_device)
                inner = slot - holder * adapter_device
                for at in range(PLANE):

                    @pl.when(holder == at)
                    def _():
                        copy_of(place, local[at].at[inner]).start()

            for distance in range(1, PLANES):

                @pl.when(kind == distance)
                def _():
                    copy_of(place, arrived[distance - 1].at[slot]).start()

    for place in range(hot_count):

        @pl.when(place < used)
        def _():
            copy_of(place, local[0].at[0]).wait()


def hot_lanes(first_row, rows, hot_count, plan_ref):
    row_ids = first_row + lax.broadcasted_iota(jnp.int32, (1, rows), 1)
    hot = jnp.zeros((1, rows), jnp.int32)
    start = jnp.int32(0)
    for at in range(SECTIONS * hot_count + 3, plan_ref.shape[0], 2):
        end = plan_ref[at]
        hot = jnp.where((row_ids >= start) & (row_ids < end), plan_ref[at + 1], hot)
        start = end
    return hot


def partial_kernel(rank, hot_count, plan_ref, rows_ref, *refs):
    tokens = refs[:PLANE]
    outs = refs[PLANE : 2 * PLANE]
    sums = refs[2 * PLANE]
    device = lax.axis_index("seq")
    rows = tokens[0].shape[0]
    half = hot_count // 2
    part = rank // PLANE
    share_rows(0, FEW, rank, hot_count, plan_ref, rows_ref, outs)

    def run(first, last):
        down = jnp.concatenate([rows_ref[at, :rank, :] for at in range(first, last)], axis=0).T
        for distance in range(PLANE):
            product = jnp.dot(
                tokens[distance][...], down, preferred_element_type=jnp.float32
            ).T
            hot = hot_lanes((device ^ distance) * rows, rows, hot_count, plan_ref)
            total = sums[distance] if first else jnp.zeros((rank, rows), jnp.float32)
            for at in range(first, last):
                piece = product[(at - first) * rank : (at - first + 1) * rank]
                total = jnp.where(hot == plan_ref[PLANE_LIST * hot_count + at], piece, total)
            sums[distance] = total

    run(0, half)

    @pl.when(plan_ref[SECTIONS * hot_count] > half)
    def _():
        run(half, hot_count)

    for distance in range(PLANE):
        for at in range(PLANE):
            total = sums[distance, at * part : (at + 1) * part]
            high = total.astype(jnp.bfloat16)
            low = (total - high.astype(jnp.float32)).astype(jnp.bfloat16)
            outs[distance][FEW, :, at * rows : (at + 1) * rows] = high
            outs[distance][FEW + 1, :, at * rows : (at + 1) * rows] = low


def finish_kernel(
    hot_count,
    plan_ref,
    base_ref,
    cosine_ref,
    sine_ref,
    slot_ref,
    *refs,
):
    shared = refs[:PLANE]
    more = refs[PLANE : 2 * PLANE]
    out_ref, low_ref, sum_ref, rows_ref, more_ref, sems = refs[2 * PLANE :]
    _, part, key_width = shared[0].shape
    rows = base_ref.shape[0]
    device = lax.axis_index("seq")
    place = lax.rem(device, PLANE)
    for at in range(PLANE):
        total = jnp.zeros((part, rows), jnp.float32)
        for distance in range(PLANE):
            for term in (FEW, FEW + 1):
                total = total + shared[distance][term, :, at * rows : (at + 1) * rows].astype(
                    jnp.float32
                )
        low_ref[at * part : (at + 1) * part] = total
    hot = hot_lanes(device * rows, rows, hot_count, plan_ref)

    def adapted(held, first_entry, count):
        entries = []
        for at in range(first_entry, first_entry + count):
            listed = plan_ref[DEVICE_LISTS * hot_count + at]
            entry = plan_ref[PLANE_LIST * hot_count + jnp.maximum(listed, 0)]
            entries.append(jnp.where(listed >= 0, entry, -1))
        result = None
        for distance in range(PLANE):
            first = pl.multiple_of((place ^ distance) * part, part)
            piece = low_ref[pl.ds(first, part), :]
            spread_rows = jnp.concatenate(
                [jnp.where(hot == entry, piece, 0.0) for entry in entries], axis=0
            ).astype(jnp.bfloat16)
            product = lax.dot_general(
                spread_rows,
                held[distance][:count].reshape(count * part, key_width),
                (((0,), (0,)), ((), ())),
                preferred_element_type=jnp.float32,
            )
            result = product if result is None else result + product
        return result

    sum_ref[...] = base_ref[...] + adapted(shared, 0, FEW)

    @pl.when(plan_ref[SECTIONS * hot_count + 2] == 0)
    def _():
        copies = [
            pltpu.make_async_copy(more[at], more_ref.at[at], sems.at[at]) for at in range(PLANE)
        ]
        for copy in copies:
            copy.start()
        for copy in copies:
            copy.wait()
        sum_ref[...] += adapted(
            [more_ref.at[at] for at in range(PLANE)], FEW, hot_count - FEW
        )

    projected = sum_ref[...]
    cosine = cosine_ref[...]
    sine = sine_ref[...]
    for head in range(key_width // HEAD):
        columns = slice(head * HEAD, (head + 1) * HEAD)
        values = projected[:, columns]
        turned = values * cosine + pltpu.roll(values, HEAD // 2, 1) * sine
        rows_ref[:, columns] = turned.astype(jnp.bfloat16)
    slots = lax.broadcasted_iota(jnp.int32, (out_ref.shape[0], rows), 0)
    placed = (slots == slot_ref[...]).astype(jnp.bfloat16)
    out_ref[...] = jnp.dot(
        placed, rows_ref[...], preferred_element_type=jnp.float32
    ).astype(jnp.bfloat16)


def turn_tables(positions):
    half_head = HEAD // 2
    frequencies = rope_theta ** (-(jnp.arange(half_head, dtype=jnp.float32) * 2.0) / HEAD)
    angles = positions.astype(jnp.float32)[:, None] * frequencies[None, :]
    cosine = jnp.cos(angles)
    sine = jnp.sin(angles)
    return (
        jnp.concatenate([cosine, cosine], axis=1),
        jnp.concatenate([-sine, sine], axis=1),
    )


def planes_outgoing(
    tokens,
    input_norm_scale,
    key_matrix,
    adapter_down_weight,
    adapter_up_weight,
    lengths,
    prompt_adapter_index,
    active_adapter_ids,
    positions,
    slot_index,
    out_rows,
):
    peer_count = PLANE * PLANES
    rows, width = tokens.shape
    quarter = width // PLANE
    adapter_device, rank, key_width = adapter_up_weight.shape
    part = rank // PLANE
    hot_count = active_adapter_ids.shape[0]
    prompt_index = prompt_adapter_index[:, 0]
    piece = jax.ShapeDtypeStruct((adapter_device, rank + part, quarter), jnp.bfloat16)
    packed = call(
        functools.partial(pack_kernel, quarter),
        [piece] * PLANE,
        [ANY, ANY],
        [ANY] * PLANE,
        [pltpu.SemaphoreType.DMA((2 * PLANE,))],
    )(jnp.swapaxes(adapter_down_weight, 1, 2), adapter_up_weight)
    local = [packed[0]] + [
        swap(packed[distance], distance, peer_count) for distance in range(1, PLANE)
    ]
    plan = call(
        functools.partial(plan_kernel, rows, adapter_device),
        jax.ShapeDtypeStruct((SECTIONS * hot_count + 3 + 2 * lengths.shape[0],), jnp.int32),
        [SMEM] * 3,
        SMEM,
    )(lengths, prompt_index, active_adapter_ids)
    tokens, local[1] = lax.optimization_barrier((tokens, local[1]))
    block = rows // 4
    normed, *columns = pl.pallas_call(
        norm_kernel,
        grid=(4,),
        out_shape=[jax.ShapeDtypeStruct((rows, width), jnp.bfloat16)]
        + [jax.ShapeDtypeStruct((rows, quarter), jnp.bfloat16)] * PLANE,
        in_specs=[
            pl.BlockSpec((block, width), lambda at: (at, 0)),
            pl.BlockSpec((1, width), lambda at: (0, 0)),
        ],
        out_specs=[pl.BlockSpec((block, width), lambda at: (at, 0))]
        + [pl.BlockSpec((block, quarter), lambda at: (at, 0))] * PLANE,
        compiler_params=pltpu.CompilerParams(vmem_limit_bytes=VMEM_LIMIT),
    )(tokens, input_norm_scale.reshape(1, width))
    second = swap(columns[1], 1, peer_count)
    plan, positions, slot_index, second = lax.optimization_barrier(
        (plan, positions, slot_index, second)
    )

    rest = jax.ShapeDtypeStruct((hot_count - FEW, part, key_width), jnp.bfloat16)

    def share(parts):
        return [parts[0]] + [
            swap(parts[distance], distance, peer_count) for distance in range(1, PLANE)
        ]

    def branch(slots):
        def run(plan, third, fourth, *local):
            sends = call(
                functools.partial(select_kernel, slots, hot_count, adapter_device),
                [
                    jax.ShapeDtypeStruct((slot, rank + part, quarter), jnp.bfloat16)
                    for slot in slots
                ],
                [SMEM] + [VMEM] * PLANE,
                [VMEM] * len(slots),
            )(plan, *local)
            arrived = [
                swap(send, (at + 1) * PLANE, peer_count) for at, send in enumerate(sends)
            ]
            third = swap(third, 2, peer_count)
            fourth = swap(fourth, 3, peer_count)
            collected, *more = call(
                functools.partial(collect_kernel, hot_count, adapter_device),
                [jax.ShapeDtypeStruct((hot_count, rank + part, quarter), jnp.bfloat16)]
                + ([] if slots[0] == hot_count else [rest] * PLANE),
                [SMEM] + [ANY] * (PLANE + PLANES - 1),
                [VMEM] + [ANY] * (0 if slots[0] == hot_count else PLANE),
                [pltpu.SemaphoreType.DMA((hot_count,))],
            )(plan, *local, *arrived)
            if not more:
                more = share(
                    call(
                        functools.partial(share_kernel, FEW, rank, hot_count),
                        [rest] * PLANE,
                        [SMEM, VMEM],
                        [VMEM] * PLANE,
                    )(plan, collected)
                )
            return (third, fourth, collected, *more)

        return run

    cases = [branch(slots) for slots in SLOT_CASES + ((hot_count,) * (PLANES - 1),)]
    third, fourth, used_rows, *more = lax.switch(
        plan[SECTIONS * hot_count + 1], cases, plan, columns[2], columns[3], *local
    )

    shared = call(
        functools.partial(partial_kernel, rank, hot_count),
        [jax.ShapeDtypeStruct((FEW + 2, part, key_width), jnp.bfloat16)] * PLANE,
        [SMEM] + [VMEM] * (1 + PLANE),
        [VMEM] * PLANE,
        [pltpu.VMEM((PLANE, rank, rows), jnp.float32)],
        flops=2 * hot_count * rank * width * rows,
        bytes_accessed=6 * 1024 * 1024,
    )(plan, used_rows, columns[0], second, third, fourth)
    normed, positions, own = lax.optimization_barrier((normed, positions, shared[0]))
    shared = share([own, *shared[1:]])
    base = jnp.dot(normed, key_matrix, preferred_element_type=jnp.float32)
    cosine, sine = turn_tables(positions)
    return call(
        functools.partial(finish_kernel, hot_count),
        jax.ShapeDtypeStruct((out_rows, key_width), jnp.bfloat16),
        [SMEM] + [VMEM] * (4 + PLANE) + [ANY] * PLANE,
        VMEM,
        [
            pltpu.VMEM((rank, rows), jnp.float32),
            pltpu.VMEM((rows, key_width), jnp.float32),
            pltpu.VMEM((rows, key_width), jnp.bfloat16),
            pltpu.VMEM((PLANE, *rest.shape), jnp.bfloat16),
            pltpu.SemaphoreType.DMA((PLANE,)),
        ],
        flops=2 * rows * key_width * (hot_count * rank + out_rows),
        bytes_accessed=6 * 1024 * 1024,
    )(
        plan,
        base,
        cosine,
        sine,
        slot_index.reshape(1, rows),
        *shared,
        *more,
    )


def gathered_outgoing(
    tokens,
    input_norm_scale,
    key_matrix,
    adapter_down_weight,
    adapter_up_weight,
    active_adapter_ids,
    positions,
    hot_slots,
    slot_index,
    out_rows,
):
    float_rows = tokens.astype(jnp.float32)
    inverse_rms = lax.rsqrt(jnp.mean(float_rows * float_rows, axis=1, keepdims=True) + norm_eps)
    normed = (float_rows * inverse_rms * input_norm_scale[None, :]).astype(jnp.bfloat16)
    adapter_device = adapter_down_weight.shape[0]
    down_list = []
    up_list = []
    for entry in range(active_adapter_ids.shape[0]):
        adapter = active_adapter_ids[entry]
        for weight, gathered in ((adapter_down_weight, down_list), (adapter_up_weight, up_list)):
            mine = lax.dynamic_index_in_dim(weight, adapter % adapter_device, 0, keepdims=False)
            gathered.append(spread(mine, "seq", adapter // adapter_device))
    down_matrices = jnp.concatenate(down_list, axis=1)
    up_matrices = jnp.concatenate(up_list, axis=0)
    base_proj = jnp.dot(normed, key_matrix, preferred_element_type=jnp.float32)
    low_rank = jnp.dot(normed, down_matrices, preferred_element_type=jnp.float32).astype(
        jnp.bfloat16
    )
    column_owned = (jnp.arange(down_matrices.shape[1], dtype=jnp.int32) // ADAPTER_RANK)[
        None, :
    ] == hot_slots[:, None]
    low_rank = jnp.where(column_owned, low_rank, jnp.zeros_like(low_rank))
    projected = base_proj + jnp.dot(low_rank, up_matrices, preferred_element_type=jnp.float32)
    key_rows = rotate(projected, positions).astype(jnp.bfloat16)
    return jnp.zeros((out_rows, key_rows.shape[1]), jnp.bfloat16).at[slot_index].set(key_rows)


def on_device(
    tokens,
    input_norm_scale,
    key_matrix,
    adapter_down_weight,
    adapter_up_weight,
    lengths,
    prompt_adapter_index,
    active_adapter_ids,
    token_cache_device,
):
    rows_dev = tokens.shape[0]
    peer_count = lax.axis_size("seq")
    slot_count = max(4, 2 * rows_dev // peer_count)
    key_width = key_matrix.shape[1]
    targets = token_cache_device[:, 0]
    row_order = jnp.arange(rows_dev, dtype=jnp.int32)
    earlier = row_order[None, :] < row_order[:, None]
    rank_within = jnp.sum(
        ((targets[:, None] == targets[None, :]) & earlier).astype(jnp.int32), axis=1
    )
    slot_index = targets * slot_count + rank_within
    positions, hot_slots = locate(
        lengths, prompt_adapter_index, lax.axis_index("seq") * rows_dev, rows_dev
    )
    out_rows = peer_count * slot_count
    if peer_count == PLANE * PLANES:
        outgoing = planes_outgoing(
            tokens,
            input_norm_scale,
            key_matrix,
            adapter_down_weight,
            adapter_up_weight,
            lengths,
            prompt_adapter_index,
            active_adapter_ids,
            positions,
            slot_index,
            out_rows,
        )
    else:
        outgoing = gathered_outgoing(
            tokens,
            input_norm_scale,
            key_matrix,
            adapter_down_weight,
            adapter_up_weight,
            active_adapter_ids,
            positions,
            hot_slots,
            slot_index,
            out_rows,
        )
    outgoing = outgoing.reshape(peer_count, slot_count, key_width)
    result = lax.all_to_all(outgoing, "seq", split_axis=0, concat_axis=0, tiled=True)
    return result.reshape(out_rows, key_width)


def solution(mesh):
    in_specs = (
        P(("groups", "seq"), None),
        P(),
        P(),
        P("seq", None, None),
        P("seq", None, None),
        P("groups"),
        P("groups", None),
        P("groups"),
        P(("groups", "seq"), None),
    )
    out_specs = P(("groups", "seq"), None)
    return jax.shard_map(
        on_device, mesh=mesh, in_specs=in_specs, out_specs=out_specs, check_vma=False
    )
```

```python
import functools

import jax
import jax.numpy as jnp
from jax import lax
from jax.experimental import pallas as pl
from jax.experimental.pallas import tpu as pltpu
from jax.sharding import PartitionSpec as P

HEAD = 128
ADAPTER_RANK = 64


rope_theta = 500000.0
norm_eps = 1e-05


def spread(array, axis, root):
    mine = lax.axis_index(axis) == root
    return lax.psum(jnp.where(mine, array, jnp.zeros_like(array)), axis)


def rotate(projected, positions):
    half_head = HEAD // 2
    frequencies = rope_theta ** (-(jnp.arange(half_head, dtype=jnp.float32) * 2.0) / HEAD)
    angles = positions.astype(jnp.float32)[:, None] * frequencies[None, :]
    cosine = jnp.cos(angles)[:, None, :]
    sine_table = jnp.sin(angles)[:, None, :]
    per_head = projected.reshape(projected.shape[0], -1, HEAD)
    first_half = per_head[..., :half_head]
    second_half = per_head[..., half_head:]
    turned = jnp.concatenate(
        [
            first_half * cosine - second_half * sine_table,
            second_half * cosine + first_half * sine_table,
        ],
        axis=-1,
    )
    return turned.reshape(projected.shape)


def locate(lengths, prompt_adapter_index, first_row, row_count):
    prompt_ends = jnp.cumsum(lengths)
    prompt_starts = prompt_ends - lengths
    row_ids = first_row + jnp.arange(row_count, dtype=jnp.int32)
    prompt_ids = jnp.sum((prompt_ends[None, :] <= row_ids[:, None]).astype(jnp.int32), axis=1)
    prompt_match = prompt_ids[:, None] == jnp.arange(lengths.shape[0], dtype=jnp.int32)[None, :]
    prompt_start = jnp.sum(jnp.where(prompt_match, prompt_starts[None, :], 0), axis=1)
    hot_slots = jnp.sum(jnp.where(prompt_match, prompt_adapter_index[:, 0][None, :], 0), axis=1)
    return (row_ids - prompt_start, hot_slots)


PLANE = 4
PLANES = 4
SLOT_CASES = (
    (2, 1, 1),
    (2, 2, 1),
    (2, 1, 2),
    (3, 2, 1),
    (3, 1, 2),
    (3, 2, 2),
    (3, 3, 1),
    (3, 1, 3),
    (4, 3, 2),
    (4, 2, 3),
    (4, 4, 1),
    (4, 1, 4),
    (4, 3, 3),
)
FEW = 3
ANY = pl.BlockSpec(memory_space=pl.ANY)
SMEM = pl.BlockSpec(memory_space=pltpu.SMEM)
VMEM = pl.BlockSpec(memory_space=pltpu.VMEM)
VMEM_LIMIT = 40 * 1024 * 1024


def swap(value, distance, peer_count):
    return lax.ppermute(value, "seq", [(i, i ^ distance) for i in range(peer_count)])


def call(kernel, out_shape, in_specs, out_specs, scratch=(), **cost):
    return pl.pallas_call(
        kernel,
        out_shape=out_shape,
        in_specs=in_specs,
        out_specs=out_specs,
        scratch_shapes=list(scratch),
        compiler_params=pltpu.CompilerParams(vmem_limit_bytes=VMEM_LIMIT),
        cost_estimate=pl.CostEstimate(transcendentals=0, **cost) if cost else None,
    )


FROM_KIND, FROM_SLOT, PLANE_LIST, DEVICE_LISTS, SECTIONS = 3, 4, 5, 6, 10


def bit_of(mask, entry):
    return lax.shift_right_logical(mask, entry) & 1


def plan_kernel(rows, adapter_device, length_ref, index_ref, id_ref, plan_ref):
    hot_count = id_ref.shape[0]
    device = lax.axis_index("seq")
    plane = lax.div(device, PLANE)
    place = device - plane * PLANE
    for at in range(FROM_KIND * hot_count):
        plan_ref[at] = 0
    for at in range(PLANE_LIST * hot_count, SECTIONS * hot_count):
        plan_ref[at] = -1
    devices = PLANE * PLANES
    uses = [jnp.int32(0)] * devices
    start = jnp.int32(0)
    for prompt in range(length_ref.shape[0]):
        end = start + length_ref[prompt]
        bit = lax.shift_left(jnp.int32(1), index_ref[prompt])
        plan_ref[SECTIONS * hot_count + 3 + 2 * prompt] = end
        plan_ref[SECTIONS * hot_count + 4 + 2 * prompt] = index_ref[prompt]
        for at in range(devices):
            hit = (start < (at + 1) * rows) & (end > at * rows)
            uses[at] = uses[at] | jnp.where(hit, bit, 0)
        start = end
    need = []
    for at in range(PLANES):
        mask = uses[at * PLANE]
        for inner in range(1, PLANE):
            mask = mask | uses[at * PLANE + inner]
        need.append(mask)

    def pick(masks, which):
        total = masks[0]
        for at in range(1, len(masks)):
            total = jnp.where(which == at, masks[at], total)
        return total

    def list_bits(section, mask, values):
        count = jnp.int32(0)
        for entry in range(hot_count):

            @pl.when(bit_of(mask, entry) == 1)
            def _():
                plan_ref[section * hot_count + count] = values[entry]

            count = count + bit_of(mask, entry)
        return count

    owner_plane = []
    kind = []
    slot = []
    local = []
    for entry in range(hot_count):
        adapter = id_ref[entry]
        owner = lax.div(adapter, adapter_device)
        owner_plane.append(lax.div(owner, PLANE))
        local.append(
            ((owner - owner_plane[entry] * PLANE) ^ place) * adapter_device
            + adapter
            - owner * adapter_device
        )
        kind.append(jnp.int32(0))
        slot.append(local[entry])
    need_here = pick(need, plane)
    for distance in range(1, PLANES):
        other = plane ^ distance
        need_there = pick(need, other)
        sent = jnp.int32(0)
        taken = jnp.int32(0)
        for entry in range(hot_count):
            plan_ref[(distance - 1) * hot_count + sent] = local[entry]
            sent = sent + jnp.where(owner_plane[entry] == plane, bit_of(need_there, entry), 0)
            wanted = jnp.where(owner_plane[entry] == other, bit_of(need_here, entry), 0)
            kind[entry] = jnp.where(wanted == 1, distance, kind[entry])
            slot[entry] = jnp.where(wanted == 1, taken, slot[entry])
            taken = taken + wanted
    for entry in range(hot_count):
        plan_ref[FROM_KIND * hot_count + entry] = kind[entry]
        plan_ref[FROM_SLOT * hot_count + entry] = slot[entry]
    listed = [jnp.int32(0)]
    for entry in range(hot_count):
        listed.append(listed[entry] + bit_of(need_here, entry))
    plan_ref[SECTIONS * hot_count] = list_bits(
        PLANE_LIST, need_here, [jnp.int32(entry) for entry in range(hot_count)]
    )
    for distance in range(PLANE):
        list_bits(DEVICE_LISTS + distance, pick(uses, device ^ distance), listed)
    most = []
    for distance in range(1, PLANES):
        largest = jnp.int32(0)
        for at in range(PLANES):
            count = jnp.int32(0)
            for entry in range(hot_count):
                wanted = bit_of(need[at ^ distance], entry)
                count = count + jnp.where(owner_plane[entry] == at, wanted, 0)
            largest = jnp.maximum(largest, count)
        most.append(largest)
    few = jnp.bool_(True)
    for at in range(devices):
        count = jnp.int32(0)
        for entry in range(hot_count):
            count = count + bit_of(uses[at], entry)
        few = few & (count <= FEW)
    case = jnp.int32(len(SLOT_CASES))
    for at in reversed(range(len(SLOT_CASES))):
        fits = few
        for distance in range(PLANES - 1):
            fits = fits & (most[distance] <= SLOT_CASES[at][distance])
        case = jnp.where(fits, at, case)
    plan_ref[SECTIONS * hot_count + 1] = case
    plan_ref[SECTIONS * hot_count + 2] = jnp.where(few, 1, 0)


def norm_kernel(token_ref, scale_ref, out_ref, *quarter_refs):
    values = token_ref[...].astype(jnp.float32)
    inverse_rms = lax.rsqrt(jnp.mean(values * values, axis=1, keepdims=True) + norm_eps)
    out_ref[...] = (values * inverse_rms * scale_ref[...]).astype(jnp.bfloat16)
    place = lax.rem(lax.axis_index("seq"), PLANE)
    quarter = quarter_refs[0].shape[1]
    for distance in range(PLANE):
        first = pl.multiple_of((place ^ distance) * quarter, quarter)
        quarter_refs[distance][...] = out_ref[:, pl.ds(first, quarter)]


def pack_kernel(quarter, down_ref, up_ref, *refs):
    outs = refs[:PLANE]
    sems = refs[PLANE]
    place = lax.rem(lax.axis_index("seq"), PLANE)
    rank = down_ref.shape[1]
    part = rank // PLANE
    copies = []
    for distance in range(PLANE):
        other = place ^ distance
        columns = pl.ds(pl.multiple_of(other * quarter, quarter), quarter)
        copies.append(
            pltpu.make_async_copy(
                down_ref.at[:, :, columns],
                outs[distance].at[:, pl.ds(0, rank), :],
                sems.at[2 * distance],
            )
        )
        rows = pl.ds(pl.multiple_of(other * part, part), part)
        copies.append(
            pltpu.make_async_copy(
                up_ref.at[:, rows, :],
                outs[distance].at[:, pl.ds(rank, part), :],
                sems.at[2 * distance + 1],
            )
        )
    for copy in copies:
        copy.start()
    for copy in copies:
        copy.wait()


def select_kernel(slots, hot_count, adapter_device, plan_ref, *refs):
    local = refs[:PLANE]
    outs = refs[PLANE:]
    for distance in range(1, PLANES):
        for slot in range(slots[distance - 1]):
            index = plan_ref[(distance - 1) * hot_count + slot]
            holder = lax.div(index, adapter_device)
            inner = index - holder * adapter_device
            for at in range(PLANE):

                @pl.when(holder == at)
                def _():
                    outs[distance - 1][slot] = local[at][inner]


def share_rows(first, count, rank, hot_count, plan_ref, rows_ref, outs):
    for distance in range(PLANE):
        for at in range(count):
            listed = plan_ref[(DEVICE_LISTS + distance) * hot_count + first + at]
            outs[distance][at] = rows_ref[jnp.maximum(listed, 0), rank:, :]


def share_kernel(first, rank, hot_count, plan_ref, rows_ref, *outs):
    share_rows(first, outs[0].shape[0], rank, hot_count, plan_ref, rows_ref, outs)


def collect_kernel(hot_count, adapter_device, plan_ref, *refs):
    local = refs[:PLANE]
    arrived = refs[PLANE : PLANE + PLANES - 1]
    out_ref, sems = refs[PLANE + PLANES - 1], refs[-1]
    used = plan_ref[SECTIONS * hot_count]

    def copy_of(place, source):
        return pltpu.make_async_copy(source, out_ref.at[place], sems.at[place])

    for place in range(hot_count):

        @pl.when(place < used)
        def _():
            entry = plan_ref[PLANE_LIST * hot_count + place]
            kind = plan_ref[FROM_KIND * hot_count + entry]
            slot = plan_ref[FROM_SLOT * hot_count + entry]

            @pl.when(kind == 0)
            def _():
                holder = lax.div(slot, adapter_device)
                inner = slot - holder * adapter_device
                for at in range(PLANE):

                    @pl.when(holder == at)
                    def _():
                        copy_of(place, local[at].at[inner]).start()

            for distance in range(1, PLANES):

                @pl.when(kind == distance)
                def _():
                    copy_of(place, arrived[distance - 1].at[slot]).start()

    for place in range(hot_count):

        @pl.when(place < used)
        def _():
            copy_of(place, local[0].at[0]).wait()


def hot_lanes(first_row, rows, hot_count, plan_ref):
    row_ids = first_row + lax.broadcasted_iota(jnp.int32, (1, rows), 1)
    hot = jnp.zeros((1, rows), jnp.int32)
    start = jnp.int32(0)
    for at in range(SECTIONS * hot_count + 3, plan_ref.shape[0], 2):
        end = plan_ref[at]
        hot = jnp.where((row_ids >= start) & (row_ids < end), plan_ref[at + 1], hot)
        start = end
    return hot


def partial_kernel(rank, hot_count, plan_ref, rows_ref, *refs):
    tokens = refs[:PLANE]
    outs = refs[PLANE : 2 * PLANE]
    sums = refs[2 * PLANE]
    device = lax.axis_index("seq")
    rows = tokens[0].shape[0]
    half = hot_count // 2
    part = rank // PLANE
    share_rows(0, FEW, rank, hot_count, plan_ref, rows_ref, outs)

    def run(first, last):
        down = jnp.concatenate([rows_ref[at, :rank, :] for at in range(first, last)], axis=0).T
        for distance in range(PLANE):
            product = jnp.dot(
                tokens[distance][...], down, preferred_element_type=jnp.float32
            ).T
            hot = hot_lanes((device ^ distance) * rows, rows, hot_count, plan_ref)
            total = sums[distance] if first else jnp.zeros((rank, rows), jnp.float32)
            for at in range(first, last):
                piece = product[(at - first) * rank : (at - first + 1) * rank]
                total = jnp.where(hot == plan_ref[PLANE_LIST * hot_count + at], piece, total)
            sums[distance] = total

    run(0, half)

    @pl.when(plan_ref[SECTIONS * hot_count] > half)
    def _():
        run(half, hot_count)

    for distance in range(PLANE):
        for at in range(PLANE):
            total = sums[distance, at * part : (at + 1) * part]
            high = total.astype(jnp.bfloat16)
            low = (total - high.astype(jnp.float32)).astype(jnp.bfloat16)
            outs[distance][FEW, :, at * rows : (at + 1) * rows] = high
            outs[distance][FEW + 1, :, at * rows : (at + 1) * rows] = low


def finish_kernel(
    hot_count,
    plan_ref,
    base_ref,
    cosine_ref,
    sine_ref,
    slot_ref,
    *refs,
):
    shared = refs[:PLANE]
    more = refs[PLANE : 2 * PLANE]
    out_ref, low_ref, sum_ref, rows_ref, more_ref, sems = refs[2 * PLANE :]
    _, part, key_width = shared[0].shape
    rows = base_ref.shape[0]
    device = lax.axis_index("seq")
    place = lax.rem(device, PLANE)
    for at in range(PLANE):
        total = jnp.zeros((part, rows), jnp.float32)
        for distance in range(PLANE):
            for term in (FEW, FEW + 1):
                total = total + shared[distance][term, :, at * rows : (at + 1) * rows].astype(
                    jnp.float32
                )
        low_ref[at * part : (at + 1) * part] = total
    hot = hot_lanes(device * rows, rows, hot_count, plan_ref)

    def adapted(held, first_entry, count):
        entries = []
        for at in range(first_entry, first_entry + count):
            listed = plan_ref[DEVICE_LISTS * hot_count + at]
            entry = plan_ref[PLANE_LIST * hot_count + jnp.maximum(listed, 0)]
            entries.append(jnp.where(listed >= 0, entry, -1))
        result = None
        for distance in range(PLANE):
            first = pl.multiple_of((place ^ distance) * part, part)
            piece = low_ref[pl.ds(first, part), :]
            spread_rows = jnp.concatenate(
                [jnp.where(hot == entry, piece, 0.0) for entry in entries], axis=0
            ).astype(jnp.bfloat16)
            product = lax.dot_general(
                spread_rows,
                held[distance][:count].reshape(count * part, key_width),
                (((0,), (0,)), ((), ())),
                preferred_element_type=jnp.float32,
            )
            result = product if result is None else result + product
        return result

    sum_ref[...] = base_ref[...] + adapted(shared, 0, FEW)

    @pl.when(plan_ref[SECTIONS * hot_count + 2] == 0)
    def _():
        copies = [
            pltpu.make_async_copy(more[at], more_ref.at[at], sems.at[at]) for at in range(PLANE)
        ]
        for copy in copies:
            copy.start()
        for copy in copies:
            copy.wait()
        sum_ref[...] += adapted(
            [more_ref.at[at] for at in range(PLANE)], FEW, hot_count - FEW
        )

    projected = sum_ref[...]
    cosine = cosine_ref[...]
    sine = sine_ref[...]
    for head in range(key_width // HEAD):
        columns = slice(head * HEAD, (head + 1) * HEAD)
        values = projected[:, columns]
        turned = values * cosine + pltpu.roll(values, HEAD // 2, 1) * sine
        rows_ref[:, columns] = turned.astype(jnp.bfloat16)
    slots = lax.broadcasted_iota(jnp.int32, (out_ref.shape[0], rows), 0)
    placed = (slots == slot_ref[...]).astype(jnp.bfloat16)
    out_ref[...] = jnp.dot(
        placed, rows_ref[...], preferred_element_type=jnp.float32
    ).astype(jnp.bfloat16)


def turn_tables(positions):
    half_head = HEAD // 2
    frequencies = rope_theta ** (-(jnp.arange(half_head, dtype=jnp.float32) * 2.0) / HEAD)
    angles = positions.astype(jnp.float32)[:, None] * frequencies[None, :]
    cosine = jnp.cos(angles)
    sine = jnp.sin(angles)
    return (
        jnp.concatenate([cosine, cosine], axis=1),
        jnp.concatenate([-sine, sine], axis=1),
    )


def planes_outgoing(
    tokens,
    input_norm_scale,
    key_matrix,
    adapter_down_weight,
    adapter_up_weight,
    lengths,
    prompt_adapter_index,
    active_adapter_ids,
    positions,
    slot_index,
    out_rows,
):
    peer_count = PLANE * PLANES
    rows, width = tokens.shape
    quarter = width // PLANE
    adapter_device, rank, key_width = adapter_up_weight.shape
    part = rank // PLANE
    hot_count = active_adapter_ids.shape[0]
    prompt_index = prompt_adapter_index[:, 0]
    piece = jax.ShapeDtypeStruct((adapter_device, rank + part, quarter), jnp.bfloat16)
    packed = call(
        functools.partial(pack_kernel, quarter),
        [piece] * PLANE,
        [ANY, ANY],
        [ANY] * PLANE,
        [pltpu.SemaphoreType.DMA((2 * PLANE,))],
    )(jnp.swapaxes(adapter_down_weight, 1, 2), adapter_up_weight)
    local = [packed[0]] + [
        swap(packed[distance], distance, peer_count) for distance in range(1, PLANE)
    ]
    plan = call(
        functools.partial(plan_kernel, rows, adapter_device),
        jax.ShapeDtypeStruct((SECTIONS * hot_count + 3 + 2 * lengths.shape[0],), jnp.int32),
        [SMEM] * 3,
        SMEM,
    )(lengths, prompt_index, active_adapter_ids)
    tokens, local[1] = lax.optimization_barrier((tokens, local[1]))
    block = rows // 4
    normed, *columns = pl.pallas_call(
        norm_kernel,
        grid=(4,),
        out_shape=[jax.ShapeDtypeStruct((rows, width), jnp.bfloat16)]
        + [jax.ShapeDtypeStruct((rows, quarter), jnp.bfloat16)] * PLANE,
        in_specs=[
            pl.BlockSpec((block, width), lambda at: (at, 0)),
            pl.BlockSpec((1, width), lambda at: (0, 0)),
        ],
        out_specs=[pl.BlockSpec((block, width), lambda at: (at, 0))]
        + [pl.BlockSpec((block, quarter), lambda at: (at, 0))] * PLANE,
        compiler_params=pltpu.CompilerParams(vmem_limit_bytes=VMEM_LIMIT),
    )(tokens, input_norm_scale.reshape(1, width))
    second = swap(columns[1], 1, peer_count)
    plan, positions, slot_index, second = lax.optimization_barrier(
        (plan, positions, slot_index, second)
    )

    rest = jax.ShapeDtypeStruct((hot_count - FEW, part, key_width), jnp.bfloat16)

    def share(parts):
        return [parts[0]] + [
            swap(parts[distance], distance, peer_count) for distance in range(1, PLANE)
        ]

    def branch(slots):
        def run(plan, third, fourth, *local):
            sends = call(
                functools.partial(select_kernel, slots, hot_count, adapter_device),
                [
                    jax.ShapeDtypeStruct((slot, rank + part, quarter), jnp.bfloat16)
                    for slot in slots
                ],
                [SMEM] + [VMEM] * PLANE,
                [VMEM] * len(slots),
            )(plan, *local)
            arrived = [
                swap(send, (at + 1) * PLANE, peer_count) for at, send in enumerate(sends)
            ]
            third = swap(third, 2, peer_count)
            fourth = swap(fourth, 3, peer_count)
            collected, *more = call(
                functools.partial(collect_kernel, hot_count, adapter_device),
                [jax.ShapeDtypeStruct((hot_count, rank + part, quarter), jnp.bfloat16)]
                + ([] if slots[0] == hot_count else [rest] * PLANE),
                [SMEM] + [ANY] * (PLANE + PLANES - 1),
                [VMEM] + [ANY] * (0 if slots[0] == hot_count else PLANE),
                [pltpu.SemaphoreType.DMA((hot_count,))],
            )(plan, *local, *arrived)
            if not more:
                more = share(
                    call(
                        functools.partial(share_kernel, FEW, rank, hot_count),
                        [rest] * PLANE,
                        [SMEM, VMEM],
                        [VMEM] * PLANE,
                    )(plan, collected)
                )
            return (third, fourth, collected, *more)

        return run

    cases = [branch(slots) for slots in SLOT_CASES + ((hot_count,) * (PLANES - 1),)]
    third, fourth, used_rows, *more = lax.switch(
        plan[SECTIONS * hot_count + 1], cases, plan, columns[2], columns[3], *local
    )

    shared = call(
        functools.partial(partial_kernel, rank, hot_count),
        [jax.ShapeDtypeStruct((FEW + 2, part, key_width), jnp.bfloat16)] * PLANE,
        [SMEM] + [VMEM] * (1 + PLANE),
        [VMEM] * PLANE,
        [pltpu.VMEM((PLANE, rank, rows), jnp.float32)],
        flops=2 * hot_count * rank * width * rows,
        bytes_accessed=6 * 1024 * 1024,
    )(plan, used_rows, columns[0], second, third, fourth)
    normed, positions, own = lax.optimization_barrier((normed, positions, shared[0]))
    shared = share([own, *shared[1:]])
    base = jnp.dot(normed, key_matrix, preferred_element_type=jnp.float32)
    cosine, sine = turn_tables(positions)
    return call(
        functools.partial(finish_kernel, hot_count),
        jax.ShapeDtypeStruct((out_rows, key_width), jnp.bfloat16),
        [SMEM] + [VMEM] * (4 + PLANE) + [ANY] * PLANE,
        VMEM,
        [
            pltpu.VMEM((rank, rows), jnp.float32),
            pltpu.VMEM((rows, key_width), jnp.float32),
            pltpu.VMEM((rows, key_width), jnp.bfloat16),
            pltpu.VMEM((PLANE, *rest.shape), jnp.bfloat16),
            pltpu.SemaphoreType.DMA((PLANE,)),
        ],
        flops=2 * rows * key_width * (hot_count * rank + out_rows),
        bytes_accessed=6 * 1024 * 1024,
    )(
        plan,
        base,
        cosine,
        sine,
        slot_index.reshape(1, rows),
        *shared,
        *more,
    )


def gathered_outgoing(
    tokens,
    input_norm_scale,
    key_matrix,
    adapter_down_weight,
    adapter_up_weight,
    active_adapter_ids,
    positions,
    hot_slots,
    slot_index,
    out_rows,
):
    float_rows = tokens.astype(jnp.float32)
    inverse_rms = lax.rsqrt(jnp.mean(float_rows * float_rows, axis=1, keepdims=True) + norm_eps)
    normed = (float_rows * inverse_rms * input_norm_scale[None, :]).astype(jnp.bfloat16)
    adapter_device = adapter_down_weight.shape[0]
    down_list = []
    up_list = []
    for entry in range(active_adapter_ids.shape[0]):
        adapter = active_adapter_ids[entry]
        for weight, gathered in ((adapter_down_weight, down_list), (adapter_up_weight, up_list)):
            mine = lax.dynamic_index_in_dim(weight, adapter % adapter_device, 0, keepdims=False)
            gathered.append(spread(mine, "seq", adapter // adapter_device))
    down_matrices = jnp.concatenate(down_list, axis=1)
    up_matrices = jnp.concatenate(up_list, axis=0)
    base_proj = jnp.dot(normed, key_matrix, preferred_element_type=jnp.float32)
    low_rank = jnp.dot(normed, down_matrices, preferred_element_type=jnp.float32).astype(
        jnp.bfloat16
    )
    column_owned = (jnp.arange(down_matrices.shape[1], dtype=jnp.int32) // ADAPTER_RANK)[
        None, :
    ] == hot_slots[:, None]
    low_rank = jnp.where(column_owned, low_rank, jnp.zeros_like(low_rank))
    projected = base_proj + jnp.dot(low_rank, up_matrices, preferred_element_type=jnp.float32)
    key_rows = rotate(projected, positions).astype(jnp.bfloat16)
    return jnp.zeros((out_rows, key_rows.shape[1]), jnp.bfloat16).at[slot_index].set(key_rows)


def on_device(
    tokens,
    input_norm_scale,
    key_matrix,
    adapter_down_weight,
    adapter_up_weight,
    lengths,
    prompt_adapter_index,
    active_adapter_ids,
    token_cache_device,
):
    rows_dev = tokens.shape[0]
    peer_count = lax.axis_size("seq")
    slot_count = max(4, 2 * rows_dev // peer_count)
    key_width = key_matrix.shape[1]
    targets = token_cache_device[:, 0]
    row_order = jnp.arange(rows_dev, dtype=jnp.int32)
    earlier = row_order[None, :] < row_order[:, None]
    rank_within = jnp.sum(
        ((targets[:, None] == targets[None, :]) & earlier).astype(jnp.int32), axis=1
    )
    slot_index = targets * slot_count + rank_within
    positions, hot_slots = locate(
        lengths, prompt_adapter_index, lax.axis_index("seq") * rows_dev, rows_dev
    )
    out_rows = peer_count * slot_count
    if peer_count == PLANE * PLANES:
        outgoing = planes_outgoing(
            tokens,
            input_norm_scale,
            key_matrix,
            adapter_down_weight,
            adapter_up_weight,
            lengths,
            prompt_adapter_index,
            active_adapter_ids,
            positions,
            slot_index,
            out_rows,
        )
    else:
        outgoing = gathered_outgoing(
            tokens,
            input_norm_scale,
            key_matrix,
            adapter_down_weight,
            adapter_up_weight,
            active_adapter_ids,
            positions,
            hot_slots,
            slot_index,
            out_rows,
        )
    outgoing = outgoing.reshape(peer_count, slot_count, key_width)
    result = lax.all_to_all(outgoing, "seq", split_axis=0, concat_axis=0, tiled=True)
    return result.reshape(out_rows, key_width)


def solution(mesh):
    in_specs = (
        P(("groups", "seq"), None),
        P(),
        P(),
        P("seq", None, None),
        P("seq", None, None),
        P("groups"),
        P("groups", None),
        P("groups"),
        P(("groups", "seq"), None),
    )
    out_specs = P(("groups", "seq"), None)
    return jax.shard_map(
        on_device, mesh=mesh, in_specs=in_specs, out_specs=out_specs, check_vma=False
    )
```

```python
import functools

import jax
import jax.numpy as jnp
from jax import lax
from jax.experimental import pallas as pl
from jax.experimental.pallas import tpu as pltpu
from jax.sharding import PartitionSpec as P

HEAD = 128
ADAPTER_RANK = 64


rope_theta = 500000.0
norm_eps = 1e-05


def spread(array, axis, root):
    mine = lax.axis_index(axis) == root
    return lax.psum(jnp.where(mine, array, jnp.zeros_like(array)), axis)


def rotate(projected, positions):
    half_head = HEAD // 2
    frequencies = rope_theta ** (-(jnp.arange(half_head, dtype=jnp.float32) * 2.0) / HEAD)
    angles = positions.astype(jnp.float32)[:, None] * frequencies[None, :]
    cosine = jnp.cos(angles)[:, None, :]
    sine_table = jnp.sin(angles)[:, None, :]
    per_head = projected.reshape(projected.shape[0], -1, HEAD)
    first_half = per_head[..., :half_head]
    second_half = per_head[..., half_head:]
    turned = jnp.concatenate(
        [
            first_half * cosine - second_half * sine_table,
            second_half * cosine + first_half * sine_table,
        ],
        axis=-1,
    )
    return turned.reshape(projected.shape)


def locate(lengths, prompt_adapter_index, first_row, row_count):
    prompt_ends = jnp.cumsum(lengths)
    prompt_starts = prompt_ends - lengths
    row_ids = first_row + jnp.arange(row_count, dtype=jnp.int32)
    prompt_ids = jnp.sum((prompt_ends[None, :] <= row_ids[:, None]).astype(jnp.int32), axis=1)
    prompt_match = prompt_ids[:, None] == jnp.arange(lengths.shape[0], dtype=jnp.int32)[None, :]
    prompt_start = jnp.sum(jnp.where(prompt_match, prompt_starts[None, :], 0), axis=1)
    hot_slots = jnp.sum(jnp.where(prompt_match, prompt_adapter_index[:, 0][None, :], 0), axis=1)
    return (row_ids - prompt_start, hot_slots)


PLANE = 4
PLANES = 4
SLOT_CASES = (
    (2, 1, 1),
    (2, 2, 1),
    (2, 1, 2),
    (3, 2, 1),
    (3, 1, 2),
    (3, 2, 2),
    (3, 3, 1),
    (3, 1, 3),
    (4, 3, 2),
    (4, 2, 3),
    (4, 4, 1),
    (4, 1, 4),
    (4, 3, 3),
)
FEW = 3
ANY = pl.BlockSpec(memory_space=pl.ANY)
SMEM = pl.BlockSpec(memory_space=pltpu.SMEM)
VMEM = pl.BlockSpec(memory_space=pltpu.VMEM)
VMEM_LIMIT = 40 * 1024 * 1024


def swap(value, distance, peer_count):
    return lax.ppermute(value, "seq", [(i, i ^ distance) for i in range(peer_count)])


def call(kernel, out_shape, in_specs, out_specs, scratch=(), **cost):
    return pl.pallas_call(
        kernel,
        out_shape=out_shape,
        in_specs=in_specs,
        out_specs=out_specs,
        scratch_shapes=list(scratch),
        compiler_params=pltpu.CompilerParams(vmem_limit_bytes=VMEM_LIMIT),
        cost_estimate=pl.CostEstimate(transcendentals=0, **cost) if cost else None,
    )


FROM_KIND, FROM_SLOT, PLANE_LIST, DEVICE_LISTS, SECTIONS = 3, 4, 5, 6, 10


def bit_of(mask, entry):
    return lax.shift_right_logical(mask, entry) & 1


def plan_kernel(rows, adapter_device, length_ref, index_ref, id_ref, plan_ref):
    hot_count = id_ref.shape[0]
    device = lax.axis_index("seq")
    plane = lax.div(device, PLANE)
    place = device - plane * PLANE
    for at in range(FROM_KIND * hot_count):
        plan_ref[at] = 0
    for at in range(PLANE_LIST * hot_count, SECTIONS * hot_count):
        plan_ref[at] = -1
    devices = PLANE * PLANES
    uses = [jnp.int32(0)] * devices
    start = jnp.int32(0)
    for prompt in range(length_ref.shape[0]):
        end = start + length_ref[prompt]
        bit = lax.shift_left(jnp.int32(1), index_ref[prompt])
        plan_ref[SECTIONS * hot_count + 3 + 2 * prompt] = end
        plan_ref[SECTIONS * hot_count + 4 + 2 * prompt] = index_ref[prompt]
        for at in range(devices):
            hit = (start < (at + 1) * rows) & (end > at * rows)
            uses[at] = uses[at] | jnp.where(hit, bit, 0)
        start = end
    need = []
    for at in range(PLANES):
        mask = uses[at * PLANE]
        for inner in range(1, PLANE):
            mask = mask | uses[at * PLANE + inner]
        need.append(mask)

    def pick(masks, which):
        total = masks[0]
        for at in range(1, len(masks)):
            total = jnp.where(which == at, masks[at], total)
        return total

    def list_bits(section, mask, values):
        count = jnp.int32(0)
        for entry in range(hot_count):

            @pl.when(bit_of(mask, entry) == 1)
            def _():
                plan_ref[section * hot_count + count] = values[entry]

            count = count + bit_of(mask, entry)
        return count

    owner_plane = []
    kind = []
    slot = []
    local = []
    for entry in range(hot_count):
        adapter = id_ref[entry]
        owner = lax.div(adapter, adapter_device)
        owner_plane.append(lax.div(owner, PLANE))
        local.append(
            ((owner - owner_plane[entry] * PLANE) ^ place) * adapter_device
            + adapter
            - owner * adapter_device
        )
        kind.append(jnp.int32(0))
        slot.append(local[entry])
    need_here = pick(need, plane)
    for distance in range(1, PLANES):
        other = plane ^ distance
        need_there = pick(need, other)
        sent = jnp.int32(0)
        taken = jnp.int32(0)
        for entry in range(hot_count):
            plan_ref[(distance - 1) * hot_count + sent] = local[entry]
            sent = sent + jnp.where(owner_plane[entry] == plane, bit_of(need_there, entry), 0)
            wanted = jnp.where(owner_plane[entry] == other, bit_of(need_here, entry), 0)
            kind[entry] = jnp.where(wanted == 1, distance, kind[entry])
            slot[entry] = jnp.where(wanted == 1, taken, slot[entry])
            taken = taken + wanted
    for entry in range(hot_count):
        plan_ref[FROM_KIND * hot_count + entry] = kind[entry]
        plan_ref[FROM_SLOT * hot_count + entry] = slot[entry]
    listed = [jnp.int32(0)]
    for entry in range(hot_count):
        listed.append(listed[entry] + bit_of(need_here, entry))
    plan_ref[SECTIONS * hot_count] = list_bits(
        PLANE_LIST, need_here, [jnp.int32(entry) for entry in range(hot_count)]
    )
    for distance in range(PLANE):
        list_bits(DEVICE_LISTS + distance, pick(uses, device ^ distance), listed)
    most = []
    for distance in range(1, PLANES):
        largest = jnp.int32(0)
        for at in range(PLANES):
            count = jnp.int32(0)
            for entry in range(hot_count):
                wanted = bit_of(need[at ^ distance], entry)
                count = count + jnp.where(owner_plane[entry] == at, wanted, 0)
            largest = jnp.maximum(largest, count)
        most.append(largest)
    few = jnp.bool_(True)
    for at in range(devices):
        count = jnp.int32(0)
        for entry in range(hot_count):
            count = count + bit_of(uses[at], entry)
        few = few & (count <= FEW)
    case = jnp.int32(len(SLOT_CASES))
    for at in reversed(range(len(SLOT_CASES))):
        fits = few
        for distance in range(PLANES - 1):
            fits = fits & (most[distance] <= SLOT_CASES[at][distance])
        case = jnp.where(fits, at, case)
    plan_ref[SECTIONS * hot_count + 1] = case
    plan_ref[SECTIONS * hot_count + 2] = jnp.where(few, 1, 0)


def norm_kernel(token_ref, scale_ref, out_ref, *quarter_refs):
    values = token_ref[...].astype(jnp.float32)
    inverse_rms = lax.rsqrt(jnp.mean(values * values, axis=1, keepdims=True) + norm_eps)
    out_ref[...] = (values * inverse_rms * scale_ref[...]).astype(jnp.bfloat16)
    place = lax.rem(lax.axis_index("seq"), PLANE)
    quarter = quarter_refs[0].shape[1]
    for distance in range(PLANE):
        first = pl.multiple_of((place ^ distance) * quarter, quarter)
        quarter_refs[distance][...] = out_ref[:, pl.ds(first, quarter)]


def pack_kernel(quarter, down_ref, up_ref, *refs):
    outs = refs[:PLANE]
    sems = refs[PLANE]
    place = lax.rem(lax.axis_index("seq"), PLANE)
    rank = down_ref.shape[1]
    part = rank // PLANE
    copies = []
    for distance in range(PLANE):
        other = place ^ distance
        columns = pl.ds(pl.multiple_of(other * quarter, quarter), quarter)
        copies.append(
            pltpu.make_async_copy(
                down_ref.at[:, :, columns],
                outs[distance].at[:, pl.ds(0, rank), :],
                sems.at[2 * distance],
            )
        )
        rows = pl.ds(pl.multiple_of(other * part, part), part)
        copies.append(
            pltpu.make_async_copy(
                up_ref.at[:, rows, :],
                outs[distance].at[:, pl.ds(rank, part), :],
                sems.at[2 * distance + 1],
            )
        )
    for copy in copies:
        copy.start()
    for copy in copies:
        copy.wait()


def select_kernel(slots, hot_count, adapter_device, plan_ref, *refs):
    local = refs[:PLANE]
    outs = refs[PLANE:]
    for distance in range(1, PLANES):
        for slot in range(slots[distance - 1]):
            index = plan_ref[(distance - 1) * hot_count + slot]
            holder = lax.div(index, adapter_device)
            inner = index - holder * adapter_device
            for at in range(PLANE):

                @pl.when(holder == at)
                def _():
                    outs[distance - 1][slot] = local[at][inner]


def share_rows(first, count, rank, hot_count, plan_ref, rows_ref, outs):
    for distance in range(PLANE):
        for at in range(count):
            listed = plan_ref[(DEVICE_LISTS + distance) * hot_count + first + at]
            outs[distance][at] = rows_ref[jnp.maximum(listed, 0), rank:, :]


def share_kernel(first, rank, hot_count, plan_ref, rows_ref, *outs):
    share_rows(first, outs[0].shape[0], rank, hot_count, plan_ref, rows_ref, outs)


def collect_kernel(hot_count, adapter_device, plan_ref, *refs):
    local = refs[:PLANE]
    arrived = refs[PLANE : PLANE + PLANES - 1]
    out_ref, sems = refs[PLANE + PLANES - 1], refs[-1]
    used = plan_ref[SECTIONS * hot_count]

    def copy_of(place, source):
        return pltpu.make_async_copy(source, out_ref.at[place], sems.at[place])

    for place in range(hot_count):

        @pl.when(place < used)
        def _():
            entry = plan_ref[PLANE_LIST * hot_count + place]
            kind = plan_ref[FROM_KIND * hot_count + entry]
            slot = plan_ref[FROM_SLOT * hot_count + entry]

            @pl.when(kind == 0)
            def _():
                holder = lax.div(slot, adapter_device)
                inner = slot - holder * adapter_device
                for at in range(PLANE):

                    @pl.when(holder == at)
                    def _():
                        copy_of(place, local[at].at[inner]).start()

            for distance in range(1, PLANES):

                @pl.when(kind == distance)
                def _():
                    copy_of(place, arrived[distance - 1].at[slot]).start()

    for place in range(hot_count):

        @pl.when(place < used)
        def _():
            copy_of(place, local[0].at[0]).wait()


def hot_lanes(first_row, rows, hot_count, plan_ref):
    row_ids = first_row + lax.broadcasted_iota(jnp.int32, (1, rows), 1)
    hot = jnp.zeros((1, rows), jnp.int32)
    start = jnp.int32(0)
    for at in range(SECTIONS * hot_count + 3, plan_ref.shape[0], 2):
        end = plan_ref[at]
        hot = jnp.where((row_ids >= start) & (row_ids < end), plan_ref[at + 1], hot)
        start = end
    return hot


def partial_kernel(rank, hot_count, plan_ref, rows_ref, *refs):
    tokens = refs[:PLANE]
    outs = refs[PLANE : 2 * PLANE]
    sums = refs[2 * PLANE]
    device = lax.axis_index("seq")
    rows = tokens[0].shape[0]
    half = hot_count // 2
    part = rank // PLANE
    share_rows(0, FEW, rank, hot_count, plan_ref, rows_ref, outs)

    def run(first, last):
        down = jnp.concatenate([rows_ref[at, :rank, :] for at in range(first, last)], axis=0).T
        for distance in range(PLANE):
            product = jnp.dot(
                tokens[distance][...], down, preferred_element_type=jnp.float32
            ).T
            hot = hot_lanes((device ^ distance) * rows, rows, hot_count, plan_ref)
            total = sums[distance] if first else jnp.zeros((rank, rows), jnp.float32)
            for at in range(first, last):
                piece = product[(at - first) * rank : (at - first + 1) * rank]
                total = jnp.where(hot == plan_ref[PLANE_LIST * hot_count + at], piece, total)
            sums[distance] = total

    run(0, half)

    @pl.when(plan_ref[SECTIONS * hot_count] > half)
    def _():
        run(half, hot_count)

    for distance in range(PLANE):
        for at in range(PLANE):
            total = sums[distance, at * part : (at + 1) * part]
            high = total.astype(jnp.bfloat16)
            low = (total - high.astype(jnp.float32)).astype(jnp.bfloat16)
            outs[distance][FEW, :, at * rows : (at + 1) * rows] = high
            outs[distance][FEW + 1, :, at * rows : (at + 1) * rows] = low


def finish_kernel(
    hot_count,
    plan_ref,
    base_ref,
    cosine_ref,
    sine_ref,
    slot_ref,
    *refs,
):
    shared = refs[:PLANE]
    more = refs[PLANE : 2 * PLANE]
    out_ref, low_ref, sum_ref, rows_ref, more_ref, sems = refs[2 * PLANE :]
    _, part, key_width = shared[0].shape
    rows = base_ref.shape[0]
    device = lax.axis_index("seq")
    place = lax.rem(device, PLANE)
    for at in range(PLANE):
        total = jnp.zeros((part, rows), jnp.float32)
        for distance in range(PLANE):
            for term in (FEW, FEW + 1):
                total = total + shared[distance][term, :, at * rows : (at + 1) * rows].astype(
                    jnp.float32
                )
        low_ref[at * part : (at + 1) * part] = total
    hot = hot_lanes(device * rows, rows, hot_count, plan_ref)

    def adapted(held, first_entry, count):
        entries = []
        for at in range(first_entry, first_entry + count):
            listed = plan_ref[DEVICE_LISTS * hot_count + at]
            entry = plan_ref[PLANE_LIST * hot_count + jnp.maximum(listed, 0)]
            entries.append(jnp.where(listed >= 0, entry, -1))
        result = None
        for distance in range(PLANE):
            first = pl.multiple_of((place ^ distance) * part, part)
            piece = low_ref[pl.ds(first, part), :]
            spread_rows = jnp.concatenate(
                [jnp.where(hot == entry, piece, 0.0) for entry in entries], axis=0
            ).astype(jnp.bfloat16)
            product = lax.dot_general(
                spread_rows,
                held[distance][:count].reshape(count * part, key_width),
                (((0,), (0,)), ((), ())),
                preferred_element_type=jnp.float32,
            )
            result = product if result is None else result + product
        return result

    sum_ref[...] = base_ref[...] + adapted(shared, 0, FEW)

    @pl.when(plan_ref[SECTIONS * hot_count + 2] == 0)
    def _():
        copies = [
            pltpu.make_async_copy(more[at], more_ref.at[at], sems.at[at]) for at in range(PLANE)
        ]
        for copy in copies:
            copy.start()
        for copy in copies:
            copy.wait()
        sum_ref[...] += adapted(
            [more_ref.at[at] for at in range(PLANE)], FEW, hot_count - FEW
        )

    projected = sum_ref[...]
    cosine = cosine_ref[...]
    sine = sine_ref[...]
    for head in range(key_width // HEAD):
        columns = slice(head * HEAD, (head + 1) * HEAD)
        values = projected[:, columns]
        turned = values * cosine + pltpu.roll(values, HEAD // 2, 1) * sine
        rows_ref[:, columns] = turned.astype(jnp.bfloat16)
    slots = lax.broadcasted_iota(jnp.int32, (out_ref.shape[0], rows), 0)
    placed = (slots == slot_ref[...]).astype(jnp.bfloat16)
    out_ref[...] = jnp.dot(
        placed, rows_ref[...], preferred_element_type=jnp.float32
    ).astype(jnp.bfloat16)


def turn_tables(positions):
    half_head = HEAD // 2
    frequencies = rope_theta ** (-(jnp.arange(half_head, dtype=jnp.float32) * 2.0) / HEAD)
    angles = positions.astype(jnp.float32)[:, None] * frequencies[None, :]
    cosine = jnp.cos(angles)
    sine = jnp.sin(angles)
    return (
        jnp.concatenate([cosine, cosine], axis=1),
        jnp.concatenate([-sine, sine], axis=1),
    )


def planes_outgoing(
    tokens,
    input_norm_scale,
    key_matrix,
    adapter_down_weight,
    adapter_up_weight,
    lengths,
    prompt_adapter_index,
    active_adapter_ids,
    positions,
    slot_index,
    out_rows,
):
    peer_count = PLANE * PLANES
    rows, width = tokens.shape
    quarter = width // PLANE
    adapter_device, rank, key_width = adapter_up_weight.shape
    part = rank // PLANE
    hot_count = active_adapter_ids.shape[0]
    prompt_index = prompt_adapter_index[:, 0]
    piece = jax.ShapeDtypeStruct((adapter_device, rank + part, quarter), jnp.bfloat16)
    packed = call(
        functools.partial(pack_kernel, quarter),
        [piece] * PLANE,
        [ANY, ANY],
        [ANY] * PLANE,
        [pltpu.SemaphoreType.DMA((2 * PLANE,))],
    )(jnp.swapaxes(adapter_down_weight, 1, 2), adapter_up_weight)
    plan = call(
        functools.partial(plan_kernel, rows, adapter_device),
        jax.ShapeDtypeStruct((SECTIONS * hot_count + 3 + 2 * lengths.shape[0],), jnp.int32),
        [SMEM] * 3,
        SMEM,
    )(lengths, prompt_index, active_adapter_ids)
    plan, near = lax.optimization_barrier((plan, packed[1]))
    local = [packed[0], swap(near, 1, peer_count)] + [
        swap(packed[distance], distance, peer_count) for distance in range(2, PLANE)
    ]
    tokens, local[1] = lax.optimization_barrier((tokens, local[1]))
    block = rows // 4
    normed, *columns = pl.pallas_call(
        norm_kernel,
        grid=(4,),
        out_shape=[jax.ShapeDtypeStruct((rows, width), jnp.bfloat16)]
        + [jax.ShapeDtypeStruct((rows, quarter), jnp.bfloat16)] * PLANE,
        in_specs=[
            pl.BlockSpec((block, width), lambda at: (at, 0)),
            pl.BlockSpec((1, width), lambda at: (0, 0)),
        ],
        out_specs=[pl.BlockSpec((block, width), lambda at: (at, 0))]
        + [pl.BlockSpec((block, quarter), lambda at: (at, 0))] * PLANE,
        compiler_params=pltpu.CompilerParams(vmem_limit_bytes=VMEM_LIMIT),
    )(tokens, input_norm_scale.reshape(1, width))
    second = swap(columns[1], 1, peer_count)
    plan, positions, slot_index, second = lax.optimization_barrier(
        (plan, positions, slot_index, second)
    )

    rest = jax.ShapeDtypeStruct((hot_count - FEW, part, key_width), jnp.bfloat16)

    def share(parts):
        return [parts[0]] + [
            swap(parts[distance], distance, peer_count) for distance in range(1, PLANE)
        ]

    def branch(slots):
        def run(plan, third, fourth, *local):
            sends = call(
                functools.partial(select_kernel, slots, hot_count, adapter_device),
                [
                    jax.ShapeDtypeStruct((slot, rank + part, quarter), jnp.bfloat16)
                    for slot in slots
                ],
                [SMEM] + [VMEM] * PLANE,
                [VMEM] * len(slots),
            )(plan, *local)
            arrived = [
                swap(send, (at + 1) * PLANE, peer_count) for at, send in enumerate(sends)
            ]
            third = swap(third, 2, peer_count)
            fourth = swap(fourth, 3, peer_count)
            collected, *more = call(
                functools.partial(collect_kernel, hot_count, adapter_device),
                [jax.ShapeDtypeStruct((hot_count, rank + part, quarter), jnp.bfloat16)]
                + ([] if slots[0] == hot_count else [rest] * PLANE),
                [SMEM] + [ANY] * (PLANE + PLANES - 1),
                [VMEM] + [ANY] * (0 if slots[0] == hot_count else PLANE),
                [pltpu.SemaphoreType.DMA((hot_count,))],
            )(plan, *local, *arrived)
            if not more:
                more = share(
                    call(
                        functools.partial(share_kernel, FEW, rank, hot_count),
                        [rest] * PLANE,
                        [SMEM, VMEM],
                        [VMEM] * PLANE,
                    )(plan, collected)
                )
            return (third, fourth, collected, *more)

        return run

    cases = [branch(slots) for slots in SLOT_CASES + ((hot_count,) * (PLANES - 1),)]
    third, fourth, used_rows, *more = lax.switch(
        plan[SECTIONS * hot_count + 1], cases, plan, columns[2], columns[3], *local
    )

    shared = call(
        functools.partial(partial_kernel, rank, hot_count),
        [jax.ShapeDtypeStruct((FEW + 2, part, key_width), jnp.bfloat16)] * PLANE,
        [SMEM] + [VMEM] * (1 + PLANE),
        [VMEM] * PLANE,
        [pltpu.VMEM((PLANE, rank, rows), jnp.float32)],
        flops=2 * hot_count * rank * width * rows,
        bytes_accessed=6 * 1024 * 1024,
    )(plan, used_rows, columns[0], second, third, fourth)
    normed, positions, own = lax.optimization_barrier((normed, positions, shared[0]))
    shared = share([own, *shared[1:]])
    base = jnp.dot(normed, key_matrix, preferred_element_type=jnp.float32)
    cosine, sine = turn_tables(positions)
    return call(
        functools.partial(finish_kernel, hot_count),
        jax.ShapeDtypeStruct((out_rows, key_width), jnp.bfloat16),
        [SMEM] + [VMEM] * (4 + PLANE) + [ANY] * PLANE,
        VMEM,
        [
            pltpu.VMEM((rank, rows), jnp.float32),
            pltpu.VMEM((rows, key_width), jnp.float32),
            pltpu.VMEM((rows, key_width), jnp.bfloat16),
            pltpu.VMEM((PLANE, *rest.shape), jnp.bfloat16),
            pltpu.SemaphoreType.DMA((PLANE,)),
        ],
        flops=2 * rows * key_width * (hot_count * rank + out_rows),
        bytes_accessed=6 * 1024 * 1024,
    )(
        plan,
        base,
        cosine,
        sine,
        slot_index.reshape(1, rows),
        *shared,
        *more,
    )


def gathered_outgoing(
    tokens,
    input_norm_scale,
    key_matrix,
    adapter_down_weight,
    adapter_up_weight,
    active_adapter_ids,
    positions,
    hot_slots,
    slot_index,
    out_rows,
):
    float_rows = tokens.astype(jnp.float32)
    inverse_rms = lax.rsqrt(jnp.mean(float_rows * float_rows, axis=1, keepdims=True) + norm_eps)
    normed = (float_rows * inverse_rms * input_norm_scale[None, :]).astype(jnp.bfloat16)
    adapter_device = adapter_down_weight.shape[0]
    down_list = []
    up_list = []
    for entry in range(active_adapter_ids.shape[0]):
        adapter = active_adapter_ids[entry]
        for weight, gathered in ((adapter_down_weight, down_list), (adapter_up_weight, up_list)):
            mine = lax.dynamic_index_in_dim(weight, adapter % adapter_device, 0, keepdims=False)
            gathered.append(spread(mine, "seq", adapter // adapter_device))
    down_matrices = jnp.concatenate(down_list, axis=1)
    up_matrices = jnp.concatenate(up_list, axis=0)
    base_proj = jnp.dot(normed, key_matrix, preferred_element_type=jnp.float32)
    low_rank = jnp.dot(normed, down_matrices, preferred_element_type=jnp.float32).astype(
        jnp.bfloat16
    )
    column_owned = (jnp.arange(down_matrices.shape[1], dtype=jnp.int32) // ADAPTER_RANK)[
        None, :
    ] == hot_slots[:, None]
    low_rank = jnp.where(column_owned, low_rank, jnp.zeros_like(low_rank))
    projected = base_proj + jnp.dot(low_rank, up_matrices, preferred_element_type=jnp.float32)
    key_rows = rotate(projected, positions).astype(jnp.bfloat16)
    return jnp.zeros((out_rows, key_rows.shape[1]), jnp.bfloat16).at[slot_index].set(key_rows)


def on_device(
    tokens,
    input_norm_scale,
    key_matrix,
    adapter_down_weight,
    adapter_up_weight,
    lengths,
    prompt_adapter_index,
    active_adapter_ids,
    token_cache_device,
):
    rows_dev = tokens.shape[0]
    peer_count = lax.axis_size("seq")
    slot_count = max(4, 2 * rows_dev // peer_count)
    key_width = key_matrix.shape[1]
    targets = token_cache_device[:, 0]
    row_order = jnp.arange(rows_dev, dtype=jnp.int32)
    earlier = row_order[None, :] < row_order[:, None]
    rank_within = jnp.sum(
        ((targets[:, None] == targets[None, :]) & earlier).astype(jnp.int32), axis=1
    )
    slot_index = targets * slot_count + rank_within
    positions, hot_slots = locate(
        lengths, prompt_adapter_index, lax.axis_index("seq") * rows_dev, rows_dev
    )
    out_rows = peer_count * slot_count
    if peer_count == PLANE * PLANES:
        outgoing = planes_outgoing(
            tokens,
            input_norm_scale,
            key_matrix,
            adapter_down_weight,
            adapter_up_weight,
            lengths,
            prompt_adapter_index,
            active_adapter_ids,
            positions,
            slot_index,
            out_rows,
        )
    else:
        outgoing = gathered_outgoing(
            tokens,
            input_norm_scale,
            key_matrix,
            adapter_down_weight,
            adapter_up_weight,
            active_adapter_ids,
            positions,
            hot_slots,
            slot_index,
            out_rows,
        )
    outgoing = outgoing.reshape(peer_count, slot_count, key_width)
    result = lax.all_to_all(outgoing, "seq", split_axis=0, concat_axis=0, tiled=True)
    return result.reshape(out_rows, key_width)


def solution(mesh):
    in_specs = (
        P(("groups", "seq"), None),
        P(),
        P(),
        P("seq", None, None),
        P("seq", None, None),
        P("groups"),
        P("groups", None),
        P("groups"),
        P(("groups", "seq"), None),
    )
    out_specs = P(("groups", "seq"), None)
    return jax.shard_map(
        on_device, mesh=mesh, in_specs=in_specs, out_specs=out_specs, check_vma=False
    )
```
